32 devices in a mesh: fsdp: 8 (over z, x), rep: 4 (over y, core).
Axes of the slice: x: 2, y: 2, z: 4, core: 2. Of those that a mesh axis runs over, the one named last changes fastest.
Arguments:
- tokens: bfloat16 [2, 2048, 2048], P(None, ('fsdp', 'rep')), may hold values from -6 to 6
- lengths: int32 [2, 32], P(None, ('fsdp', 'rep')), may hold values from 16 to 64, as said below
- offsets: int32 [2, 32], P(None, ('fsdp', 'rep')), may hold values from 0 to 48, as said below
- norm_gain: bfloat16 [2048], P(('fsdp', 'rep')), may hold values from 0.5 to 1.5
- mamba_in: bfloat16 [2048, 6704], P(('fsdp', 'rep')), may hold values from -0.125 to 0.125
- conv_taps: float32 [4, 3584], replicated, may hold values from -3 to 3
- conv_bias: float32 [3584], replicated, may hold values from -3 to 3
- step_bias: float32 [48], replicated, may hold values from -4 to -1
- decay_log: float32 [48], replicated, may hold values from -3 to 1
- skip_weight: float32 [48], replicated, may hold values from 0.5 to 1.5
- mamba_gain: float32 [3072], replicated, may hold values from 0.5 to 1.5
- mamba_out: bfloat16 [3072, 2048], P(None, ('fsdp', 'rep')), may hold values from -0.109375 to 0.109375
- query_weight: bfloat16 [2048, 1024], P(('fsdp', 'rep')), may hold values from -0.125 to 0.125
- key_weight: bfloat16 [2048, 256], P(('fsdp', 'rep')), may hold values from -0.125 to 0.125
- value_weight: bfloat16 [2048, 256], P(('fsdp', 'rep')), may hold values from -0.125 to 0.125
- output_weight: bfloat16 [1024, 2048], P(None, ('fsdp', 'rep')), may hold values from -0.75 to 0.75
- second_gain: bfloat16 [2048], P(('fsdp', 'rep')), may hold values from 0.5 to 1.5
- gate_weight: bfloat16 [2048, 4096], P(('fsdp', 'rep')), may hold values from -0.125 to 0.125
- up_weight: bfloat16 [2048, 4096], P(('fsdp', 'rep')), may hold values from -0.125 to 0.125
- down_weight: bfloat16 [4096, 2048], P(None, ('fsdp', 'rep')), may hold values from -0.09375 to 0.09375
- cotangent: bfloat16 [2, 2048, 2048], P(None, ('fsdp', 'rep')), may hold values from -6 to 6
Outputs:
- output: bfloat16 [2, 2048, 2048], P(None, ('fsdp', 'rep'))
- grad_tokens: float32 [2, 2048, 2048], P(None, ('fsdp', 'rep'))
- grad_norm_gain: float32 [2048], P(('fsdp', 'rep'))
- grad_mamba_in: float32 [2048, 6704], P(('fsdp', 'rep'))
- grad_conv_taps: float32 [4, 3584], replicated
- grad_conv_bias: float32 [3584], replicated
- grad_step_bias: float32 [48], replicated
- grad_decay_log: float32 [48], replicated
- grad_skip_weight: float32 [48], replicated
- grad_mamba_gain: float32 [3072], replicated
- grad_mamba_out: float32 [3072, 2048], P(None, ('fsdp', 'rep'))
- grad_query_weight: float32 [2048, 1024], P(('fsdp', 'rep'))
- grad_key_weight: float32 [2048, 256], P(('fsdp', 'rep'))
- grad_value_weight: float32 [2048, 256], P(('fsdp', 'rep'))
- grad_output_weight: float32 [1024, 2048], P(None, ('fsdp', 'rep'))
- grad_second_gain: float32 [2048], P(('fsdp', 'rep'))
- grad_gate_weight: float32 [2048, 4096], P(('fsdp', 'rep'))
- grad_up_weight: float32 [2048, 4096], P(('fsdp', 'rep'))
- grad_down_weight: float32 [4096, 2048], P(None, ('fsdp', 'rep'))
The draws below stay inside these ranges and needn't reach their ends.
Inputs may be any that keep to these rules, and one draw needn't show every extreme that they name: `lengths`: each block holds a sequence of 16 to 64 tokens; in every draw some block holds exactly 64 and some exactly 16. offsets + lengths <= 64 in every block.
All inputs are finite; a program needn't handle non-finite values.
Results may differ from the reference program's by a relative error of at most 0.0095.
Values may be sent and summed in bfloat16 or wider, within the bound.
No kernel may reach another device: no remote copies, remote signals or barrier semaphores. Data moves between devices by JAX's collectives and lax.ppermute only.
A program may use at most 448 MiB of HBM per device.

```python
import math
import jax
import jax.numpy as jnp
from jax import lax

D = 2048
H = 48
KW = 4
QH = 8
KVH = 2
HD = 128
FF = 4096
LMAX = 64
MB = 2
DI = 3072
IN_W = 6704
CONV_W = 3584
SLOTS = 2048
N_FSDP = 8
N_REP = 4
DEVICES = 32


def slot_draw(key):
    key_length, key_offset, key_batch, key_device = jax.random.split(key, 4)
    shape = (MB, DEVICES)
    lengths = jax.random.randint(key_length, shape, LMAX // 4, LMAX + 1)
    batch_pick = jax.random.randint(key_batch, (), 0, MB)
    device_pick = jax.random.randint(key_device, (), 0, DEVICES)
    batch_ids = jnp.arange(MB)[:, None]
    device_ids = jnp.arange(DEVICES)[None, :]
    longest = (batch_ids == batch_pick) & (device_ids == device_pick)
    shortest = (batch_ids == batch_pick) & (device_ids == (device_pick + 1) % DEVICES)
    lengths = jnp.where(longest, LMAX, jnp.where(shortest, LMAX // 4, lengths))
    offsets = jax.random.randint(key_offset, shape, 0, LMAX - lengths + 1)
    offsets = jnp.where(longest, 0, jnp.where(shortest, LMAX - LMAX // 4, offsets))
    return (lengths.astype(jnp.int32), offsets.astype(jnp.int32))


def draw_lengths(key, part):
    return slot_draw(key)[0]


def draw_offsets(key, part):
    return slot_draw(key)[1]


def strengthened(drawn, rng, source, target, parts, factor):
    owner, partner = [(jnp.arange(drawn.shape[axis_at]) // (drawn.shape[axis_at] // parts)).reshape([-1 if axis == axis_at else 1 for axis in range(drawn.ndim)]) for axis_at in (source, target)]
    chosen = jax.random.permutation(rng, parts)[partner]
    strong = (owner == chosen) | (owner == (partner + parts // 2) % parts)
    return jnp.where(strong, factor * drawn, drawn)


def level_of(own_key, extent, shards, smallest, high):
    def one(axis_at, parts):
        draws = jax.random.uniform(jax.random.fold_in(jax.random.fold_in(own_key, 6), axis_at), (parts,), jnp.float32, smallest / len(shards), high / len(shards))
        return jnp.repeat(jnp.exp(draws), extent[axis_at] // parts).reshape((-1,) + (1,) * (len(extent) - axis_at - 1))

    level = one(*shards[0])
    for cut in shards[1:]:
        level = level * one(*cut)
    return level


def normal_values(stream_key, extent, deviation, reach, cuts=(), kind=jnp.bfloat16):
    entries = deviation * jax.random.normal(stream_key, extent, jnp.float32)
    if cuts:
        entries = entries * level_of(stream_key, extent, cuts, -0.22, 0.18)
    return jnp.clip(entries, -reach, reach).astype(kind)


def heavy_noise(stream_key, extent, scale, bound, cuts, heavy, kind=jnp.bfloat16):
    drawn = scale * jax.random.normal(stream_key, extent, jnp.float32)
    if cuts:
        drawn = drawn * level_of(stream_key, extent, cuts, -0.22, 0.18)
    return jnp.clip(strengthened(drawn, jax.random.fold_in(stream_key, 3), *heavy), -bound, bound).astype(kind)


def setup_inputs(seed: int = 0) -> dict:
    key_of = jax.random.split(jax.random.key(seed), 22)
    tokens = normal_values(key_of[0], (MB, SLOTS, D), 1.0, 6.0, ((1, 32),))
    lengths = draw_lengths(jax.random.fold_in(key_of[21], 71), 0)
    offsets = draw_offsets(jax.random.fold_in(key_of[21], 71), 0)
    norm_gain = jnp.clip(1.0 + 0.1 * jax.random.normal(key_of[3], (D,), jnp.float32), 0.5, 1.5).astype(jnp.bfloat16)
    mamba_in = normal_values(key_of[4], (D, IN_W), D ** -0.5, 0.125, ((0, 32),))
    conv_taps = normal_values(key_of[5], (KW, CONV_W), 0.5, 3.0, (), jnp.float32)
    conv_bias = normal_values(key_of[6], (CONV_W,), 0.5, 3.0, (), jnp.float32)
    step_bias = jnp.clip(jax.random.uniform(key_of[7], (H,), jnp.float32, -4.0, -1.0), -4.0, -1.0)
    decay_log = jnp.clip(jax.random.uniform(key_of[8], (H,), jnp.float32, -3.0, 1.0), -3.0, 1.0)
    skip_weight = jnp.clip(jax.random.uniform(key_of[9], (H,), jnp.float32, 0.5, 1.5), 0.5, 1.5)
    mamba_gain = jnp.clip(1.0 + 0.1 * jax.random.normal(key_of[10], (DI,), jnp.float32), 0.5, 1.5)
    mamba_out = normal_values(key_of[11], (DI, D), DI ** -0.5, 0.109375, ((1, 32),))
    query_weight = normal_values(key_of[12], (D, QH * HD), D ** -0.5, 0.125, ((0, 32),))
    key_weight = normal_values(key_of[13], (D, KVH * HD), D ** -0.5, 0.125, ((0, 32),))
    value_weight = normal_values(key_of[14], (D, KVH * HD), D ** -0.5, 0.125, ((0, 32),))
    output_weight = normal_values(key_of[15], (QH * HD, D), (QH * HD // 16) ** -0.5, 0.75, ((1, 32),))
    second_gain = jnp.clip(1.0 + 0.1 * jax.random.normal(key_of[16], (D,), jnp.float32), 0.5, 1.5).astype(jnp.bfloat16)
    gate_weight = normal_values(key_of[17], (D, FF), D ** -0.5, 0.125, ((0, 32),))
    up_weight = normal_values(key_of[18], (D, FF), D ** -0.5, 0.125, ((0, 32),))
    down_weight = normal_values(key_of[19], (FF, D), FF ** -0.5, 0.09375, ((1, 32),))
    cotangent = heavy_noise(key_of[20], (MB, SLOTS, D), 1.0, 6.0, ((1, 32),), (1, 2, 32, 2.75))
    return dict(tokens=tokens, lengths=lengths, offsets=offsets, norm_gain=norm_gain, mamba_in=mamba_in, conv_taps=conv_taps, conv_bias=conv_bias, step_bias=step_bias, decay_log=decay_log, skip_weight=skip_weight, mamba_gain=mamba_gain, mamba_out=mamba_out, query_weight=query_weight, key_weight=key_weight, value_weight=value_weight, output_weight=output_weight, second_gain=second_gain, gate_weight=gate_weight, up_weight=up_weight, down_weight=down_weight, cotangent=cotangent)


epsilon = 1e-05
rope_base = 100000000000.0
highest = lax.Precision.HIGHEST

@jax.custom_vjp
def low(v):
    return lax.optimization_barrier(v.astype(jnp.bfloat16)).astype(jnp.float32)

@jax.custom_vjp
def low_back(v):
    return v

def low_keep(v):
    return (low(v), None)

def low_pass(kept, grad):
    return (grad,)

def back_keep(v):
    return (v, None)

def back_low(kept, grad):
    return (low(grad),)
low.defvjp(low_keep, low_pass)
low_back.defvjp(back_keep, back_low)

def matmul(left, weight):
    flat = left.reshape(-1, left.shape[-1])
    result = jnp.dot(flat, weight, precision=highest, preferred_element_type=jnp.float32)
    return result.reshape(left.shape[:-1] + (weight.shape[1],))

def root_norm(values, gain):
    return values * lax.rsqrt(lax.optimization_barrier(jnp.mean(values * values, axis=-1, keepdims=True)) + epsilon) * gain

def layout(lengths, offsets, width):
    rows = jnp.arange(width, dtype=jnp.int32)
    starts = offsets[:, None]
    inside = (rows[None, :] >= starts) & (rows[None, :] < starts + lengths[:, None])
    causal = rows[:, None] >= rows[None, :]
    segment = inside[:, :, None] & inside[:, None, :] & causal[None]
    positions = (rows[None, :] - starts).astype(jnp.float32)
    return (inside.astype(jnp.float32), segment, positions)

def mamba_core(projected, conv_taps, conv_bias, step_bias, decay_log, skip_weight, mamba_gain, inside, segment):
    inner = mamba_gain.shape[0]
    heads = step_bias.shape[0]
    state = (projected.shape[-1] - 2 * inner - heads) // 2
    taps = conv_taps.shape[0]
    batch = projected.shape[0]
    length = projected.shape[1]
    gate = projected[..., :inner]
    conv_in = projected[..., inner:2 * inner + 2 * state] * inside[..., None]
    step_raw = projected[..., 2 * inner + 2 * state:]
    padded = jnp.pad(conv_in, ((0, 0), (taps - 1, 0), (0, 0)))
    convolved = conv_bias + jnp.zeros_like(conv_in)
    for tap in range(taps):
        convolved = convolved + conv_taps[tap] * padded[:, tap:tap + length]
    active = jax.nn.silu(convolved)
    head_values = active[..., :inner].reshape(batch, length, heads, inner // heads)
    b_state = active[..., inner:inner + state]
    c_state = active[..., inner + state:]
    step_size = jax.nn.softplus(step_raw + step_bias)
    cumulative = jnp.cumsum(step_size * -jnp.exp(decay_log), axis=1)
    spread = cumulative[:, :, None, :] - cumulative[:, None, :, :]
    allowed = segment[..., None]
    decay = jnp.where(allowed, jnp.exp(jnp.where(allowed, spread, 0.0)), 0.0)
    intersection = jnp.einsum('sin,sjn->sij', c_state, b_state, precision=highest)
    mixing = decay * intersection[..., None]
    scaled = head_values * step_size[..., None]
    result = jnp.einsum('sijh,sjhp->sihp', mixing, scaled, precision=highest)
    result = result + skip_weight[:, None] * head_values
    result = result.reshape(batch, length, inner) * jax.nn.silu(gate)
    return root_norm(result, mamba_gain)

def attention_core(queries, keys, values, positions, segment):
    batch = queries.shape[0]
    length = queries.shape[1]
    half = HD // 2
    freqs = rope_base ** (-jnp.arange(half, dtype=jnp.float32) * 2.0 / HD)
    angles = positions[..., None] * freqs
    cosine = jnp.cos(angles)[:, :, None, :]
    sine = jnp.sin(angles)[:, :, None, :]

    def rotate(tensor, heads):
        split = tensor.reshape(batch, length, heads, HD)
        first = split[..., :half]
        second = split[..., half:]
        return jnp.concatenate([first * cosine - second * sine, first * sine + second * cosine], axis=-1)
    rot_query = rotate(queries, QH).reshape(batch, length, KVH, QH // KVH, HD)
    rot_key = rotate(keys, KVH)
    head_values = values.reshape(batch, length, KVH, HD)
    scores = jnp.einsum('sikgd,sjkd->skgij', rot_query, rot_key, precision=highest) / math.sqrt(HD)
    allowed = segment | jnp.eye(length, dtype=jnp.bool_)[None]
    scores = jnp.where(allowed[:, None, None], scores, -1e+30)
    peak = lax.optimization_barrier(jnp.max(scores, axis=-1, keepdims=True))
    probs = jnp.exp(scores - peak)
    probs = probs / lax.optimization_barrier(jnp.sum(probs, axis=-1, keepdims=True))
    mixed = jnp.einsum('skgij,sjkd->sikgd', probs, head_values, precision=highest)
    return mixed.reshape(batch, length, QH * HD)

def layer(params, tokens, lengths, offsets):
    norm_gain, mamba_in, conv_taps, conv_bias, step_bias, decay_log, skip_weight, mamba_gain, mamba_out, query_weight, key_weight, value_weight, output_weight, second_gain, gate_weight, up_weight, down_weight = params
    inside, segment, positions = layout(lengths, offsets, tokens.shape[1])
    mask_col = inside[..., None]
    normed = low(root_norm(tokens, norm_gain))
    projected = low_back(matmul(normed, mamba_in))
    queries = low_back(matmul(normed, query_weight))
    keys = low_back(matmul(normed, key_weight))
    values = low_back(matmul(normed, value_weight))
    mamba_norm = low(mamba_core(projected, conv_taps, conv_bias, step_bias, decay_log, skip_weight, mamba_gain, inside, segment))
    attn_mix = low(attention_core(queries, keys, values, positions, segment))
    mamba_branch = low_back(matmul(mamba_norm, mamba_out))
    attn_branch = low_back(matmul(attn_mix, output_weight))
    hidden = tokens + mask_col * (mamba_branch + attn_branch)
    second = low(root_norm(hidden, second_gain))
    gate_act = low_back(matmul(second, gate_weight))
    up_act = low_back(matmul(second, up_weight))
    product = low(jax.nn.silu(gate_act) * up_act)
    return hidden + mask_col * low_back(matmul(product, down_weight))

def reference(tokens, lengths, offsets, norm_gain, mamba_in, conv_taps, conv_bias, step_bias, decay_log, skip_weight, mamba_gain, mamba_out, query_weight, key_weight, value_weight, output_weight, second_gain, gate_weight, up_weight, down_weight, cotangent):
    params = (norm_gain.astype(jnp.float32), mamba_in.astype(jnp.float32), conv_taps.astype(jnp.float32), conv_bias.astype(jnp.float32), step_bias.astype(jnp.float32), decay_log.astype(jnp.float32), skip_weight.astype(jnp.float32), mamba_gain.astype(jnp.float32), mamba_out.astype(jnp.float32), query_weight.astype(jnp.float32), key_weight.astype(jnp.float32), value_weight.astype(jnp.float32), output_weight.astype(jnp.float32), second_gain.astype(jnp.float32), gate_weight.astype(jnp.float32), up_weight.astype(jnp.float32), down_weight.astype(jnp.float32))
    count = MB * N_FSDP * N_REP
    group = math.gcd(count, max(1, 4096 // LMAX))
    sequences = tokens.astype(jnp.float32).reshape(count // group, group, LMAX, D)
    seq_lengths = lengths.reshape(count // group, group).astype(jnp.int32)
    seq_offsets = offsets.reshape(count // group, group).astype(jnp.int32)
    block = jax.checkpoint(layer)

    def forward(weights, inputs):

        def step(carry, item):
            return (carry, block(weights, item[0], item[1], item[2]))
        unused, results = lax.scan(step, jnp.zeros((), jnp.float32), (inputs, seq_lengths, seq_offsets))
        return results
    result, pull = jax.vjp(forward, params, sequences)
    grads, grad_inputs = pull(cotangent.astype(jnp.float32).reshape(result.shape))
    return (result.reshape(tokens.shape).astype(jnp.bfloat16), grad_inputs.reshape(tokens.shape), grads[0], grads[1], grads[2], grads[3], grads[4], grads[5], grads[6], grads[7], grads[8], grads[9], grads[10], grads[11], grads[12], grads[13], grads[14], grads[15], grads[16])
```

```python
import math

import jax
import jax.numpy as jnp
from jax import lax
from jax.sharding import Mesh
from jax.sharding import PartitionSpec as P

HD = 128
TP = 4

epsilon = 1e-05
rope_base = 100000000000.0
highest = lax.Precision.HIGHEST
f32 = jnp.float32
bf16 = jnp.bfloat16


def inverse_root(values):
    return lax.rsqrt(jnp.mean(values * values, axis=-1, keepdims=True) + epsilon)


def norm_back(values, root, grad):
    return root * grad - values * root**3 * jnp.mean(values * grad, axis=-1, keepdims=True)


def dot_nn(left, right):
    return jnp.dot(left, right, preferred_element_type=f32)


def dot_nt(left, right):
    return lax.dot_general(left, right, (((1,), (1,)), ((), ())), preferred_element_type=f32)


def dot_tn(left, right):
    return lax.dot_general(left, right, (((0,), (0,)), ((), ())), preferred_element_type=f32)


def layout(lengths, offsets, width):
    rows = jnp.arange(width, dtype=jnp.int32)
    starts = offsets[:, None]
    inside = (rows[None, :] >= starts) & (rows[None, :] < starts + lengths[:, None])
    causal = rows[:, None] >= rows[None, :]
    segment = inside[:, :, None] & inside[:, None, :] & causal[None]
    positions = (rows[None, :] - starts).astype(f32)
    return inside.astype(f32), segment, positions


def mamba_core(gate, conv_in, step_raw, taps, bias, step_bias, decay_log, skip_weight, inside, segment):
    batch, length, inner = gate.shape
    heads = step_bias.shape[0]
    state = (conv_in.shape[-1] - inner) // 2
    conv_in = conv_in * inside[..., None]
    padded = jnp.pad(conv_in, ((0, 0), (taps.shape[0] - 1, 0), (0, 0)))
    convolved = bias + jnp.zeros_like(conv_in)
    for tap in range(taps.shape[0]):
        convolved = convolved + taps[tap] * padded[:, tap : tap + length]
    active = jax.nn.silu(convolved)
    head_values = active[..., :inner].reshape(batch, length, heads, inner // heads)
    b_state = active[..., inner : inner + state]
    c_state = active[..., inner + state :]
    step_size = jax.nn.softplus(step_raw + step_bias)
    cumulative = jnp.cumsum(step_size * -jnp.exp(decay_log), axis=1)
    spread = cumulative[:, :, None, :] - cumulative[:, None, :, :]
    allowed = segment[..., None]
    decay = jnp.where(allowed, jnp.exp(jnp.where(allowed, spread, 0.0)), 0.0)
    intersection = jnp.einsum("sin,sjn->sij", c_state, b_state, precision=highest)
    mixing = decay * intersection[..., None]
    scaled = head_values * step_size[..., None]
    result = jnp.einsum("sijh,sjhp->sihp", mixing, scaled, precision=highest)
    result = result + skip_weight[:, None] * head_values
    return result.reshape(batch, length, inner) * jax.nn.silu(gate)


def attention_core(queries, keys, values, positions, segment):
    batch, length = queries.shape[:2]
    half = HD // 2
    freqs = rope_base ** (-jnp.arange(half, dtype=f32) * 2.0 / HD)
    angles = positions[..., None] * freqs
    cosine = jnp.cos(angles)[:, :, None, :]
    sine = jnp.sin(angles)[:, :, None, :]

    def rotate(tensor):
        split = tensor.reshape(batch, length, -1, HD)
        first = split[..., :half]
        second = split[..., half:]
        return jnp.concatenate(
            [first * cosine - second * sine, first * sine + second * cosine], axis=-1
        )

    rot_query = rotate(queries)
    rot_key = rotate(keys)[:, :, 0]
    scores = jnp.einsum("sigd,sjd->sgij", rot_query, rot_key, precision=highest) / math.sqrt(HD)
    allowed = segment | jnp.eye(length, dtype=jnp.bool_)[None]
    scores = jnp.where(allowed[:, None], scores, -1e30)
    peak = jnp.max(scores, axis=-1, keepdims=True)
    probs = jnp.exp(scores - peak)
    probs = probs / jnp.sum(probs, axis=-1, keepdims=True)
    mixed = jnp.einsum("sgij,sjd->sigd", probs, values, precision=highest)
    return mixed.reshape(batch, length, -1)


def local(
    tokens,
    lengths,
    offsets,
    norm_gain,
    mamba_in,
    conv_taps,
    conv_bias,
    step_bias,
    decay_log,
    skip_weight,
    mamba_gain,
    mamba_out,
    query_weight,
    key_weight,
    value_weight,
    output_weight,
    second_gain,
    gate_weight,
    up_weight,
    down_weight,
    cotangent,
):
    me = lax.axis_index("tp")
    peers = lax.axis_size("fs")
    batches, width, model = tokens.shape
    rows = batches * width
    shard = mamba_in.shape[0]
    inner = mamba_gain.shape[0]
    heads = step_bias.shape[0]
    state = (mamba_in.shape[1] - 2 * inner - heads) // 2
    q_cols = query_weight.shape[1]
    kv_heads = key_weight.shape[1] // HD
    hidden_units = gate_weight.shape[1]
    inner_t, heads_t, q_t, ff_t = inner // TP, heads // TP, q_cols // TP, hidden_units // TP
    kv_of = [t * kv_heads // TP for t in range(TP)]
    pad = 128

    def cut(weight, size):
        return weight.reshape(shard, TP, size).transpose(1, 0, 2)

    def same(weight):
        return jnp.broadcast_to(weight[None], (TP,) + weight.shape)

    def per_kv(weight):
        split = weight.reshape(shard, kv_heads, HD).transpose(1, 0, 2)
        return jnp.stack([split[k] for k in kv_of])

    steps = cut(mamba_in[:, 2 * inner + 2 * state :], heads_t)
    steps = jnp.concatenate(
        [
            steps,
            same(norm_gain[:, None]),
            same(second_gain[:, None]),
            jnp.zeros((TP, shard, pad - heads_t - 2), bf16),
        ],
        axis=2,
    )
    mixer_shard = jnp.concatenate(
        [
            cut(mamba_in[:, :inner], inner_t),
            cut(mamba_in[:, inner : 2 * inner], inner_t),
            same(mamba_in[:, 2 * inner : 2 * inner + 2 * state]),
            steps,
            cut(query_weight, q_t),
            per_kv(key_weight),
            per_kv(value_weight),
            cut(mamba_out.T, inner_t),
            cut(output_weight.T, q_t),
        ],
        axis=2,
    )
    mlp_shard = jnp.concatenate(
        [cut(gate_weight, ff_t), cut(up_weight, ff_t), cut(down_weight.T, ff_t)], axis=2
    )
    in_cols = mixer_shard.shape[2] - inner_t - q_t

    def collect(shards):
        mine = lax.all_to_all(shards, "tp", split_axis=0, concat_axis=0)
        return lax.all_gather(mine.reshape(TP * shard, -1), "fs", axis=0, tiled=True)

    def deliver(grads):
        part = lax.psum_scatter(grads.astype(bf16), "fs", scatter_dimension=0, tiled=True)
        part = part.reshape(TP, shard, -1)
        return lax.all_to_all(part, "tp", split_axis=0, concat_axis=0).astype(f32)

    def order(values):
        split = values.reshape(values.shape[:-1] + (TP, peers, shard))
        return jnp.swapaxes(split, -3, -2).reshape(values.shape)

    def unorder(values):
        split = values.reshape(values.shape[:-1] + (peers, TP, shard))
        return jnp.swapaxes(split, -3, -2).reshape(values.shape)

    def spread(values):
        return lax.all_gather(values, "tp", axis=0, tiled=True)

    def reduce(values):
        return lax.psum_scatter(
            values.astype(bf16), "tp", scatter_dimension=0, tiled=True
        ).astype(f32)

    mixer = collect(mixer_shard)
    mlp = collect(mlp_shard)
    w_in, w_out = mixer[:, :in_cols], mixer[:, in_cols:]
    w_gate, w_up, w_down = mlp[:, :ff_t], mlp[:, ff_t : 2 * ff_t], mlp[:, 2 * ff_t :]

    inside_own, _, _ = layout(lengths[:, 0], offsets[:, 0], width)
    mask_own = inside_own.reshape(rows, 1)
    inside, segment, positions = layout(spread(lengths[:, 0]), spread(offsets[:, 0]), width)
    mask = inside.reshape(-1, 1)
    seqs = inside.shape[0]

    source = order(tokens.reshape(rows, model))
    upstream = order(cotangent.reshape(rows, model))
    source_all = spread(source).astype(f32)
    upstream_all = spread(upstream)
    source = source.astype(f32)
    upstream = upstream.astype(f32)

    gain_col = 2 * inner_t + 2 * state + heads_t
    gain_first = w_in[:, gain_col].astype(f32)
    gain_second = w_in[:, gain_col + 1].astype(f32)

    def own(values, size):
        return lax.dynamic_slice_in_dim(values, me * size, size, axis=-1)

    taps_t = jnp.concatenate([own(conv_taps[:, :inner], inner_t), conv_taps[:, inner:]], axis=1)
    bias_t = jnp.concatenate([own(conv_bias[:inner], inner_t), conv_bias[inner:]])
    step_bias_t = own(step_bias, heads_t)
    decay_t = own(decay_log, heads_t)
    skip_t = own(skip_weight, heads_t)
    mamba_gain_t = own(mamba_gain, inner_t)

    normed = (source_all * inverse_root(source_all) * gain_first).astype(bf16)
    projected = dot_nn(normed, w_in).reshape(seqs, width, in_cols)
    conv_cols = inner_t + 2 * state
    gate = projected[..., :inner_t]
    conv_in = projected[..., inner_t : inner_t + conv_cols]
    step_raw = projected[..., inner_t + conv_cols : inner_t + conv_cols + heads_t]
    at = inner_t + conv_cols + pad
    queries, keys, values = (
        projected[..., at : at + q_t],
        projected[..., at + q_t : at + q_t + HD],
        projected[..., at + q_t + HD :],
    )
    gated, mamba_pull = jax.vjp(
        lambda *a: mamba_core(*a, inside, segment),
        gate,
        conv_in,
        step_raw,
        taps_t,
        bias_t,
        step_bias_t,
        decay_t,
        skip_t,
    )
    gated = gated.reshape(-1, inner_t)
    squares = lax.psum(jnp.sum(gated * gated, axis=-1, keepdims=True), "tp")
    mamba_root = lax.rsqrt(squares / inner + epsilon)
    mamba_norm = (gated * mamba_root * mamba_gain_t).astype(bf16)
    mixed, attn_pull = jax.vjp(
        lambda q, k, v: attention_core(q, k, v, positions, segment), queries, keys, values
    )
    branches = jnp.concatenate([mamba_norm, mixed.reshape(-1, q_t).astype(bf16)], axis=1)
    hidden = source + mask_own * reduce(dot_nt(branches, w_out))

    second_root = inverse_root(hidden)
    second = spread((hidden * second_root * gain_second).astype(bf16))
    gate_act = dot_nn(second, w_gate)
    up_act = dot_nn(second, w_up)
    product = (jax.nn.silu(gate_act) * up_act).astype(bf16)
    output = (hidden + mask_own * reduce(dot_nt(product, w_down))).astype(bf16)

    down_grad = (mask * upstream_all.astype(f32)).astype(bf16)
    d_product = dot_nn(down_grad, w_down)
    sig = jax.nn.sigmoid(gate_act)
    gate_grad = (d_product * up_act * sig * (1.0 + gate_act * (1.0 - sig))).astype(bf16)
    up_grad = (d_product * gate_act * sig).astype(bf16)
    d_second = reduce(dot_nt(gate_grad, w_gate) + dot_nt(up_grad, w_up))
    d_hidden = upstream + norm_back(hidden, second_root, d_second * gain_second)
    mlp_grads = deliver(
        jnp.concatenate(
            [dot_tn(second, gate_grad), dot_tn(second, up_grad), dot_tn(down_grad, product)], axis=1
        )
    )

    branch_grad = spread((mask_own * d_hidden).astype(bf16))
    d_branches = dot_nn(branch_grad, w_out)
    grad_out = dot_tn(branch_grad, branches)
    d_mamba = d_branches[:, :inner_t] * mamba_gain_t
    dots = lax.psum(jnp.sum(gated * d_mamba, axis=-1, keepdims=True), "tp")
    d_gated = mamba_root * d_mamba - gated * mamba_root**3 * (dots / inner)
    grad_mamba_gain = jnp.sum(gated * mamba_root * d_branches[:, :inner_t], axis=0)
    mamba_grads = mamba_pull(d_gated.reshape(seqs, width, -1))
    attn_grads = attn_pull(d_branches[:, inner_t:].reshape(seqs, width, -1))
    proj_grad = jnp.concatenate(
        [
            mamba_grads[0],
            mamba_grads[1],
            jnp.pad(mamba_grads[2], ((0, 0), (0, 0), (0, pad - heads_t))),
            attn_grads[0],
            attn_grads[1],
            attn_grads[2],
        ],
        axis=-1,
    )
    proj_grad = proj_grad.reshape(-1, in_cols).astype(bf16)
    d_normed = reduce(dot_nt(proj_grad, w_in))
    source_root = inverse_root(source)
    token_grads = unorder(d_hidden + norm_back(source, source_root, d_normed * gain_first))
    mixer_grads = deliver(jnp.concatenate([dot_tn(normed, proj_grad), grad_out], axis=1))

    def whole(grads, start, size):
        return grads[:, :, start : start + size].transpose(1, 0, 2).reshape(shard, TP * size)

    def joined(grads, start):
        split = grads[:, :, start : start + HD]
        return jnp.concatenate(
            [sum(split[t] for t in range(TP) if kv_of[t] == k) for k in range(kv_heads)], axis=1
        )

    at = inner_t + conv_cols
    grad_mamba_in = jnp.concatenate(
        [
            whole(mixer_grads, 0, inner_t),
            whole(mixer_grads, inner_t, inner_t),
            mixer_grads[:, :, 2 * inner_t : at].sum(0),
            whole(mixer_grads, at, heads_t),
        ],
        axis=1,
    )
    at += pad
    grad_query = whole(mixer_grads, at, q_t)
    grad_key = joined(mixer_grads, at + q_t)
    grad_value = joined(mixer_grads, at + q_t + HD)
    grad_mamba_out = whole(mixer_grads, in_cols, inner_t).T
    grad_output = whole(mixer_grads, in_cols + inner_t, q_t).T
    grad_gate = whole(mlp_grads, 0, ff_t)
    grad_up = whole(mlp_grads, ff_t, ff_t)
    grad_down = whole(mlp_grads, 2 * ff_t, ff_t).T

    def gain_grad(pairs, gain):
        return sum(jnp.sum(w.astype(f32) * g, axis=1) for w, g in pairs) / gain.astype(f32)

    grad_norm_gain = gain_grad(
        (
            (mamba_in, grad_mamba_in),
            (query_weight, grad_query),
            (key_weight, grad_key),
            (value_weight, grad_value),
        ),
        norm_gain,
    )
    grad_second_gain = gain_grad(((gate_weight, grad_gate), (up_weight, grad_up)), second_gain)

    small = jnp.concatenate(
        [
            mamba_grads[3].reshape(-1),
            mamba_grads[4],
            grad_mamba_gain,
            mamba_grads[5],
            mamba_grads[6],
            mamba_grads[7],
        ]
    )
    small = lax.all_gather(lax.psum(small, "fs"), "tp", axis=0)
    kernel = conv_taps.shape[0]
    conv = small[:, : (kernel + 1) * conv_cols].reshape(TP, kernel + 1, conv_cols)
    conv = jnp.concatenate(
        [conv[:, :, :inner_t].transpose(1, 0, 2).reshape(kernel + 1, inner), conv[:, :, inner_t:].sum(0)],
        axis=1,
    )
    at = (kernel + 1) * conv_cols
    return (
        unorder(output).reshape(tokens.shape),
        token_grads.reshape(tokens.shape),
        grad_norm_gain,
        grad_mamba_in,
        conv[:kernel],
        conv[kernel],
        small[:, at + inner_t : at + inner_t + heads_t].reshape(-1),
        small[:, at + inner_t + heads_t : at + inner_t + 2 * heads_t].reshape(-1),
        small[:, at + inner_t + 2 * heads_t :].reshape(-1),
        small[:, at : at + inner_t].reshape(-1),
        grad_mamba_out,
        grad_query,
        grad_key,
        grad_value,
        grad_output,
        grad_second_gain,
        grad_gate,
        grad_up,
        grad_down,
    )


def solution(mesh):
    count = mesh.devices.size
    grid = Mesh(mesh.devices.reshape(TP, count // TP), ("tp", "fs"))
    every = ("tp", "fs")
    down, across, slots = P(every, None), P(None, every), P(None, every, None)
    line, copied = P(every), P()
    return jax.shard_map(
        local,
        mesh=grid,
        in_specs=(
            slots, across, across, line, down, copied, copied, copied, copied, copied, copied,
            across, down, down, down, across, line, down, down, across, slots,
        ),
        out_specs=(
            slots, slots, line, down, copied, copied, copied, copied, copied, copied,
            across, down, down, down, across, line, down, down, across,
        ),
        check_vma=False,
    )
```

```python
import functools
import math

import jax
import jax.numpy as jnp
from jax import lax
from jax.experimental import pallas as pl
from jax.experimental.pallas import tpu as pltpu
from jax.sharding import Mesh
from jax.sharding import PartitionSpec as P

HD = 128
TP = 4

epsilon = 1e-05
rope_base = 100000000000.0
highest = lax.Precision.HIGHEST
f32 = jnp.float32
bf16 = jnp.bfloat16


def inverse_root(values):
    return lax.rsqrt(jnp.mean(values * values, axis=-1, keepdims=True) + epsilon)


def norm_back(values, root, grad):
    return root * grad - values * root**3 * jnp.mean(values * grad, axis=-1, keepdims=True)


def dot_nn(left, right):
    return jnp.dot(left, right, preferred_element_type=f32)


def dot_nt(left, right):
    return lax.dot_general(left, right, (((1,), (1,)), ((), ())), preferred_element_type=f32)


def inside_rows(length, offset, width):
    rows = jnp.arange(width, dtype=jnp.int32)[:, None]
    return ((rows >= offset) & (rows < offset + length)).astype(f32)


def turn_table(offsets, width):
    half = HD // 2
    freqs = rope_base ** (-jnp.arange(half, dtype=f32) * 2.0 / HD)
    rows = jnp.arange(width, dtype=jnp.int32)
    positions = (rows[None, :] - offsets[:, None]).astype(f32)
    angles = positions.reshape(-1, 1) * freqs
    cosine, sine = jnp.cos(angles), jnp.sin(angles)
    return jnp.concatenate([cosine, cosine, -sine, sine], axis=1)


def mm(left, right, dims, precision=lax.Precision.HIGH):
    return lax.dot_general(left, right, (dims, ((), ())), precision=precision, preferred_element_type=f32)


NN = ((1,), (0,))
NT = ((1,), (1,))
TN = ((0,), (0,))


def iota(shape, axis):
    return lax.broadcasted_iota(jnp.int32, shape, axis)


def down_rows(values, count):
    if count == 0:
        return values
    return jnp.where(iota(values.shape, 0) >= count, pltpu.roll(values, count, axis=0), 0.0)


def up_rows(values, count):
    if count == 0:
        return values
    length = values.shape[0]
    return jnp.where(
        iota(values.shape, 0) < length - count, pltpu.roll(values, length - count, axis=0), 0.0
    )


def head_sums(values, spread):
    return mm(values, spread, NT)


def mamba_shared(proj, start, count, taps_ref, bias_ref, steps_ref, inner, state, heads):
    length = proj.shape[0]
    conv_cols = inner + 2 * state
    row = iota((length, 1), 0)
    inside = ((row >= start) & (row < start + count)).astype(f32)
    conv_in = proj[:, inner : inner + conv_cols] * inside
    kernel = taps_ref.shape[0]
    conv = bias_ref[...] + jnp.zeros_like(conv_in)
    for tap in range(kernel):
        conv = conv + taps_ref[tap : tap + 1, :] * down_rows(conv_in, kernel - 1 - tap)
    sig = jax.nn.sigmoid(conv)
    active = conv * sig
    pad = steps_ref.shape[1]
    lane = iota((length, pad), 1)
    raw = jnp.where(lane < heads, proj[:, inner + conv_cols : inner + conv_cols + pad] + steps_ref[0:1, :], 0.0)
    step = jnp.where(lane < heads, jnp.maximum(raw, 0.0) + jnp.log1p(jnp.exp(-jnp.abs(raw))), 0.0)
    rate = -jnp.exp(steps_ref[1:2, :])
    lower = (iota((length, length), 0) >= iota((length, length), 1)).astype(f32)
    cum = mm(lower, step * rate, NN, highest)
    size = inner // heads
    spread = (iota((pad, inner), 0) == iota((pad, inner), 1) // size).astype(f32)
    step_x = mm(step, spread, NN)
    cum_x = mm(cum, spread, NN, highest)
    at = iota((length, inner), 1) % length
    diagonal = iota((length, inner), 0) == at
    cum_row = jnp.sum(jnp.where(diagonal, cum_x, 0.0), axis=0, keepdims=True)
    allowed = (
        (at <= iota((length, inner), 0)) & (inside > 0.0) & (at >= start) & (at < start + count)
    )
    decay = jnp.where(allowed, jnp.exp(jnp.where(allowed, cum_x - cum_row, 0.0)), 0.0)
    xs = active[:, :inner]
    b_state = active[:, inner : inner + state]
    c_state = active[:, inner + state :]
    inter = mm(c_state, b_state, NT)
    pair = jnp.concatenate([inter, inter], axis=1)
    mixing = decay * jnp.concatenate([pair] * (inner // pair.shape[1]), axis=1)
    return dict(
        inside=inside, conv_in=conv_in, conv=conv, sig=sig, raw=raw, step=step, rate=rate,
        spread=spread, step_x=step_x, diagonal=diagonal, decay=decay, mixing=mixing, xs=xs,
        b_state=b_state, c_state=c_state, lower=lower, lane=lane,
    )


def two_blocks(values):
    left = iota(values.shape, 1) < values.shape[1] // 2
    return jnp.concatenate([jnp.where(left, values, 0.0), jnp.where(left, 0.0, values)], axis=0)


def turn(values, cosine, sine):
    return values * cosine + pltpu.roll(values, HD // 2, axis=1) * sine


def attention_shared(proj, at, start, count, cosine, sine):
    length = proj.shape[0]
    kv = proj.shape[1] - 2 * HD
    queries = jnp.concatenate(
        [turn(proj[:, c : c + HD], cosine, sine) for c in range(at, kv, HD)], axis=0
    )
    keys = turn(proj[:, kv : kv + HD], cosine, sine)
    values = proj[:, kv + HD :]
    scores = mm(queries, keys, NT) * (1.0 / math.sqrt(HD))
    row = iota(scores.shape, 0) % length
    col = iota(scores.shape, 1)
    end = start + count
    allowed = ((row >= start) & (row < end) & (col >= start) & (col <= row)) | (row == col)
    scores = jnp.where(allowed, scores, -1e30)
    probs = jnp.exp(scores - jnp.max(scores, axis=1, keepdims=True))
    probs = probs / jnp.sum(probs, axis=1, keepdims=True)
    return queries, keys, values, probs


def specs(*shapes):
    return [pl.BlockSpec(s, lambda i: (0, 0)) for s in shapes]


def rows_spec(length, cols):
    return pl.BlockSpec((length, cols), lambda i: (i, 0))


def their_spec(length, each, k):
    return pl.BlockSpec((1, 1, length), lambda i: (i ^ (THEIRS[k][0] * each), 0, 0))


big = pltpu.CompilerParams(vmem_limit_bytes=50 * 1024 * 1024)


def costs(microseconds):
    return pl.CostEstimate(
        flops=microseconds * 10**9, bytes_accessed=microseconds * 10**5, transcendentals=0
    )


def inside_of(slots_ref, seq, length):
    row = iota((length, 1), 0)
    start = slots_ref[seq, 1]
    return ((row >= start) & (row < start + slots_ref[seq, 0])).astype(f32)


def as_row(column):
    length = column.shape[0]
    same = iota((length, length), 0) == iota((length, length), 1)
    return jnp.sum(jnp.where(same, column, 0.0), axis=0, keepdims=True)


def as_column(row):
    length = row.shape[1]
    same = iota((length, length), 0) == iota((length, length), 1)
    return jnp.sum(jnp.where(same, row, 0.0), axis=1, keepdims=True)


THEIRS = ((0, 1, 2, 3), (2, 3, 0, 1), (3, 2, 1, 0), (1, 0, 3, 2))


def group_total(refs, seq):
    each = refs[0].shape[0] // TP
    return sum(ref[THEIRS[k][seq // each] * each + seq % each] for k, ref in enumerate(refs))


def joined_rows(refs):
    own, far, pair, near, last = refs
    half = far.shape[1]
    count = own.shape[0]
    left = jnp.concatenate([own[:, :half], far[...], pair[...]], axis=0)
    right = jnp.concatenate([own[:, half:], last[:count, :], near[...], last[count:, :]], axis=0)
    return jnp.concatenate([left, right], axis=1)


def put_left(values, refs):
    half = values.shape[0] // 2
    refs[0][...] = values[:half]
    refs[1][...] = values[half:].astype(bf16)


def put_right(values, refs):
    one = values.shape[0] // TP
    refs[2][:one, :] = values[:one]
    refs[2][one:, :] = values[2 * one : 3 * one]
    refs[3][:one, :] = values[one : 2 * one].astype(bf16)
    refs[3][one:, :] = values[3 * one :].astype(bf16)


def put_tiles(values, refs):
    step = pl.program_id(0)
    middle = pl.num_programs(0) // 2

    @pl.when(step < middle)
    def _():
        put_left(values, refs)

    @pl.when(step >= middle)
    def _():
        put_right(values, refs)


def halves_out(rows, model, tile):
    middle = model // tile // 2
    left = pl.BlockSpec((rows // 2, tile), lambda j: (0, jnp.minimum(j, middle - 1)))
    right = pl.BlockSpec((rows // 2, tile), lambda j: (0, jnp.maximum(j - middle, 0)))
    shapes = [jax.ShapeDtypeStruct((rows // 2, model // 2), t) for t in (f32, bf16, f32, bf16)]
    return [left, left, right, right], shapes


def both_halves(refs):
    kept, got, kept_right, got_right = refs
    return jnp.concatenate(
        [kept[...] + got[...].astype(f32), kept_right[...] + got_right[...].astype(f32)], axis=1
    )


def inner_kernel(
    inner, state, heads, tiles, slots_ref, p0, p1, p2, p3, p4, weight_ref, gains_in_ref, taps_ref, bias_ref,
    steps_ref, skip_ref, turn_ref, normed_ref, proj_ref, y_ref, square_ref, mixed_ref, gains_ref,
):
    step = pl.program_id(0)
    tile = weight_ref.shape[1]

    @pl.when(step == 0)
    def _():
        rows = joined_rows((p0, p1, p2, p3, p4)).astype(f32)
        turned = jnp.transpose(gains_in_ref[...].astype(f32))
        gains_ref[0:1, :] = turned[heads : heads + 1]
        gains_ref[1:2, :] = turned[heads + 1 : heads + 2]
        normed_ref[...] = (rows * inverse_root(rows) * turned[heads : heads + 1]).astype(bf16)

    @pl.when(step < tiles)
    def _():
        at = pl.multiple_of(step * tile, tile)
        proj_ref[:, pl.ds(at, tile)] = jnp.dot(
            normed_ref[...], weight_ref[...], preferred_element_type=f32
        )

    @pl.when(step >= tiles)
    def _():
        seq = step - tiles
        length = y_ref.shape[0]
        proj = proj_ref[pl.ds(pl.multiple_of(seq * length, length), length), :]
        start = slots_ref[seq, 1]
        count = slots_ref[seq, 0]
        m = mamba_shared(proj, start, count, taps_ref, bias_ref, steps_ref, inner, state, heads)
        scaled = m["xs"] * m["step_x"]
        wide = 2 * length
        parts = [
            mm(m["mixing"][:, c : c + wide], two_blocks(scaled[:, c : c + wide]), NN)
            for c in range(0, inner, wide)
        ]
        y = jnp.concatenate(parts, axis=1) + skip_ref[...] * m["xs"]
        y_ref[...] = y
        gate = proj[:, :inner]
        gated = y * gate * jax.nn.sigmoid(gate)
        square_ref[0] = as_row(jnp.sum(gated * gated, axis=1, keepdims=True))
        at = 2 * inner + 2 * state + steps_ref.shape[1]
        _, _, values, probs = attention_shared(
            proj, at, start, count, turn_ref[:, :HD], turn_ref[:, HD:]
        )
        mixed = mm(probs, values, NN)
        mixed_ref[...] = jnp.concatenate(
            [mixed[r : r + length] for r in range(0, mixed.shape[0], length)], axis=1
        ).astype(mixed_ref.dtype)


def mixer_inner(slots, rows, weight, taps, bias, steps, skip, turns, inner, state, heads, tile=384):
    model, cols = weight.shape
    seqs = slots.shape[0]
    pieces = rows
    rows = TP * pieces[0].shape[0]
    length = rows // seqs
    tiles = cols // tile
    pad = steps.shape[1]
    at_steps = (2 * inner + 2 * state) // pad
    q_cols = cols - 2 * inner - 2 * state - pad - 2 * HD

    def seq_spec(*shape):
        zeros = (0,) * (len(shape) - 1)
        return pl.BlockSpec(shape, lambda j: (jnp.maximum(j - tiles, 0),) + zeros)

    return pl.pallas_call(
        functools.partial(inner_kernel, inner, state, heads, tiles),
        grid=(tiles + seqs,),
        in_specs=[pl.BlockSpec(memory_space=pltpu.SMEM)]
        + specs(*[p.shape for p in pieces])
        + [
            pl.BlockSpec((model, tile), lambda j: (0, jnp.minimum(j, tiles - 1))),
            pl.BlockSpec((model, pad), lambda j: (0, at_steps)),
        ]
        + specs(taps.shape, bias.shape, steps.shape, skip.shape)
        + [seq_spec(length, turns.shape[1])],
        out_specs=specs((rows, model), (rows, cols))
        + [seq_spec(length, inner), seq_spec(1, 1, length), seq_spec(length, q_cols)]
        + specs((8, model)),
        out_shape=[
            jax.ShapeDtypeStruct((rows, model), bf16),
            jax.ShapeDtypeStruct((rows, cols), f32),
            jax.ShapeDtypeStruct((rows, inner), f32),
            jax.ShapeDtypeStruct((seqs, 1, length), f32),
            jax.ShapeDtypeStruct((rows, q_cols), bf16),
            jax.ShapeDtypeStruct((8, model), f32),
        ],
        compiler_params=big,
        cost_estimate=costs(18),
    )(slots, *pieces, weight, weight, taps, bias, steps, skip, turns)


def outer_kernel(inner, gate_ref, y_ref, mixed_ref, gain_ref, s0, s1, s2, s3, weight_ref, branches_ref, root_ref, *halves):
    @pl.when(pl.program_id(0) == 0)
    def _():
        length = root_ref.shape[2]
        for seq in range(root_ref.shape[0]):
            rows = slice(seq * length, (seq + 1) * length)
            root = lax.rsqrt(group_total((s0, s1, s2, s3), seq) / (TP * inner) + epsilon)
            root_ref[seq] = root
            gate = gate_ref[rows, :]
            gated = y_ref[rows, :] * gate * jax.nn.sigmoid(gate)
            branches_ref[rows, :inner] = (gated * as_column(root) * gain_ref[...]).astype(bf16)
        branches_ref[:, inner:] = mixed_ref[...]

    put_tiles(dot_nt(branches_ref[...], weight_ref[...]), halves)


def mixer_outer(proj, y, mixed, gain, squares, weight, tile=512):
    rows, inner = y.shape
    model, cols = weight.shape
    half_specs, half_shapes = halves_out(rows, model, tile)
    return pl.pallas_call(
        functools.partial(outer_kernel, inner),
        grid=(model // tile,),
        in_specs=specs((rows, inner), y.shape, mixed.shape, gain.shape)
        + [pl.BlockSpec(squares[0].shape, lambda j: (0, 0, 0))] * TP
        + [pl.BlockSpec((tile, cols), lambda j: (j, 0))],
        out_specs=specs((rows, cols))
        + [pl.BlockSpec(squares[0].shape, lambda j: (0, 0, 0))]
        + half_specs,
        out_shape=[
            jax.ShapeDtypeStruct((rows, cols), bf16),
            jax.ShapeDtypeStruct(squares[0].shape, f32),
        ]
        + half_shapes,
        compiler_params=big,
        cost_estimate=costs(4),
    )(proj, y, mixed, gain, *squares, weight)


def back_out_kernel(left_ref, weight_ref, *halves):
    put_tiles(dot_nt(left_ref[...], weight_ref[...]), halves)


def back_out(left, weight, column, tile=512):
    rows, cols = left.shape
    model = weight.shape[0]
    half_specs, half_shapes = halves_out(rows, model, tile)
    return pl.pallas_call(
        back_out_kernel,
        grid=(model // tile,),
        in_specs=specs(left.shape) + [pl.BlockSpec((tile, cols), lambda j: (j, column))],
        out_specs=half_specs,
        out_shape=half_shapes,
        compiler_params=big,
        cost_estimate=costs(4),
    )(left, weight)


def inside_all(slots_ref, seqs, length):
    return jnp.concatenate([inside_of(slots_ref, seq, length) for seq in range(seqs)], axis=0)


def hidden_kernel(slots_ref, k0, k1, k2, k3, source_ref, gains_ref, hidden_ref, second_ref):
    length = source_ref.shape[0] * TP // slots_ref.shape[0]
    inside = inside_all(slots_ref, slots_ref.shape[0] // TP, length)
    hidden = source_ref[...].astype(f32) + inside * both_halves((k0, k1, k2, k3))
    hidden_ref[...] = hidden
    second_ref[...] = (hidden * inverse_root(hidden) * gains_ref[1:2, :]).astype(bf16)


def row_call(kernel, slots, halves, *others):
    shape = others[0].shape
    return pl.pallas_call(
        kernel,
        grid=(1,),
        in_specs=[pl.BlockSpec(memory_space=pltpu.SMEM)]
        + specs(*[h.shape for h in halves], *[o.shape for o in others]),
        out_specs=specs(shape, shape),
        out_shape=[jax.ShapeDtypeStruct(shape, f32), jax.ShapeDtypeStruct(shape, bf16)],
        compiler_params=big,
        cost_estimate=costs(2),
    )(slots, *halves, *others)


def feed_kernel(
    slots_ref, s0, s1, s2, s3, s4, c0, c1, c2, c3, c4, gate_ref, up_ref, down_ref,
    second_ref, down_grad_ref, product_ref, gate_grad_ref, up_grad_ref, h0, h1, h2, h3, total,
):
    step = pl.program_id(0)

    @pl.when(step == 0)
    def _():
        second_ref[...] = joined_rows((s0, s1, s2, s3, s4))
        seqs = slots_ref.shape[0]
        inside = inside_all(slots_ref, seqs, TP * s0.shape[0] // seqs)
        down_grad_ref[...] = (inside * joined_rows((c0, c1, c2, c3, c4)).astype(f32)).astype(bf16)
        total[...] = jnp.zeros_like(total)

    second = second_ref[...]
    gate = jnp.dot(second, gate_ref[...], preferred_element_type=f32)
    up = jnp.dot(second, up_ref[...], preferred_element_type=f32)
    d_product = jnp.dot(down_grad_ref[...], down_ref[...], preferred_element_type=f32)
    sig = jax.nn.sigmoid(gate)
    swish = gate * sig
    product_ref[...] = (swish * up).astype(bf16)
    gate_grad = (d_product * up * sig * (1.0 + gate * (1.0 - sig))).astype(bf16)
    up_grad = (d_product * swish).astype(bf16)
    gate_grad_ref[...] = gate_grad
    up_grad_ref[...] = up_grad
    total[...] += dot_nt(gate_grad, gate_ref[...]) + dot_nt(up_grad, up_ref[...])

    @pl.when(step == pl.num_programs(0) - 1)
    def _():
        middle = total.shape[1] // 2
        put_left(total[:, :middle], (h0, h1))
        put_right(total[:, middle:], (h0, h1, h2, h3))


def feed_forward(slots, second, cotangent, weight, units, tile=512):
    count, model = second[0].shape
    rows = TP * count
    steps = units // tile
    half_shapes = halves_out(rows, model, tile)[1]
    shapes = [p.shape for p in second]
    unit = pl.BlockSpec((rows, tile), lambda j: (0, j))
    return pl.pallas_call(
        feed_kernel,
        grid=(steps,),
        in_specs=[pl.BlockSpec(memory_space=pltpu.SMEM)]
        + specs(*shapes, *shapes)
        + [
            pl.BlockSpec((model, tile), lambda j, at=at: (0, at * steps + j))
            for at in range(3)
        ],
        out_specs=specs((rows, model), (rows, model))
        + [unit] * 3
        + specs(*[h.shape for h in half_shapes]),
        out_shape=[jax.ShapeDtypeStruct((rows, model), bf16)] * 2
        + [jax.ShapeDtypeStruct((rows, units), bf16)] * 3
        + half_shapes,
        scratch_shapes=[pltpu.VMEM((rows, model), f32)],
        compiler_params=big,
        cost_estimate=costs(9),
    )(slots, *second, *cotangent, weight, weight, weight)


def back_hidden_kernel(slots_ref, k0, k1, k2, k3, hidden_ref, cotangent_ref, gains_ref, d_hidden_ref, branch_ref):
    grad = both_halves((k0, k1, k2, k3)) * gains_ref[1:2, :]
    hidden = hidden_ref[...]
    d_hidden = cotangent_ref[...].astype(f32) + norm_back(hidden, inverse_root(hidden), grad)
    d_hidden_ref[...] = d_hidden
    seqs = slots_ref.shape[0]
    inside = inside_all(slots_ref, seqs // TP, hidden.shape[0] * TP // seqs)
    branch_ref[...] = (inside * d_hidden).astype(bf16)


def back_outer_kernel(tiles, b0, b1, b2, b3, b4, weight_ref, gate_ref, y_ref, gain_ref, branch_ref, grad_ref, dots_ref, total):
    step = pl.program_id(0)

    @pl.when(step == 0)
    def _():
        branch_ref[...] = joined_rows((b0, b1, b2, b3, b4))
        total[...] = jnp.zeros_like(total)

    grad = jnp.dot(branch_ref[...], weight_ref[...], preferred_element_type=f32)
    grad_ref[...] = grad

    @pl.when(step < tiles)
    def _():
        gate = gate_ref[...]
        gated = y_ref[...] * gate * jax.nn.sigmoid(gate)
        total[...] += jnp.sum(gated * gain_ref[...] * grad, axis=1, keepdims=True)

    @pl.when(step == pl.num_programs(0) - 1)
    def _():
        length = dots_ref.shape[2]
        for seq in range(dots_ref.shape[0]):
            dots_ref[seq] = as_row(total[seq * length : (seq + 1) * length, :])


def back_outer(branch, weight, proj, y, gain, seqs, tile=256):
    model = weight.shape[0]
    rows, inner = y.shape
    cols = weight.shape[1]
    tiles = inner // tile
    length = rows // seqs
    inner_spec = pl.BlockSpec((rows, tile), lambda j: (0, jnp.minimum(j, tiles - 1)))
    return pl.pallas_call(
        functools.partial(back_outer_kernel, tiles),
        grid=(cols // tile,),
        in_specs=specs(*[p.shape for p in branch])
        + [
            pl.BlockSpec((model, tile), lambda j: (0, j)),
            inner_spec,
            inner_spec,
            pl.BlockSpec((1, tile), lambda j: (0, jnp.minimum(j, tiles - 1))),
        ],
        out_specs=specs((rows, model))
        + [
            pl.BlockSpec((rows, tile), lambda j: (0, j)),
            pl.BlockSpec((seqs, 1, length), lambda j: (0, 0, 0)),
        ],
        out_shape=[
            jax.ShapeDtypeStruct((rows, model), bf16),
            jax.ShapeDtypeStruct((rows, cols), f32),
            jax.ShapeDtypeStruct((seqs, 1, length), f32),
        ],
        scratch_shapes=[pltpu.VMEM((rows, 1), f32)],
        compiler_params=big,
        cost_estimate=costs(5),
    )(*branch, weight, proj, y, gain)


def backward_kernel(
    inner, state, heads, slots_ref, proj_ref, taps_ref, bias_ref, steps_ref, skip_ref, turn_ref,
    gain_ref, y_ref, grad_ref, root_ref, d0, d1, d2, d3, proj_grad_ref, conv_grad_ref, inner_grad_ref, step_grad_ref,
):
    step_id = pl.program_id(0)
    start = slots_ref[step_id, 1]
    count = slots_ref[step_id, 0]
    proj = proj_ref[...]
    length = proj.shape[0]
    conv_cols = inner + 2 * state
    pad = steps_ref.shape[1]
    m = mamba_shared(proj, start, count, taps_ref, bias_ref, steps_ref, inner, state, heads)
    xs, decay, mixing = m["xs"], m["decay"], m["mixing"]
    scaled = xs * m["step_x"]
    gate = proj[:, :inner]
    gate_sig = jax.nn.sigmoid(gate)
    y = y_ref[...]
    root = as_column(root_ref[0])
    mean = as_column(sum(ref[0] for ref in (d0, d1, d2, d3))) / (TP * inner)
    gated = y * gate * gate_sig
    d_norm = grad_ref[:, :inner]
    d_gated = root * (d_norm * gain_ref[...]) - gated * (root * root * root * mean)
    dy = d_gated * gate * gate_sig
    d_gate = d_gated * y * gate_sig * (1.0 + gate * (1.0 - gate_sig))
    wide = 2 * length
    back, d_mix = [], []
    for c in range(0, inner, wide):
        dy_pair = dy[:, c : c + wide]
        full = mm(mixing[:, c : c + wide], dy_pair, TN)
        left = iota((length, wide), 1) < length
        back.append(jnp.where(left, full[:length], full[length:]))
        d_mix.append(mm(dy_pair, two_blocks(scaled[:, c : c + wide]), NT))
    back = jnp.concatenate(back, axis=1)
    d_mix = jnp.concatenate(d_mix, axis=1)
    d_xs = skip_ref[...] * dy + m["step_x"] * back
    flow = d_mix * mixing
    flow = flow - jnp.where(m["diagonal"], jnp.sum(flow, axis=0, keepdims=True), 0.0)
    d_cum = head_sums(flow, m["spread"])
    d_rate = mm(m["lower"], d_cum, TN, highest)
    d_step = head_sums(xs * back, m["spread"]) + d_rate * m["rate"]
    d_raw = jnp.where(m["lane"] < heads, d_step * jax.nn.sigmoid(m["raw"]), 0.0)
    d_inter = d_mix * decay
    pair = d_inter[:, :wide]
    for c in range(wide, inner, wide):
        pair = pair + d_inter[:, c : c + wide]
    d_inter = pair[:, :length] + pair[:, length:]
    d_b = mm(d_inter, m["c_state"], TN)
    d_c = mm(d_inter, m["b_state"], NN)
    d_active = jnp.concatenate([d_xs, d_b, d_c], axis=1)
    sig, conv = m["sig"], m["conv"]
    d_conv = d_active * sig * (1.0 + conv * (1.0 - sig))
    kernel = taps_ref.shape[0]
    d_in = jnp.zeros_like(d_conv)
    conv_rows = []
    for tap in range(kernel):
        back_by = kernel - 1 - tap
        d_in = d_in + taps_ref[tap : tap + 1, :] * up_rows(d_conv, back_by)
        conv_rows.append(jnp.sum(d_conv * down_rows(m["conv_in"], back_by), axis=0, keepdims=True))
    conv_rows.append(jnp.sum(d_conv, axis=0, keepdims=True))
    conv_rows.append(jnp.zeros((8 - kernel - 1, conv_cols), f32))
    conv_rows = jnp.concatenate(conv_rows, axis=0)
    inner_rows = jnp.concatenate(
        [
            jnp.sum(gated * root * d_norm, axis=0, keepdims=True),
            jnp.sum(dy * xs, axis=0, keepdims=True),
            jnp.zeros((6, inner), f32),
        ],
        axis=0,
    )
    step_rows = jnp.concatenate(
        [
            jnp.sum(d_raw, axis=0, keepdims=True),
            jnp.sum(d_rate * m["step"] * m["rate"], axis=0, keepdims=True),
            jnp.zeros((6, pad), f32),
        ],
        axis=0,
    )

    @pl.when(step_id == 0)
    def _():
        conv_grad_ref[...] = jnp.zeros_like(conv_grad_ref)
        inner_grad_ref[...] = jnp.zeros_like(inner_grad_ref)
        step_grad_ref[...] = jnp.zeros_like(step_grad_ref)

    conv_grad_ref[...] += conv_rows
    inner_grad_ref[...] += inner_rows
    step_grad_ref[...] += step_rows

    at = inner + conv_cols + pad
    cosine, sine = turn_ref[:, :HD], turn_ref[:, HD:]
    queries, keys, values, probs = attention_shared(proj, at, start, count, cosine, sine)
    d_out = jnp.concatenate(
        [grad_ref[:, c : c + HD] for c in range(inner, grad_ref.shape[1], HD)], axis=0
    )
    d_values = mm(probs, d_out, TN)
    d_probs = mm(d_out, values, NT)
    d_scores = probs * (d_probs - jnp.sum(probs * d_probs, axis=1, keepdims=True)) * (1.0 / math.sqrt(HD))
    d_queries = mm(d_scores, keys, NN)
    d_keys = mm(d_scores, queries, TN)
    outs = [d_gate, d_in * m["inside"], d_raw]
    outs += [turn(d_queries[r : r + length], cosine, -sine) for r in range(0, d_queries.shape[0], length)]
    outs += [turn(d_keys, cosine, -sine), d_values]
    proj_grad_ref[...] = jnp.concatenate(outs, axis=1).astype(proj_grad_ref.dtype)


def mixer_backward(
    slots, proj, taps, bias, steps, skip, turns, gain, y, grads, root, dots, inner, state, heads
):
    seqs = slots.shape[0]
    rows, cols = proj.shape
    length = rows // seqs
    conv_cols = inner + 2 * state
    pad = steps.shape[1]
    return pl.pallas_call(
        functools.partial(backward_kernel, inner, state, heads),
        grid=(seqs,),
        in_specs=[pl.BlockSpec(memory_space=pltpu.SMEM), rows_spec(length, cols)]
        + specs(taps.shape, bias.shape, steps.shape, skip.shape)
        + [rows_spec(length, turns.shape[1])]
        + specs(gain.shape)
        + [rows_spec(length, inner), rows_spec(length, grads.shape[1])]
        + [pl.BlockSpec((1, 1, length), lambda i: (i, 0, 0))]
        + [their_spec(length, seqs // TP, k) for k in range(TP)],
        out_specs=[rows_spec(length, cols)] + specs((8, conv_cols), (8, inner), (8, pad)),
        out_shape=[
            jax.ShapeDtypeStruct((rows, cols), bf16),
            jax.ShapeDtypeStruct((8, conv_cols), f32),
            jax.ShapeDtypeStruct((8, inner), f32),
            jax.ShapeDtypeStruct((8, pad), f32),
        ],
        compiler_params=big,
        cost_estimate=costs(17),
    )(slots, proj, taps, bias, steps, skip, turns, gain, y, grads, root, *dots)


def chip_kernel(keep_ref, got_ref, mine_ref, along_y_ref, along_x_ref, across_x_ref, across_y_ref):
    total = (keep_ref[...].astype(f32) + got_ref[...].astype(f32)).astype(bf16)
    block = mine_ref.shape[0]
    half = across_x_ref.shape[0]
    mine_ref[...] = total[:block]
    along_y_ref[...] = total[block : 2 * block]
    along_x_ref[...] = total[2 * block : 3 * block]
    across_x_ref[...] = total[3 * block : 3 * block + half]
    across_y_ref[...] = total[3 * block + half :]


def along_kernel(along_y_ref, along_x_ref, by_x_ref, by_y_ref, to_y_ref, to_x_ref):
    half = by_x_ref.shape[0]
    to_y_ref[...] = along_y_ref[...]
    to_y_ref[:half, :] = (along_y_ref[:half, :].astype(f32) + by_x_ref[...].astype(f32)).astype(bf16)
    to_x_ref[...] = along_x_ref[...]
    to_x_ref[half:, :] = (along_x_ref[half:, :].astype(f32) + by_y_ref[...].astype(f32)).astype(bf16)


def plane_kernel(mine_ref, by_x_ref, by_y_ref, *outs):
    total = mine_ref[...].astype(f32) + by_x_ref[...].astype(f32) + by_y_ref[...].astype(f32)
    size = outs[0].shape[0]
    for k, out in enumerate(outs):
        out[...] = total[k * size : (k + 1) * size].astype(bf16)


def by_columns(kernel, row_counts, *arrays, tile=896):
    cols = arrays[0].shape[1]

    def of(rows):
        return pl.BlockSpec((rows, tile), lambda j: (0, j))

    return pl.pallas_call(
        kernel,
        grid=(cols // tile,),
        in_specs=[of(a.shape[0]) for a in arrays],
        out_specs=[of(r) for r in row_counts],
        out_shape=[jax.ShapeDtypeStruct((r, cols), bf16) for r in row_counts],
        compiler_params=big,
        cost_estimate=costs(3),
    )(*arrays)


def own_columns(me, refs, start, size, out_ref, at=0):
    for k, ref in enumerate(refs):
        place = pl.multiple_of((me ^ k) * size, 128)
        out_ref[:, pl.ds(at + place, size)] = ref[:, start : start + size].astype(f32)


def gain_sum(pairs, gain_ref):
    total = sum(
        jnp.sum(weight[...].astype(f32) * grad[...], axis=1, keepdims=True) for weight, grad in pairs
    )
    return total / gain_ref[...].astype(f32)


def unpack_mlp_kernel(units, me_ref, g0, g1, g2, g3, gate_ref, up_ref, gain_ref, grad_gate, grad_up, grad_down, grad_gain):
    for i, out in enumerate((grad_gate, grad_up, grad_down)):
        own_columns(me_ref[0], (g0, g1, g2, g3), i * units, units, out)
    grad_gain[...] = gain_sum(((gate_ref, grad_gate), (up_ref, grad_up)), gain_ref)


def unpack_out_kernel(inner, q_cols, me_ref, g0, g1, g2, g3, grad_mamba, grad_output):
    own_columns(me_ref[0], (g0, g1, g2, g3), 0, inner, grad_mamba)
    own_columns(me_ref[0], (g0, g1, g2, g3), inner, q_cols, grad_output)


def unpack_in_kernel(
    inner, state, heads, pad, me_ref, g0, g1, g2, g3, mamba_ref, query_ref, key_ref, value_ref, gain_ref,
    grad_mamba, grad_query, grad_key, grad_value, grad_gain,
):
    me = me_ref[0]
    refs = (g0, g1, g2, g3)
    own_columns(me, refs, 0, inner, grad_mamba)
    own_columns(me, refs, inner, inner, grad_mamba, TP * inner)
    at, out_at = 2 * inner, 2 * TP * inner
    shared = sum(ref[:, at : at + 2 * state].astype(f32) for ref in refs)
    grad_mamba[:, out_at : out_at + 2 * state] = shared
    at, out_at = at + 2 * state, out_at + 2 * state
    lane = iota((grad_mamba.shape[0], pad), 1)
    steps = jnp.zeros((grad_mamba.shape[0], pad), f32)
    for k, ref in enumerate(refs):
        piece = jnp.where(lane < heads, ref[:, at : at + pad].astype(f32), 0.0)
        steps = steps + pltpu.roll(piece, (me ^ k) * heads, axis=1)
    grad_mamba[:, out_at : out_at + TP * heads] = steps[:, : TP * heads]
    at += pad
    q_cols = query_ref.shape[1] // TP
    own_columns(me, refs, at, q_cols, grad_query)
    at += q_cols
    for out, start in ((grad_key, at), (grad_value, at + HD)):
        for first in (0, 2):
            both = refs[first][:, start : start + HD].astype(f32)
            both = both + refs[first + 1][:, start : start + HD].astype(f32)
            place = pl.multiple_of(((me ^ first) // 2) * HD, HD)
            out[:, pl.ds(place, HD)] = both
    pairs = ((mamba_ref, grad_mamba), (query_ref, grad_query), (key_ref, grad_key), (value_ref, grad_value))
    grad_gain[...] = gain_sum(pairs, gain_ref)


def unpack(kernel, me, parts, others, widths):
    rows = parts[0].shape[0]
    shapes = [(rows, w) for w in widths]
    return pl.pallas_call(
        kernel,
        grid=(1,),
        in_specs=[pl.BlockSpec(memory_space=pltpu.SMEM)]
        + specs(*[p.shape for p in parts], *[o.shape for o in others]),
        out_specs=specs(*shapes),
        out_shape=[jax.ShapeDtypeStruct(shape, f32) for shape in shapes],
        compiler_params=big,
        cost_estimate=costs(5),
    )(me, *parts, *others)


def weight_grad_kernel(bounds, mine, blocks, table_ref, *refs):
    parts = len(bounds)
    lefts = [refs[2 * mine * p : 2 * mine * p + mine] for p in range(parts)]
    rights = [refs[2 * mine * p + mine : 2 * mine * (p + 1)] for p in range(parts)]
    rest = refs[2 * mine * parts :]
    outs, plain, turned = rest[: -1 - parts], rest[-1 - parts], rest[-parts:]
    step = pl.program_id(0)
    size = plain.shape[0] // blocks

    @pl.when(step == 0)
    def _():
        for part in range(parts):
            plain[...] = jnp.concatenate([jnp.transpose(ref[...]) for ref in lefts[part]], axis=1)
            for block in range(blocks):
                at = pl.multiple_of(table_ref[block] * size, size)
                turned[part][block * size : (block + 1) * size, :] = plain[pl.ds(at, size), :]

    for part, (low, high) in enumerate(bounds):

        @pl.when((step >= low) & (step < high))
        def _(part=part):
            right = jnp.concatenate([ref[...] for ref in rights[part]], axis=0)
            full = jnp.dot(turned[part][...], right, preferred_element_type=f32)
            half = full.shape[0] // len(outs)
            for i, out in enumerate(outs):
                out[...] = full[i * half : (i + 1) * half].astype(out.dtype)


def weight_grads(table, pieces, pairs, tile=512):
    mine = len(pairs[0][0])
    rows, model = pairs[0][0][0].shape
    bounds, specs_in, args, low, cols = [], [], [], 0, 0
    for left, right, start, count in pairs:
        tiles = pl.cdiv(count, tile)
        first, last = low - start // tile, low + tiles - 1
        specs_in += [pl.BlockSpec((rows, model), lambda j: (0, 0))] * mine
        specs_in += [
            pl.BlockSpec(
                (rows, tile),
                lambda j, low=low, last=last, first=first: (0, jnp.clip(j, low, last) - first),
            )
        ] * mine
        args += list(left) + list(right)
        bounds.append((low, low + tiles))
        low += tiles
        cols += count
    return pl.pallas_call(
        functools.partial(weight_grad_kernel, tuple(bounds), mine, table.shape[0]),
        grid=(low,),
        in_specs=[pl.BlockSpec(memory_space=pltpu.SMEM)] + specs_in,
        out_specs=[pl.BlockSpec((model // pieces, tile), lambda j: (0, j))] * pieces,
        out_shape=[jax.ShapeDtypeStruct((model // pieces, cols), bf16)] * pieces,
        scratch_shapes=[pltpu.VMEM((model, mine * rows), bf16)] * (1 + len(pairs)),
        compiler_params=big,
        cost_estimate=costs(1 + cols // 256),
    )(table, *args)


def local(
    plane,
    tokens,
    lengths,
    offsets,
    norm_gain,
    mamba_in,
    conv_taps,
    conv_bias,
    step_bias,
    decay_log,
    skip_weight,
    mamba_gain,
    mamba_out,
    query_weight,
    key_weight,
    value_weight,
    output_weight,
    second_gain,
    gate_weight,
    up_weight,
    down_weight,
    cotangent,
):
    me = lax.axis_index("tp")
    peers = lax.axis_size(plane)
    batches, width, model = tokens.shape
    rows = batches * width
    shard = mamba_in.shape[0]
    inner = mamba_gain.shape[0]
    heads = step_bias.shape[0]
    state = (mamba_in.shape[1] - 2 * inner - heads) // 2
    q_cols = query_weight.shape[1]
    kv_heads = key_weight.shape[1] // HD
    hidden_units = gate_weight.shape[1]
    inner_t, heads_t, q_t, ff_t = inner // TP, heads // TP, q_cols // TP, hidden_units // TP
    pad = 128

    def swap(values, k, axis="tp"):
        size = lax.axis_size(axis)
        return lax.ppermute(values, axis, [(i, i ^ k) for i in range(size)])

    def spread_first(values):
        half = values.shape[1] // 2
        return swap(values[:, :half], 3), swap(values[:, half:], 1)

    def spread_second(values, far, near):
        half = values.shape[1] // 2
        pair = swap(jnp.concatenate([values[:, :half], far], axis=0), 1)
        last = swap(jnp.concatenate([values[:, half:], near], axis=0), 3)
        return values, far, pair, near, last

    def spread(values):
        return spread_second(values, *spread_first(values))

    def reduce_send(halves):
        return swap(halves[1], 1), swap(halves[3], 3)

    def reduce_add(halves, got, got_right):
        return halves[0] + got.astype(f32), halves[2] + got_right.astype(f32)

    def reduce_first(*halves):
        return reduce_add(halves, *reduce_send(halves))

    def reduce_second(pair, last):
        half = pair.shape[0] // 2
        got = swap(pair[half:].astype(bf16), 3)
        got_right = swap(last[half:].astype(bf16), 1)
        return pair[:half], got, last[:half], got_right

    def reduce(*halves):
        return reduce_second(*reduce_first(*halves))

    def everywhere(values):
        return [values] + [swap(values, k) for k in range(1, TP)]

    def absolute(parts):
        stacked = jnp.stack(parts)
        return jnp.concatenate(
            [lax.dynamic_index_in_dim(stacked, me ^ t, 0) for t in range(TP)], axis=0
        )

    cube = len(plane) == 3

    def order(values):
        lead = values.shape[:-1]
        if cube:
            split = values.reshape(lead + (TP, 2, 2, 2, shard))
            split = jnp.moveaxis(split, (-2, -4, -3, -5), (-5, -4, -3, -2))
        else:
            split = jnp.swapaxes(values.reshape(lead + (TP, peers, shard)), -3, -2)
        return split.reshape(values.shape)

    def unorder(values):
        lead = values.shape[:-1]
        if cube:
            split = values.reshape(lead + (2, 2, 2, TP, shard))
            split = jnp.moveaxis(split, (-5, -4, -3, -2), (-2, -4, -3, -5))
        else:
            split = jnp.swapaxes(values.reshape(lead + (peers, TP, shard)), -3, -2)
        return split.reshape(values.shape)

    blocks = jnp.arange(peers * TP, dtype=jnp.int32)
    in_group = blocks ^ me
    in_plane = blocks ^ (lax.axis_index(plane) * TP + me)

    def cut(weight, start, size, t):
        return lax.dynamic_slice_in_dim(weight, start + t * size, size, axis=1)

    def kv(weight, t):
        return cut(weight, 0, HD, t * kv_heads // TP)

    def in_slice(t):
        return jnp.concatenate(
            [
                cut(mamba_in, 0, inner_t, t),
                cut(mamba_in, inner, inner_t, t),
                mamba_in[:, 2 * inner : 2 * inner + 2 * state],
                cut(mamba_in, 2 * inner + 2 * state, heads_t, t),
                norm_gain[:, None],
                second_gain[:, None],
                jnp.zeros((shard, pad - heads_t - 2), bf16),
                cut(query_weight, 0, q_t, t),
                kv(key_weight, t),
                kv(value_weight, t),
            ],
            axis=1,
        )

    def out_slice(t):
        return jnp.concatenate([cut(mamba_out.T, 0, inner_t, t), cut(output_weight.T, 0, q_t, t)], axis=1)

    def mlp_slice(t):
        return jnp.concatenate(
            [
                cut(gate_weight, 0, ff_t, t),
                cut(up_weight, 0, ff_t, t),
                cut(down_weight.T, 0, ff_t, t),
            ],
            axis=1,
        )

    def after(values, *earlier):
        return lax.optimization_barrier((values, earlier))[0]

    def slices(make):
        return [make(me ^ k) for k in range(TP)]

    def exchange(pieces):
        return [pieces[0]] + [swap(pieces[k], k) for k in range(1, TP)]

    def gather(parts):
        return lax.all_gather(absolute(parts).reshape(TP * shard, -1), plane, axis=0, tiled=True)

    def scatter(grads):
        return lax.psum_scatter(grads, plane, scatter_dimension=0, tiled=True)

    def pass_on(part):
        part = part.reshape(TP, shard, -1)
        return exchange([part[k] for k in range(TP)])

    conv_cols = inner_t + 2 * state
    at_q = inner_t + conv_cols + pad
    in_cols = at_q + q_t + 2 * HD

    def own(values, size):
        return lax.dynamic_slice_in_dim(values, me * size, size, axis=-1)

    taps_t = jnp.concatenate([own(conv_taps[:, :inner], inner_t), conv_taps[:, inner:]], axis=1)
    bias_t = jnp.concatenate([own(conv_bias[:inner], inner_t), conv_bias[inner:]])[None]
    steps_t = jnp.pad(
        jnp.stack([own(step_bias, heads_t), own(decay_log, heads_t)]), ((0, 0), (0, pad - heads_t))
    )
    skip_t = jnp.repeat(own(skip_weight, heads_t), inner_t // heads_t)[None]
    gain_t = own(mamba_gain, inner_t)[None]
    sizes = (inner_t, state, heads_t)

    in_parts = exchange(slices(in_slice))
    w_in = gather(in_parts)
    slots = jnp.stack([lengths[:, 0], offsets[:, 0]], axis=1)
    slots = jnp.concatenate([slots] + [swap(slots, k) for k in (3, 1, 2)], axis=0)
    turns = turn_table(slots[:, 1], width)
    source = order(tokens.reshape(rows, model))
    upstream = order(cotangent.reshape(rows, model))
    prepared = (slots, turns, taps_t, bias_t, steps_t, skip_t, gain_t, in_plane, in_group, upstream)
    source, prepared = lax.optimization_barrier((source, (prepared, in_parts[1:])))
    slots, turns, taps_t, bias_t, steps_t, skip_t, gain_t, in_plane, in_group, upstream = prepared[0]
    source_all = spread(source)
    out_parts = exchange(after(slices(out_slice), source_all))
    w_out = gather(out_parts)
    mlp_parts = exchange(after(slices(mlp_slice), out_parts[1:]))

    normed, projected, y, squares, mixed, gains = mixer_inner(
        slots, source_all, w_in, taps_t, bias_t, steps_t, skip_t, turns, *sizes
    )
    w_mlp = gather(after(mlp_parts, squares))
    squares = everywhere(squares)
    upstream_all = spread(after(upstream, squares))
    branches, root, *halves = mixer_outer(projected, y, mixed, gain_t, squares, w_out)
    hidden, second = row_call(hidden_kernel, slots, reduce(*halves), source, gains)

    second_all, down_grad, product, gate_grad, up_grad, *halves = feed_forward(
        slots, spread(second), upstream_all, w_mlp, ff_t
    )
    mlp_sums = weight_grads(
        in_group,
        1,
        [
            ([second_all], [gate_grad], 0, ff_t),
            ([second_all], [up_grad], 0, ff_t),
            ([down_grad], [product], 0, ff_t),
        ],
    )
    sums = reduce_second(*reduce_add(halves, *after(reduce_send(halves), mlp_sums)))
    mlp_sums = scatter(mlp_sums[0])
    d_hidden, branch_grad = row_call(
        back_hidden_kernel, slots, sums, hidden, upstream, gains
    )
    branch_all = spread(branch_grad)
    last_halves = back_out(product, w_mlp, 2)
    branch_grad = after(branch_all, last_halves)
    branch_all, d_branches, dots = back_outer(
        branch_grad, w_out, projected, y, gain_t, slots.shape[0]
    )
    last_halves = after(last_halves, branch_grad)
    last_pair = reduce_add(last_halves, *reduce_send(last_halves))
    out_sums = weight_grads(in_group, 1, [([branch_all], [branches], 0, inner_t + q_t)])
    dots = after(everywhere(dots), (out_sums, last_pair))
    out_sums = scatter(out_sums[0])
    mlp_grads = pass_on(after(mlp_sums, dots))
    proj_grad, conv_rows, inner_rows, step_rows = mixer_backward(
        slots, projected, taps_t, bias_t, steps_t, skip_t, turns, gain_t, y, d_branches, root,
        dots, *sizes,
    )

    normed, last_pair = after((normed, last_pair), mlp_grads)
    in_sums = weight_grads(
        in_plane if cube else in_group, 2 if cube else 1, [([normed], [proj_grad], 0, in_cols)]
    )
    kernel = conv_taps.shape[0]
    small = jnp.concatenate(
        [
            conv_rows[: kernel + 1].reshape(-1),
            inner_rows[0],
            step_rows[0, :heads_t],
            step_rows[1, :heads_t],
            inner_rows[1].reshape(heads_t, -1).sum(1),
        ]
    )
    small, proj_grad = after((small, proj_grad), in_sums)
    norm_halves = back_out(proj_grad, w_in, 0)
    if cube:
        block, half = TP * shard, TP * shard // 2
        counts = (block, block, block, half, half)
        keep, send = in_sums
        mine, along_y, along_x, across_x, across_y = by_columns(
            chip_kernel, counts, keep, after(swap(send, 1, "core"), (norm_halves, out_sums))
        )
        in_parts = swap(across_x, 1, "x"), swap(across_y, 1, "y")
        norm_halves, last_pair, small = after((norm_halves, last_pair, small), across_x)
    norm_pair = reduce_send(norm_halves)
    small = everywhere(small)
    if cube:
        to_y, to_x = by_columns(
            along_kernel, (block, block), along_y, along_x, *after(in_parts, small)
        )
        in_parts = swap(to_x, 1, "x"), swap(to_y, 1, "y")
        norm_pair, last_pair, out_sums = after((norm_pair, last_pair, out_sums), to_x)
    norm_parts = reduce_second(*reduce_add(norm_halves, *norm_pair))
    last_parts = reduce_second(*last_pair)
    out_grads = pass_on(out_sums)
    if cube:
        in_parts = after(in_parts, (norm_parts, last_parts, out_grads))
        in_sums = by_columns(plane_kernel, (shard,) * TP, mine, *in_parts)
        in_grads = exchange(in_sums)
    else:
        in_sums = scatter(in_sums[0])
        in_grads = pass_on(in_sums)
    last_parts, norm_parts, small, mlp_grads, out_grads = after(
        (last_parts, norm_parts, small, mlp_grads, out_grads), in_sums
    )
    small = absolute(small)
    if cube:
        for axis in plane:
            small = small + swap(small, 1, axis)
    else:
        small = lax.psum(small, plane)

    inside_own = jnp.concatenate(
        [inside_rows(slots[m, 0], slots[m, 1], width) for m in range(batches)], axis=0
    )

    def summed(parts):
        keep, got, keep_right, got_right = parts
        return jnp.concatenate([keep + got.astype(f32), keep_right + got_right.astype(f32)], axis=1)

    output = hidden + inside_own * summed(last_parts)
    output = unorder(output.astype(bf16)).reshape(tokens.shape)
    d_normed = summed(norm_parts) * gains[0:1]
    wide = source.astype(f32)
    token_grads = d_hidden + norm_back(wide, inverse_root(wide), d_normed)
    token_grads = unorder(token_grads).reshape(tokens.shape)

    at_group = me[None].astype(jnp.int32)
    grad_gate, grad_up, grad_down, grad_second_gain = unpack(
        functools.partial(unpack_mlp_kernel, ff_t),
        at_group,
        mlp_grads,
        (gate_weight, up_weight, second_gain[:, None]),
        (hidden_units, hidden_units, hidden_units, 1),
    )
    grad_mamba_out, grad_output = unpack(
        functools.partial(unpack_out_kernel, inner_t, q_t), at_group, out_grads, (), (inner, q_cols)
    )
    grad_mamba_in, grad_query, grad_key, grad_value, grad_norm_gain = unpack(
        functools.partial(unpack_in_kernel, *sizes, pad),
        at_group,
        in_grads,
        (mamba_in, query_weight, key_weight, value_weight, norm_gain[:, None]),
        (mamba_in.shape[1], q_cols, kv_heads * HD, kv_heads * HD, 1),
    )
    grad_mamba_out, grad_output, grad_down = grad_mamba_out.T, grad_output.T, grad_down.T
    grad_norm_gain, grad_second_gain = grad_norm_gain[:, 0], grad_second_gain[:, 0]

    conv = small[:, : (kernel + 1) * conv_cols].reshape(TP, kernel + 1, conv_cols)
    conv = jnp.concatenate(
        [conv[:, :, :inner_t].transpose(1, 0, 2).reshape(kernel + 1, inner), conv[:, :, inner_t:].sum(0)],
        axis=1,
    )
    at = (kernel + 1) * conv_cols
    return (
        output,
        token_grads,
        grad_norm_gain,
        grad_mamba_in,
        conv[:kernel],
        conv[kernel],
        small[:, at + inner_t : at + inner_t + heads_t].reshape(-1),
        small[:, at + inner_t + heads_t : at + inner_t + 2 * heads_t].reshape(-1),
        small[:, at + inner_t + 2 * heads_t :].reshape(-1),
        small[:, at : at + inner_t].reshape(-1),
        grad_mamba_out,
        grad_query,
        grad_key,
        grad_value,
        grad_output,
        grad_second_gain,
        grad_gate,
        grad_up,
        grad_down,
    )


def solution(mesh):
    count = mesh.devices.size
    if tuple(mesh.devices.shape) == (8, 4):
        grid = Mesh(mesh.devices.reshape(TP, 2, 2, 2), ("tp", "x", "y", "core"))
        plane = ("core", "x", "y")
    else:
        grid = Mesh(mesh.devices.reshape(TP, count // TP), ("tp", "fs"))
        plane = ("fs",)
    every = grid.axis_names
    down, across, slots = P(every, None), P(None, every), P(None, every, None)
    line, copied = P(every), P()
    return jax.shard_map(
        functools.partial(local, plane),
        mesh=grid,
        in_specs=(
            slots, across, across, line, down, copied, copied, copied, copied, copied, copied,
            across, down, down, down, across, line, down, down, across, slots,
        ),
        out_specs=(
            slots, slots, line, down, copied, copied, copied, copied, copied, copied,
            across, down, down, down, across, line, down, down, across,
        ),
        check_vma=False,
    )
```

```python
import functools
import math

import jax
import jax.numpy as jnp
from jax import lax
from jax.experimental import pallas as pl
from jax.experimental.pallas import tpu as pltpu
from jax.sharding import Mesh
from jax.sharding import PartitionSpec as P

HD = 128
TP = 4

epsilon = 1e-05
rope_base = 100000000000.0
highest = lax.Precision.HIGHEST
f32 = jnp.float32
bf16 = jnp.bfloat16


def inverse_root(values):
    return lax.rsqrt(jnp.mean(values * values, axis=-1, keepdims=True) + epsilon)


def norm_back(values, root, grad):
    return root * grad - values * root**3 * jnp.mean(values * grad, axis=-1, keepdims=True)


def dot_nn(left, right):
    return jnp.dot(left, right, preferred_element_type=f32)


def dot_nt(left, right):
    return lax.dot_general(left, right, (((1,), (1,)), ((), ())), preferred_element_type=f32)


def inside_rows(length, offset, width):
    rows = jnp.arange(width, dtype=jnp.int32)[:, None]
    return ((rows >= offset) & (rows < offset + length)).astype(f32)


def turn_table(offsets, width):
    half = HD // 2
    freqs = rope_base ** (-jnp.arange(half, dtype=f32) * 2.0 / HD)
    rows = jnp.arange(width, dtype=jnp.int32)
    positions = (rows[None, :] - offsets[:, None]).astype(f32)
    angles = positions.reshape(-1, 1) * freqs
    cosine, sine = jnp.cos(angles), jnp.sin(angles)
    return jnp.concatenate([cosine, cosine, -sine, sine], axis=1)


def mm(left, right, dims, precision=lax.Precision.HIGH):
    return lax.dot_general(left, right, (dims, ((), ())), precision=precision, preferred_element_type=f32)


NN = ((1,), (0,))
NT = ((1,), (1,))
TN = ((0,), (0,))


def iota(shape, axis):
    return lax.broadcasted_iota(jnp.int32, shape, axis)


def down_rows(values, count):
    if count == 0:
        return values
    return jnp.where(iota(values.shape, 0) >= count, pltpu.roll(values, count, axis=0), 0.0)


def up_rows(values, count):
    if count == 0:
        return values
    length = values.shape[0]
    return jnp.where(
        iota(values.shape, 0) < length - count, pltpu.roll(values, length - count, axis=0), 0.0
    )


def head_sums(values, spread):
    return mm(values, spread, NT)


def mamba_shared(proj, start, count, taps_ref, bias_ref, steps_ref, inner, state, heads):
    length = proj.shape[0]
    conv_cols = inner + 2 * state
    row = iota((length, 1), 0)
    inside = ((row >= start) & (row < start + count)).astype(f32)
    conv_in = proj[:, inner : inner + conv_cols] * inside
    kernel = taps_ref.shape[0]
    conv = bias_ref[...] + jnp.zeros_like(conv_in)
    for tap in range(kernel):
        conv = conv + taps_ref[tap : tap + 1, :] * down_rows(conv_in, kernel - 1 - tap)
    sig = jax.nn.sigmoid(conv)
    active = conv * sig
    pad = steps_ref.shape[1]
    lane = iota((length, pad), 1)
    raw = jnp.where(lane < heads, proj[:, inner + conv_cols : inner + conv_cols + pad] + steps_ref[0:1, :], 0.0)
    step = jnp.where(lane < heads, jnp.maximum(raw, 0.0) + jnp.log1p(jnp.exp(-jnp.abs(raw))), 0.0)
    rate = -jnp.exp(steps_ref[1:2, :])
    lower = (iota((length, length), 0) >= iota((length, length), 1)).astype(f32)
    cum = mm(lower, step * rate, NN, highest)
    size = inner // heads
    spread = (iota((pad, inner), 0) == iota((pad, inner), 1) // size).astype(f32)
    step_x = mm(step, spread, NN)
    cum_x = mm(cum, spread, NN, highest)
    at = iota((length, inner), 1) % length
    diagonal = iota((length, inner), 0) == at
    cum_row = jnp.sum(jnp.where(diagonal, cum_x, 0.0), axis=0, keepdims=True)
    allowed = (
        (at <= iota((length, inner), 0)) & (inside > 0.0) & (at >= start) & (at < start + count)
    )
    decay = jnp.where(allowed, jnp.exp(jnp.where(allowed, cum_x - cum_row, 0.0)), 0.0)
    xs = active[:, :inner]
    b_state = active[:, inner : inner + state]
    c_state = active[:, inner + state :]
    inter = mm(c_state, b_state, NT)
    pair = jnp.concatenate([inter, inter], axis=1)
    mixing = decay * jnp.concatenate([pair] * (inner // pair.shape[1]), axis=1)
    return dict(
        inside=inside, conv_in=conv_in, conv=conv, sig=sig, raw=raw, step=step, rate=rate,
        spread=spread, step_x=step_x, diagonal=diagonal, decay=decay, mixing=mixing, xs=xs,
        b_state=b_state, c_state=c_state, lower=lower, lane=lane,
    )


def two_blocks(values):
    left = iota(values.shape, 1) < values.shape[1] // 2
    return jnp.concatenate([jnp.where(left, values, 0.0), jnp.where(left, 0.0, values)], axis=0)


def turn(values, cosine, sine):
    return values * cosine + pltpu.roll(values, HD // 2, axis=1) * sine


def attention_shared(proj, at, start, count, cosine, sine):
    length = proj.shape[0]
    kv = proj.shape[1] - 2 * HD
    queries = jnp.concatenate(
        [turn(proj[:, c : c + HD], cosine, sine) for c in range(at, kv, HD)], axis=0
    )
    keys = turn(proj[:, kv : kv + HD], cosine, sine)
    values = proj[:, kv + HD :]
    scores = mm(queries, keys, NT) * (1.0 / math.sqrt(HD))
    row = iota(scores.shape, 0) % length
    col = iota(scores.shape, 1)
    end = start + count
    allowed = ((row >= start) & (row < end) & (col >= start) & (col <= row)) | (row == col)
    scores = jnp.where(allowed, scores, -1e30)
    probs = jnp.exp(scores - jnp.max(scores, axis=1, keepdims=True))
    probs = probs / jnp.sum(probs, axis=1, keepdims=True)
    return queries, keys, values, probs


def specs(*shapes):
    return [pl.BlockSpec(s, lambda i: (0, 0)) for s in shapes]


def rows_spec(length, cols):
    return pl.BlockSpec((length, cols), lambda i: (i, 0))


def their_spec(length, each, k):
    return pl.BlockSpec((1, 1, length), lambda i: (i ^ (THEIRS[k][0] * each), 0, 0))


big = pltpu.CompilerParams(vmem_limit_bytes=50 * 1024 * 1024)


def costs(microseconds):
    return pl.CostEstimate(
        flops=microseconds * 10**9, bytes_accessed=microseconds * 10**5, transcendentals=0
    )


def inside_of(slots_ref, seq, length):
    row = iota((length, 1), 0)
    start = slots_ref[seq, 1]
    return ((row >= start) & (row < start + slots_ref[seq, 0])).astype(f32)


def as_row(column):
    length = column.shape[0]
    same = iota((length, length), 0) == iota((length, length), 1)
    return jnp.sum(jnp.where(same, column, 0.0), axis=0, keepdims=True)


def as_column(row):
    length = row.shape[1]
    same = iota((length, length), 0) == iota((length, length), 1)
    return jnp.sum(jnp.where(same, row, 0.0), axis=1, keepdims=True)


THEIRS = ((0, 1, 2, 3), (2, 3, 0, 1), (3, 2, 1, 0), (1, 0, 3, 2))


def group_total(refs, seq):
    each = refs[0].shape[0] // TP
    return sum(ref[THEIRS[k][seq // each] * each + seq % each] for k, ref in enumerate(refs))


def joined_rows(refs):
    own, far, pair, near, last = refs
    half = far.shape[1]
    count = own.shape[0]
    left = jnp.concatenate([own[:, :half], far[...], pair[...]], axis=0)
    right = jnp.concatenate([own[:, half:], last[:count, :], near[...], last[count:, :]], axis=0)
    return jnp.concatenate([left, right], axis=1)


def put_left(values, refs):
    half = values.shape[0] // 2
    refs[0][...] = values[:half]
    refs[1][...] = values[half:].astype(bf16)


def put_right(values, refs):
    one = values.shape[0] // TP
    refs[2][:one, :] = values[:one]
    refs[2][one:, :] = values[2 * one : 3 * one]
    refs[3][:one, :] = values[one : 2 * one].astype(bf16)
    refs[3][one:, :] = values[3 * one :].astype(bf16)


def put_tiles(values, refs):
    step = pl.program_id(0)
    middle = pl.num_programs(0) // 2

    @pl.when(step < middle)
    def _():
        put_left(values, refs)

    @pl.when(step >= middle)
    def _():
        put_right(values, refs)


def halves_out(rows, model, tile):
    middle = model // tile // 2
    left = pl.BlockSpec((rows // 2, tile), lambda j: (0, jnp.minimum(j, middle - 1)))
    right = pl.BlockSpec((rows // 2, tile), lambda j: (0, jnp.maximum(j - middle, 0)))
    shapes = [jax.ShapeDtypeStruct((rows // 2, model // 2), t) for t in (f32, bf16, f32, bf16)]
    return [left, left, right, right], shapes


def both_halves(refs):
    kept, got, kept_right, got_right = refs
    return jnp.concatenate(
        [kept[...] + got[...].astype(f32), kept_right[...] + got_right[...].astype(f32)], axis=1
    )


def inner_kernel(
    inner, state, heads, tiles, slots_ref, p0, p1, p2, p3, p4, weight_ref, gains_in_ref, taps_ref, bias_ref,
    steps_ref, skip_ref, turn_ref, normed_ref, proj_ref, y_ref, square_ref, mixed_ref, gains_ref,
):
    step = pl.program_id(0)
    tile = weight_ref.shape[1]

    @pl.when(step == 0)
    def _():
        rows = joined_rows((p0, p1, p2, p3, p4)).astype(f32)
        turned = jnp.transpose(gains_in_ref[...].astype(f32))
        gains_ref[0:1, :] = turned[heads : heads + 1]
        gains_ref[1:2, :] = turned[heads + 1 : heads + 2]
        normed_ref[...] = (rows * inverse_root(rows) * turned[heads : heads + 1]).astype(bf16)

    @pl.when(step < tiles)
    def _():
        at = pl.multiple_of(step * tile, tile)
        proj_ref[:, pl.ds(at, tile)] = jnp.dot(
            normed_ref[...], weight_ref[...], preferred_element_type=f32
        )

    @pl.when(step >= tiles)
    def _():
        seq = step - tiles
        length = y_ref.shape[0]
        proj = proj_ref[pl.ds(pl.multiple_of(seq * length, length), length), :]
        start = slots_ref[seq, 1]
        count = slots_ref[seq, 0]
        m = mamba_shared(proj, start, count, taps_ref, bias_ref, steps_ref, inner, state, heads)
        scaled = m["xs"] * m["step_x"]
        wide = 2 * length
        parts = [
            mm(m["mixing"][:, c : c + wide], two_blocks(scaled[:, c : c + wide]), NN)
            for c in range(0, inner, wide)
        ]
        y = jnp.concatenate(parts, axis=1) + skip_ref[...] * m["xs"]
        y_ref[...] = y
        gate = proj[:, :inner]
        gated = y * gate * jax.nn.sigmoid(gate)
        square_ref[0] = as_row(jnp.sum(gated * gated, axis=1, keepdims=True))
        at = 2 * inner + 2 * state + steps_ref.shape[1]
        _, _, values, probs = attention_shared(
            proj, at, start, count, turn_ref[:, :HD], turn_ref[:, HD:]
        )
        mixed = mm(probs, values, NN)
        mixed_ref[...] = jnp.concatenate(
            [mixed[r : r + length] for r in range(0, mixed.shape[0], length)], axis=1
        ).astype(mixed_ref.dtype)


def mixer_inner(slots, rows, weight, taps, bias, steps, skip, turns, inner, state, heads, tile=384):
    model, cols = weight.shape
    seqs = slots.shape[0]
    pieces = rows
    rows = TP * pieces[0].shape[0]
    length = rows // seqs
    tiles = cols // tile
    pad = steps.shape[1]
    at_steps = (2 * inner + 2 * state) // pad
    q_cols = cols - 2 * inner - 2 * state - pad - 2 * HD

    def seq_spec(*shape):
        zeros = (0,) * (len(shape) - 1)
        return pl.BlockSpec(shape, lambda j: (jnp.maximum(j - tiles, 0),) + zeros)

    return pl.pallas_call(
        functools.partial(inner_kernel, inner, state, heads, tiles),
        grid=(tiles + seqs,),
        in_specs=[pl.BlockSpec(memory_space=pltpu.SMEM)]
        + specs(*[p.shape for p in pieces])
        + [
            pl.BlockSpec((model, tile), lambda j: (0, jnp.minimum(j, tiles - 1))),
            pl.BlockSpec((model, pad), lambda j: (0, at_steps)),
        ]
        + specs(taps.shape, bias.shape, steps.shape, skip.shape)
        + [seq_spec(length, turns.shape[1])],
        out_specs=specs((rows, model), (rows, cols))
        + [seq_spec(length, inner), seq_spec(1, 1, length), seq_spec(length, q_cols)]
        + specs((8, model)),
        out_shape=[
            jax.ShapeDtypeStruct((rows, model), bf16),
            jax.ShapeDtypeStruct((rows, cols), f32),
            jax.ShapeDtypeStruct((rows, inner), f32),
            jax.ShapeDtypeStruct((seqs, 1, length), f32),
            jax.ShapeDtypeStruct((rows, q_cols), bf16),
            jax.ShapeDtypeStruct((8, model), f32),
        ],
        compiler_params=big,
        cost_estimate=costs(18),
    )(slots, *pieces, weight, weight, taps, bias, steps, skip, turns)


def outer_kernel(inner, gate_ref, y_ref, mixed_ref, gain_ref, s0, s1, s2, s3, weight_ref, branches_ref, root_ref, *halves):
    @pl.when(pl.program_id(0) == 0)
    def _():
        length = root_ref.shape[2]
        for seq in range(root_ref.shape[0]):
            rows = slice(seq * length, (seq + 1) * length)
            root = lax.rsqrt(group_total((s0, s1, s2, s3), seq) / (TP * inner) + epsilon)
            root_ref[seq] = root
            gate = gate_ref[rows, :]
            gated = y_ref[rows, :] * gate * jax.nn.sigmoid(gate)
            branches_ref[rows, :inner] = (gated * as_column(root) * gain_ref[...]).astype(bf16)
        branches_ref[:, inner:] = mixed_ref[...]

    put_tiles(dot_nt(branches_ref[...], weight_ref[...]), halves)


def mixer_outer(proj, y, mixed, gain, squares, weight, tile=512):
    rows, inner = y.shape
    model, cols = weight.shape
    half_specs, half_shapes = halves_out(rows, model, tile)
    return pl.pallas_call(
        functools.partial(outer_kernel, inner),
        grid=(model // tile,),
        in_specs=specs((rows, inner), y.shape, mixed.shape, gain.shape)
        + [pl.BlockSpec(squares[0].shape, lambda j: (0, 0, 0))] * TP
        + [pl.BlockSpec((tile, cols), lambda j: (j, 0))],
        out_specs=specs((rows, cols))
        + [pl.BlockSpec(squares[0].shape, lambda j: (0, 0, 0))]
        + half_specs,
        out_shape=[
            jax.ShapeDtypeStruct((rows, cols), bf16),
            jax.ShapeDtypeStruct(squares[0].shape, f32),
        ]
        + half_shapes,
        compiler_params=big,
        cost_estimate=costs(4),
    )(proj, y, mixed, gain, *squares, weight)


def back_out_kernel(left_ref, weight_ref, *halves):
    put_tiles(dot_nt(left_ref[...], weight_ref[...]), halves)


def back_out(left, weight, column, tile=512):
    rows, cols = left.shape
    model = weight.shape[0]
    half_specs, half_shapes = halves_out(rows, model, tile)
    return pl.pallas_call(
        back_out_kernel,
        grid=(model // tile,),
        in_specs=specs(left.shape) + [pl.BlockSpec((tile, cols), lambda j: (j, column))],
        out_specs=half_specs,
        out_shape=half_shapes,
        compiler_params=big,
        cost_estimate=costs(4),
    )(left, weight)


def inside_all(slots_ref, seqs, length):
    return jnp.concatenate([inside_of(slots_ref, seq, length) for seq in range(seqs)], axis=0)


def hidden_kernel(slots_ref, k0, k1, k2, k3, source_ref, gains_ref, hidden_ref, second_ref):
    length = source_ref.shape[0] * TP // slots_ref.shape[0]
    inside = inside_all(slots_ref, slots_ref.shape[0] // TP, length)
    hidden = source_ref[...].astype(f32) + inside * both_halves((k0, k1, k2, k3))
    hidden_ref[...] = hidden
    second_ref[...] = (hidden * inverse_root(hidden) * gains_ref[1:2, :]).astype(bf16)


def row_call(kernel, slots, halves, *others):
    shape = others[0].shape
    return pl.pallas_call(
        kernel,
        grid=(1,),
        in_specs=[pl.BlockSpec(memory_space=pltpu.SMEM)]
        + specs(*[h.shape for h in halves], *[o.shape for o in others]),
        out_specs=specs(shape, shape),
        out_shape=[jax.ShapeDtypeStruct(shape, f32), jax.ShapeDtypeStruct(shape, bf16)],
        compiler_params=big,
        cost_estimate=costs(2),
    )(slots, *halves, *others)


def feed_kernel(
    steps, blocks, slots_ref, table_ref, s0, s1, s2, s3, s4, c0, c1, c2, c3, c4, gate_ref, up_ref, down_ref,
    product_ref, h0, h1, h2, h3, grads_ref,
    second_ref, down_grad_ref, gate_grad_ref, up_grad_ref, total, second_turned, down_turned,
):
    step = pl.program_id(0)
    tile = gate_ref.shape[1]

    @pl.when(step == 0)
    def _():
        second_ref[...] = joined_rows((s0, s1, s2, s3, s4))
        seqs = slots_ref.shape[0]
        inside = inside_all(slots_ref, seqs, TP * s0.shape[0] // seqs)
        down_grad_ref[...] = (inside * joined_rows((c0, c1, c2, c3, c4)).astype(f32)).astype(bf16)
        total[...] = jnp.zeros_like(total)

    @pl.when(step < steps)
    def _():
        second = second_ref[...]
        gate = jnp.dot(second, gate_ref[...], preferred_element_type=f32)
        up = jnp.dot(second, up_ref[...], preferred_element_type=f32)
        d_product = jnp.dot(down_grad_ref[...], down_ref[...], preferred_element_type=f32)
        sig = jax.nn.sigmoid(gate)
        swish = gate * sig
        gate_grad = (d_product * up * sig * (1.0 + gate * (1.0 - sig))).astype(bf16)
        up_grad = (d_product * swish).astype(bf16)
        at = pl.ds(pl.multiple_of(step * tile, tile), tile)
        product_ref[:, at] = (swish * up).astype(bf16)
        gate_grad_ref[:, at] = gate_grad
        up_grad_ref[:, at] = up_grad
        total[...] += dot_nt(gate_grad, gate_ref[...]) + dot_nt(up_grad, up_ref[...])

    @pl.when(step == steps - 1)
    def _():
        middle = total.shape[1] // 2
        put_left(total[:, :middle], (h0, h1))
        put_right(total[:, middle:], (h0, h1, h2, h3))
        size = second_ref.shape[1] // blocks
        for source, turned in ((second_ref, second_turned), (down_grad_ref, down_turned)):
            plain = jnp.transpose(source[...])
            total_rows = plain.shape[0]
            grads_ref[:total_rows, : plain.shape[1]] = plain
            for block in range(blocks):
                start = pl.multiple_of(table_ref[block] * size, size)
                turned[block * size : (block + 1) * size, :] = grads_ref[pl.ds(start, size), : plain.shape[1]]

    for part, (turned, right) in enumerate(
        ((second_turned, gate_grad_ref), (second_turned, up_grad_ref), (down_turned, product_ref))
    ):

        @pl.when((step >= (part + 1) * steps) & (step < (part + 2) * steps))
        def _(part=part, turned=turned, right=right):
            at = pl.multiple_of((step - (part + 1) * steps) * tile, tile)
            grads_ref[...] = jnp.dot(
                turned[...], right[:, pl.ds(at, tile)], preferred_element_type=f32
            ).astype(bf16)


def feed_forward(slots, table, second, cotangent, weight, units, tile=512):
    count, model = second[0].shape
    rows = TP * count
    steps = units // tile
    half_shapes = halves_out(rows, model, tile)[1]
    shapes = [p.shape for p in second]
    return pl.pallas_call(
        functools.partial(feed_kernel, steps, table.shape[0]),
        grid=(4 * steps,),
        in_specs=[pl.BlockSpec(memory_space=pltpu.SMEM)] * 2
        + specs(*shapes, *shapes)
        + [
            pl.BlockSpec((model, tile), lambda j, at=at: (0, at * steps + jnp.minimum(j, steps - 1)))
            for at in range(3)
        ],
        out_specs=specs((rows, units), *[h.shape for h in half_shapes])
        + [pl.BlockSpec((model, tile), lambda j: (0, jnp.maximum(j - steps, 0)))],
        out_shape=[jax.ShapeDtypeStruct((rows, units), bf16)]
        + half_shapes
        + [jax.ShapeDtypeStruct((model, 3 * units), bf16)],
        scratch_shapes=[pltpu.VMEM((rows, model), bf16)] * 2
        + [pltpu.VMEM((rows, units), bf16)] * 2
        + [pltpu.VMEM((rows, model), f32)]
        + [pltpu.VMEM((model, rows), bf16)] * 2,
        compiler_params=big,
        cost_estimate=costs(30),
    )(slots, table, *second, *cotangent, weight, weight, weight)


def in_places(values, places):
    size = values.shape[1] // len(places)
    return jnp.concatenate([values[:, p * size : (p + 1) * size] for p in places], axis=1)


def output_kernel(places, slots_ref, k0, k1, k2, k3, hidden_ref, output_ref):
    seqs = slots_ref.shape[0]
    inside = inside_all(slots_ref, seqs // TP, hidden_ref.shape[0] * TP // seqs)
    output = (hidden_ref[...] + inside * both_halves((k0, k1, k2, k3))).astype(bf16)
    output_ref[...] = in_places(output, places)


def token_grad_kernel(places, k0, k1, k2, k3, hidden_ref, source_ref, gains_ref, grad_ref):
    grad = both_halves((k0, k1, k2, k3)) * gains_ref[0:1, :]
    source = source_ref[...].astype(f32)
    total = hidden_ref[...] + norm_back(source, inverse_root(source), grad)
    grad_ref[...] = in_places(total, places)


def whole_call(kernel, dtype, scalars, *arrays):
    shape = arrays[4].shape
    return pl.pallas_call(
        kernel,
        grid=(1,),
        in_specs=[pl.BlockSpec(memory_space=pltpu.SMEM)] * len(scalars) + specs(*[a.shape for a in arrays]),
        out_specs=pl.BlockSpec(shape, lambda i: (0, 0)),
        out_shape=jax.ShapeDtypeStruct(shape, dtype),
        compiler_params=big,
        cost_estimate=costs(3),
    )(*scalars, *arrays)


def back_hidden_kernel(slots_ref, k0, k1, k2, k3, hidden_ref, cotangent_ref, gains_ref, d_hidden_ref, branch_ref):
    grad = both_halves((k0, k1, k2, k3)) * gains_ref[1:2, :]
    hidden = hidden_ref[...]
    d_hidden = cotangent_ref[...].astype(f32) + norm_back(hidden, inverse_root(hidden), grad)
    d_hidden_ref[...] = d_hidden
    seqs = slots_ref.shape[0]
    inside = inside_all(slots_ref, seqs // TP, hidden.shape[0] * TP // seqs)
    branch_ref[...] = (inside * d_hidden).astype(bf16)


def back_outer_kernel(tiles, b0, b1, b2, b3, b4, weight_ref, gate_ref, y_ref, gain_ref, branch_ref, grad_ref, dots_ref, total):
    step = pl.program_id(0)

    @pl.when(step == 0)
    def _():
        branch_ref[...] = joined_rows((b0, b1, b2, b3, b4))
        total[...] = jnp.zeros_like(total)

    grad = jnp.dot(branch_ref[...], weight_ref[...], preferred_element_type=f32)
    grad_ref[...] = grad

    @pl.when(step < tiles)
    def _():
        gate = gate_ref[...]
        gated = y_ref[...] * gate * jax.nn.sigmoid(gate)
        total[...] += jnp.sum(gated * gain_ref[...] * grad, axis=1, keepdims=True)

    @pl.when(step == pl.num_programs(0) - 1)
    def _():
        length = dots_ref.shape[2]
        for seq in range(dots_ref.shape[0]):
            dots_ref[seq] = as_row(total[seq * length : (seq + 1) * length, :])


def back_outer(branch, weight, proj, y, gain, seqs, tile=256):
    model = weight.shape[0]
    rows, inner = y.shape
    cols = weight.shape[1]
    tiles = inner // tile
    length = rows // seqs
    inner_spec = pl.BlockSpec((rows, tile), lambda j: (0, jnp.minimum(j, tiles - 1)))
    return pl.pallas_call(
        functools.partial(back_outer_kernel, tiles),
        grid=(cols // tile,),
        in_specs=specs(*[p.shape for p in branch])
        + [
            pl.BlockSpec((model, tile), lambda j: (0, j)),
            inner_spec,
            inner_spec,
            pl.BlockSpec((1, tile), lambda j: (0, jnp.minimum(j, tiles - 1))),
        ],
        out_specs=specs((rows, model))
        + [
            pl.BlockSpec((rows, tile), lambda j: (0, j)),
            pl.BlockSpec((seqs, 1, length), lambda j: (0, 0, 0)),
        ],
        out_shape=[
            jax.ShapeDtypeStruct((rows, model), bf16),
            jax.ShapeDtypeStruct((rows, cols), f32),
            jax.ShapeDtypeStruct((seqs, 1, length), f32),
        ],
        scratch_shapes=[pltpu.VMEM((rows, 1), f32)],
        compiler_params=big,
        cost_estimate=costs(5),
    )(*branch, weight, proj, y, gain)


def backward_kernel(
    inner, state, heads, slots_ref, proj_ref, taps_ref, bias_ref, steps_ref, skip_ref, turn_ref,
    gain_ref, y_ref, grad_ref, root_ref, d0, d1, d2, d3, proj_grad_ref, small_ref,
):
    step_id = pl.program_id(0)
    start = slots_ref[step_id, 1]
    count = slots_ref[step_id, 0]
    proj = proj_ref[...]
    length = proj.shape[0]
    conv_cols = inner + 2 * state
    pad = steps_ref.shape[1]
    m = mamba_shared(proj, start, count, taps_ref, bias_ref, steps_ref, inner, state, heads)
    xs, decay, mixing = m["xs"], m["decay"], m["mixing"]
    scaled = xs * m["step_x"]
    gate = proj[:, :inner]
    gate_sig = jax.nn.sigmoid(gate)
    y = y_ref[...]
    root = as_column(root_ref[0])
    mean = as_column(sum(ref[0] for ref in (d0, d1, d2, d3))) / (TP * inner)
    gated = y * gate * gate_sig
    d_norm = grad_ref[:, :inner]
    d_gated = root * (d_norm * gain_ref[...]) - gated * (root * root * root * mean)
    dy = d_gated * gate * gate_sig
    d_gate = d_gated * y * gate_sig * (1.0 + gate * (1.0 - gate_sig))
    wide = 2 * length
    back, d_mix = [], []
    for c in range(0, inner, wide):
        dy_pair = dy[:, c : c + wide]
        full = mm(mixing[:, c : c + wide], dy_pair, TN)
        left = iota((length, wide), 1) < length
        back.append(jnp.where(left, full[:length], full[length:]))
        d_mix.append(mm(dy_pair, two_blocks(scaled[:, c : c + wide]), NT))
    back = jnp.concatenate(back, axis=1)
    d_mix = jnp.concatenate(d_mix, axis=1)
    d_xs = skip_ref[...] * dy + m["step_x"] * back
    flow = d_mix * mixing
    flow = flow - jnp.where(m["diagonal"], jnp.sum(flow, axis=0, keepdims=True), 0.0)
    d_cum = head_sums(flow, m["spread"])
    d_rate = mm(m["lower"], d_cum, TN, highest)
    d_step = head_sums(xs * back, m["spread"]) + d_rate * m["rate"]
    d_raw = jnp.where(m["lane"] < heads, d_step * jax.nn.sigmoid(m["raw"]), 0.0)
    d_inter = d_mix * decay
    pair = d_inter[:, :wide]
    for c in range(wide, inner, wide):
        pair = pair + d_inter[:, c : c + wide]
    d_inter = pair[:, :length] + pair[:, length:]
    d_b = mm(d_inter, m["c_state"], TN)
    d_c = mm(d_inter, m["b_state"], NN)
    d_active = jnp.concatenate([d_xs, d_b, d_c], axis=1)
    sig, conv = m["sig"], m["conv"]
    d_conv = d_active * sig * (1.0 + conv * (1.0 - sig))
    kernel = taps_ref.shape[0]
    d_in = jnp.zeros_like(d_conv)
    conv_rows = []
    for tap in range(kernel):
        back_by = kernel - 1 - tap
        d_in = d_in + taps_ref[tap : tap + 1, :] * up_rows(d_conv, back_by)
        conv_rows.append(jnp.sum(d_conv * down_rows(m["conv_in"], back_by), axis=0, keepdims=True))
    conv_rows.append(jnp.sum(d_conv, axis=0, keepdims=True))
    conv_rows.append(jnp.zeros((8 - kernel - 1, conv_cols), f32))
    conv_rows = jnp.concatenate(conv_rows, axis=0)
    inner_rows = jnp.concatenate(
        [
            jnp.sum(gated * root * d_norm, axis=0, keepdims=True),
            jnp.sum(dy * xs, axis=0, keepdims=True),
            jnp.zeros((6, inner), f32),
        ],
        axis=0,
    )
    step_rows = jnp.concatenate(
        [
            jnp.sum(d_raw, axis=0, keepdims=True),
            jnp.sum(d_rate * m["step"] * m["rate"], axis=0, keepdims=True),
            jnp.zeros((6, pad), f32),
        ],
        axis=0,
    )

    rows = jnp.concatenate([conv_rows, inner_rows, step_rows], axis=1)

    @pl.when(step_id == 0)
    def _():
        small_ref[...] = jnp.zeros_like(small_ref)

    small_ref[...] += rows

    at = inner + conv_cols + pad
    cosine, sine = turn_ref[:, :HD], turn_ref[:, HD:]
    queries, keys, values, probs = attention_shared(proj, at, start, count, cosine, sine)
    d_out = jnp.concatenate(
        [grad_ref[:, c : c + HD] for c in range(inner, grad_ref.shape[1], HD)], axis=0
    )
    d_values = mm(probs, d_out, TN)
    d_probs = mm(d_out, values, NT)
    d_scores = probs * (d_probs - jnp.sum(probs * d_probs, axis=1, keepdims=True)) * (1.0 / math.sqrt(HD))
    d_queries = mm(d_scores, keys, NN)
    d_keys = mm(d_scores, queries, TN)
    outs = [d_gate, d_in * m["inside"], d_raw]
    outs += [turn(d_queries[r : r + length], cosine, -sine) for r in range(0, d_queries.shape[0], length)]
    outs += [turn(d_keys, cosine, -sine), d_values]
    proj_grad_ref[...] = jnp.concatenate(outs, axis=1).astype(proj_grad_ref.dtype)


def mixer_backward(
    slots, proj, taps, bias, steps, skip, turns, gain, y, grads, root, dots, inner, state, heads
):
    seqs = slots.shape[0]
    rows, cols = proj.shape
    length = rows // seqs
    conv_cols = inner + 2 * state
    pad = steps.shape[1]
    return pl.pallas_call(
        functools.partial(backward_kernel, inner, state, heads),
        grid=(seqs,),
        in_specs=[pl.BlockSpec(memory_space=pltpu.SMEM), rows_spec(length, cols)]
        + specs(taps.shape, bias.shape, steps.shape, skip.shape)
        + [rows_spec(length, turns.shape[1])]
        + specs(gain.shape)
        + [rows_spec(length, inner), rows_spec(length, grads.shape[1])]
        + [pl.BlockSpec((1, 1, length), lambda i: (i, 0, 0))]
        + [their_spec(length, seqs // TP, k) for k in range(TP)],
        out_specs=[rows_spec(length, cols)] + specs((8, conv_cols + inner + pad)),
        out_shape=[
            jax.ShapeDtypeStruct((rows, cols), bf16),
            jax.ShapeDtypeStruct((8, conv_cols + inner + pad), f32),
        ],
        compiler_params=big,
        cost_estimate=costs(17),
    )(slots, proj, taps, bias, steps, skip, turns, gain, y, grads, root, *dots)


def chip_kernel(keep_ref, got_ref, mine_ref, along_y_ref, along_x_ref, across_x_ref, across_y_ref):
    total = (keep_ref[...].astype(f32) + got_ref[...].astype(f32)).astype(bf16)
    block = mine_ref.shape[0]
    half = across_x_ref.shape[0]
    mine_ref[...] = total[:block]
    along_y_ref[...] = total[block : 2 * block]
    along_x_ref[...] = total[2 * block : 3 * block]
    across_x_ref[...] = total[3 * block : 3 * block + half]
    across_y_ref[...] = total[3 * block + half :]


def along_kernel(along_y_ref, along_x_ref, by_x_ref, by_y_ref, to_y_ref, to_x_ref):
    half = by_x_ref.shape[0]
    to_y_ref[...] = along_y_ref[...]
    to_y_ref[:half, :] = (along_y_ref[:half, :].astype(f32) + by_x_ref[...].astype(f32)).astype(bf16)
    to_x_ref[...] = along_x_ref[...]
    to_x_ref[half:, :] = (along_x_ref[half:, :].astype(f32) + by_y_ref[...].astype(f32)).astype(bf16)


def plane_kernel(mine_ref, by_x_ref, by_y_ref, *outs):
    total = mine_ref[...].astype(f32) + by_x_ref[...].astype(f32) + by_y_ref[...].astype(f32)
    size = outs[0].shape[0]
    for k, out in enumerate(outs):
        out[...] = total[k * size : (k + 1) * size].astype(bf16)


def by_columns(kernel, row_counts, *arrays, tile=896):
    cols = arrays[0].shape[1]

    def of(rows):
        return pl.BlockSpec((rows, tile), lambda j: (0, j))

    return pl.pallas_call(
        kernel,
        grid=(cols // tile,),
        in_specs=[of(a.shape[0]) for a in arrays],
        out_specs=[of(r) for r in row_counts],
        out_shape=[jax.ShapeDtypeStruct((r, cols), bf16) for r in row_counts],
        compiler_params=big,
        cost_estimate=costs(3),
    )(*arrays)


def own_columns(me, refs, start, size, out_ref, at=0):
    for k, ref in enumerate(refs):
        place = pl.multiple_of((me ^ k) * size, 128)
        out_ref[:, pl.ds(at + place, size)] = ref[:, start : start + size].astype(f32)


def gain_sum(pairs, gain_ref):
    total = sum(
        jnp.sum(weight[...].astype(f32) * grad[...], axis=1, keepdims=True) for weight, grad in pairs
    )
    return total / gain_ref[...].astype(f32)


def unpack_mlp_kernel(units, me_ref, g0, g1, g2, g3, gate_ref, up_ref, gain_ref, grad_gate, grad_up, grad_down, grad_gain):
    for i, out in enumerate((grad_gate, grad_up, grad_down)):
        own_columns(me_ref[0], (g0, g1, g2, g3), i * units, units, out)
    grad_gain[...] = gain_sum(((gate_ref, grad_gate), (up_ref, grad_up)), gain_ref)


def unpack_out_kernel(inner, q_cols, me_ref, g0, g1, g2, g3, grad_mamba, grad_output):
    own_columns(me_ref[0], (g0, g1, g2, g3), 0, inner, grad_mamba)
    own_columns(me_ref[0], (g0, g1, g2, g3), inner, q_cols, grad_output)


def unpack_in_kernel(
    inner, state, heads, pad, me_ref, g0, g1, g2, g3, mamba_ref, query_ref, key_ref, value_ref, gain_ref,
    grad_mamba, grad_query, grad_key, grad_value, grad_gain,
):
    me = me_ref[0]
    refs = (g0, g1, g2, g3)
    own_columns(me, refs, 0, inner, grad_mamba)
    own_columns(me, refs, inner, inner, grad_mamba, TP * inner)
    at, out_at = 2 * inner, 2 * TP * inner
    shared = sum(ref[:, at : at + 2 * state].astype(f32) for ref in refs)
    grad_mamba[:, out_at : out_at + 2 * state] = shared
    at, out_at = at + 2 * state, out_at + 2 * state
    lane = iota((grad_mamba.shape[0], pad), 1)
    steps = jnp.zeros((grad_mamba.shape[0], pad), f32)
    for k, ref in enumerate(refs):
        piece = jnp.where(lane < heads, ref[:, at : at + pad].astype(f32), 0.0)
        steps = steps + pltpu.roll(piece, (me ^ k) * heads, axis=1)
    grad_mamba[:, out_at : out_at + TP * heads] = steps[:, : TP * heads]
    at += pad
    q_cols = query_ref.shape[1] // TP
    own_columns(me, refs, at, q_cols, grad_query)
    at += q_cols
    for out, start in ((grad_key, at), (grad_value, at + HD)):
        for first in (0, 2):
            both = refs[first][:, start : start + HD].astype(f32)
            both = both + refs[first + 1][:, start : start + HD].astype(f32)
            place = pl.multiple_of(((me ^ first) // 2) * HD, HD)
            out[:, pl.ds(place, HD)] = both
    pairs = ((mamba_ref, grad_mamba), (query_ref, grad_query), (key_ref, grad_key), (value_ref, grad_value))
    grad_gain[...] = gain_sum(pairs, gain_ref)


def unpack(kernel, me, parts, others, widths):
    rows = parts[0].shape[0]
    shapes = [(rows, w) for w in widths]
    return pl.pallas_call(
        kernel,
        grid=(1,),
        in_specs=[pl.BlockSpec(memory_space=pltpu.SMEM)]
        + specs(*[p.shape for p in parts], *[o.shape for o in others]),
        out_specs=specs(*shapes),
        out_shape=[jax.ShapeDtypeStruct(shape, f32) for shape in shapes],
        compiler_params=big,
        cost_estimate=costs(5),
    )(me, *parts, *others)


def weight_grad_kernel(bounds, mine, blocks, table_ref, *refs):
    parts = len(bounds)
    lefts = [refs[2 * mine * p : 2 * mine * p + mine] for p in range(parts)]
    rights = [refs[2 * mine * p + mine : 2 * mine * (p + 1)] for p in range(parts)]
    rest = refs[2 * mine * parts :]
    outs, plain, turned = rest[: -1 - parts], rest[-1 - parts], rest[-parts:]
    step = pl.program_id(0)
    size = plain.shape[0] // blocks

    @pl.when(step == 0)
    def _():
        for part in range(parts):
            plain[...] = jnp.concatenate([jnp.transpose(ref[...]) for ref in lefts[part]], axis=1)
            for block in range(blocks):
                at = pl.multiple_of(table_ref[block] * size, size)
                turned[part][block * size : (block + 1) * size, :] = plain[pl.ds(at, size), :]

    for part, (low, high) in enumerate(bounds):

        @pl.when((step >= low) & (step < high))
        def _(part=part):
            right = jnp.concatenate([ref[...] for ref in rights[part]], axis=0)
            full = jnp.dot(turned[part][...], right, preferred_element_type=f32)
            half = full.shape[0] // len(outs)
            for i, out in enumerate(outs):
                out[...] = full[i * half : (i + 1) * half].astype(out.dtype)


def weight_grads(table, pieces, pairs, tile=512):
    mine = len(pairs[0][0])
    rows, model = pairs[0][0][0].shape
    bounds, specs_in, args, low, cols = [], [], [], 0, 0
    for left, right, start, count in pairs:
        tiles = pl.cdiv(count, tile)
        first, last = low - start // tile, low + tiles - 1
        specs_in += [pl.BlockSpec((rows, model), lambda j: (0, 0))] * mine
        specs_in += [
            pl.BlockSpec(
                (rows, tile),
                lambda j, low=low, last=last, first=first: (0, jnp.clip(j, low, last) - first),
            )
        ] * mine
        args += list(left) + list(right)
        bounds.append((low, low + tiles))
        low += tiles
        cols += count
    return pl.pallas_call(
        functools.partial(weight_grad_kernel, tuple(bounds), mine, table.shape[0]),
        grid=(low,),
        in_specs=[pl.BlockSpec(memory_space=pltpu.SMEM)] + specs_in,
        out_specs=[pl.BlockSpec((model // pieces, tile), lambda j: (0, j))] * pieces,
        out_shape=[jax.ShapeDtypeStruct((model // pieces, cols), bf16)] * pieces,
        scratch_shapes=[pltpu.VMEM((model, mine * rows), bf16)] * (1 + len(pairs)),
        compiler_params=big,
        cost_estimate=costs(1 + cols // 256),
    )(table, *args)


def local(
    plane,
    tokens,
    lengths,
    offsets,
    norm_gain,
    mamba_in,
    conv_taps,
    conv_bias,
    step_bias,
    decay_log,
    skip_weight,
    mamba_gain,
    mamba_out,
    query_weight,
    key_weight,
    value_weight,
    output_weight,
    second_gain,
    gate_weight,
    up_weight,
    down_weight,
    cotangent,
):
    me = lax.axis_index("tp")
    peers = lax.axis_size(plane)
    batches, width, model = tokens.shape
    rows = batches * width
    shard = mamba_in.shape[0]
    inner = mamba_gain.shape[0]
    heads = step_bias.shape[0]
    state = (mamba_in.shape[1] - 2 * inner - heads) // 2
    q_cols = query_weight.shape[1]
    kv_heads = key_weight.shape[1] // HD
    hidden_units = gate_weight.shape[1]
    inner_t, heads_t, q_t, ff_t = inner // TP, heads // TP, q_cols // TP, hidden_units // TP
    pad = 128

    def swap(values, k, axis="tp"):
        size = lax.axis_size(axis)
        return lax.ppermute(values, axis, [(i, i ^ k) for i in range(size)])

    def spread_first(values):
        half = values.shape[1] // 2
        return swap(values[:, :half], 3), swap(values[:, half:], 1)

    def spread_second(values, far, near):
        half = values.shape[1] // 2
        pair = swap(jnp.concatenate([values[:, :half], far], axis=0), 1)
        last = swap(jnp.concatenate([values[:, half:], near], axis=0), 3)
        return values, far, pair, near, last

    def spread(values):
        return spread_second(values, *spread_first(values))

    def reduce_send(halves):
        return swap(halves[1], 1), swap(halves[3], 3)

    def reduce_add(halves, got, got_right):
        return halves[0] + got.astype(f32), halves[2] + got_right.astype(f32)

    def reduce_first(*halves):
        return reduce_add(halves, *reduce_send(halves))

    def reduce_second(pair, last):
        half = pair.shape[0] // 2
        got = swap(pair[half:].astype(bf16), 3)
        got_right = swap(last[half:].astype(bf16), 1)
        return pair[:half], got, last[:half], got_right

    def pair_send(one, two):
        return [swap(jnp.concatenate([one[i], two[i]], axis=0), k) for i, k in ((1, 1), (3, 3))]

    def pair_finish(one, two, got, got_right):
        rows = one[1].shape[0]
        half = rows // 2
        pairs = [
            reduce_add(h, got[i * rows : (i + 1) * rows], got_right[i * rows : (i + 1) * rows])
            for i, h in enumerate((one, two))
        ]
        sends = [
            swap(jnp.concatenate([p[i][half:].astype(bf16) for p in pairs], axis=0), k)
            for i, k in ((0, 3), (1, 1))
        ]
        return [
            (p[0][:half], sends[0][i * half : (i + 1) * half], p[1][:half], sends[1][i * half : (i + 1) * half])
            for i, p in enumerate(pairs)
        ]

    def reduce(*halves):
        return reduce_second(*reduce_first(*halves))

    def everywhere(values):
        return [values] + [swap(values, k) for k in range(1, TP)]

    def absolute(parts):
        stacked = jnp.stack(parts)
        return jnp.concatenate(
            [lax.dynamic_index_in_dim(stacked, me ^ t, 0) for t in range(TP)], axis=0
        )

    cube = len(plane) == 3

    def order(values):
        lead = values.shape[:-1]
        if cube:
            split = values.reshape(lead + (TP, 2, 2, 2, shard))
            split = jnp.moveaxis(split, (-2, -4, -3, -5), (-5, -4, -3, -2))
        else:
            split = jnp.swapaxes(values.reshape(lead + (TP, peers, shard)), -3, -2)
        return split.reshape(values.shape)

    def place(n):
        group, at = divmod(n, peers)
        if cube:
            x, y, core = at // 4, at // 2 % 2, at % 2
            at = core * 4 + x * 2 + y
        return at * TP + group

    places = [place(n) for n in range(peers * TP)]

    blocks = jnp.arange(peers * TP, dtype=jnp.int32)
    in_group = blocks ^ me
    in_plane = blocks ^ (lax.axis_index(plane) * TP + me)

    def cut(weight, start, size, t):
        return lax.dynamic_slice_in_dim(weight, start + t * size, size, axis=1)

    def kv(weight, t):
        return cut(weight, 0, HD, t * kv_heads // TP)

    slot_column = jnp.concatenate([lengths[:, 0], offsets[:, 0]]).astype(bf16)[:, None]

    def in_slice(t):
        return jnp.concatenate(
            [
                cut(mamba_in, 0, inner_t, t),
                cut(mamba_in, inner, inner_t, t),
                mamba_in[:, 2 * inner : 2 * inner + 2 * state],
                cut(mamba_in, 2 * inner + 2 * state, heads_t, t),
                norm_gain[:, None],
                second_gain[:, None],
                jnp.pad(slot_column, ((0, shard - 2 * batches), (0, pad - heads_t - 3))),
                cut(query_weight, 0, q_t, t),
                kv(key_weight, t),
                kv(value_weight, t),
            ],
            axis=1,
        )

    def out_slice(t):
        return jnp.concatenate([cut(mamba_out.T, 0, inner_t, t), cut(output_weight.T, 0, q_t, t)], axis=1)

    def mlp_slice(t):
        return jnp.concatenate(
            [
                cut(gate_weight, 0, ff_t, t),
                cut(up_weight, 0, ff_t, t),
                cut(down_weight.T, 0, ff_t, t),
            ],
            axis=1,
        )

    def after(values, *earlier):
        return lax.optimization_barrier((values, earlier))[0]

    def slices(make):
        return [make(me ^ k) for k in range(TP)]

    def exchange(pieces):
        return [pieces[0]] + [swap(pieces[k], k) for k in range(1, TP)]

    def gather(parts):
        return lax.all_gather(absolute(parts).reshape(TP * shard, -1), plane, axis=0, tiled=True)

    def scatter(grads):
        return lax.psum_scatter(grads, plane, scatter_dimension=0, tiled=True)

    def pass_on(part):
        part = part.reshape(TP, shard, -1)
        return exchange([part[k] for k in range(TP)])

    conv_cols = inner_t + 2 * state
    at_q = inner_t + conv_cols + pad
    in_cols = at_q + q_t + 2 * HD

    def own(values, size):
        return lax.dynamic_slice_in_dim(values, me * size, size, axis=-1)

    taps_t = jnp.concatenate([own(conv_taps[:, :inner], inner_t), conv_taps[:, inner:]], axis=1)
    bias_t = jnp.concatenate([own(conv_bias[:inner], inner_t), conv_bias[inner:]])[None]
    steps_t = jnp.pad(
        jnp.stack([own(step_bias, heads_t), own(decay_log, heads_t)]), ((0, 0), (0, pad - heads_t))
    )
    skip_t = jnp.repeat(own(skip_weight, heads_t), inner_t // heads_t)[None]
    gain_t = own(mamba_gain, inner_t)[None]
    sizes = (inner_t, state, heads_t)

    in_slices = slices(in_slice)
    in_parts = exchange(in_slices)
    tokens, cotangent = after((tokens, cotangent), in_slices)
    source = order(tokens.reshape(rows, model))
    upstream = order(cotangent.reshape(rows, model))
    prepared = (
        source, upstream, slices(out_slice), slices(mlp_slice),
        taps_t, bias_t, steps_t, skip_t, gain_t, in_plane, in_group,
    )
    in_parts, prepared = lax.optimization_barrier((in_parts, prepared))
    source, upstream, out_slices, mlp_slices = prepared[:4]
    taps_t, bias_t, steps_t, skip_t, gain_t, in_plane, in_group = prepared[4:]
    w_in = gather(in_parts)
    source_some, upstream_some = spread_first(source), spread_first(upstream)
    column = inner_t + 2 * state + inner_t + heads_t + 2
    slots = jnp.stack([in_parts[k][: 2 * batches, column] for k in (0, 3, 1, 2)])
    slots = after(slots, source_some).astype(jnp.int32).reshape(TP, 2, batches)
    slots = jnp.swapaxes(slots, 1, 2).reshape(TP * batches, 2)
    turns = turn_table(slots[:, 1], width)
    source_all = spread_second(source, *source_some)
    out_parts = exchange(after(out_slices, (source_all, upstream_some)))
    w_out = gather(out_parts)
    mlp_slices, upstream_some = after((mlp_slices, upstream_some), out_parts[1:])
    mlp_parts = exchange(mlp_slices)
    upstream_all = spread_second(upstream, *upstream_some)

    normed, projected, y, squares, mixed, gains = mixer_inner(
        slots, after(source_all, out_parts[1:]), w_in, taps_t, bias_t, steps_t, skip_t, turns, *sizes
    )
    squares = everywhere(after(squares, upstream_all))
    w_mlp = gather(after(mlp_parts, squares[1:]))
    branches, root, *halves = mixer_outer(projected, y, mixed, gain_t, squares, w_out)
    hidden, second = row_call(hidden_kernel, slots, reduce(*halves), source, gains)

    product, *halves, mlp_sums = feed_forward(
        slots, in_group, spread(second), upstream_all, w_mlp, ff_t
    )
    mlp_sums = scatter(mlp_sums)
    d_hidden, branch_grad = row_call(
        back_hidden_kernel, slots, reduce(*halves), hidden, upstream, gains
    )

    branch_all = spread(branch_grad)
    last_halves = back_out(product, w_mlp, 2)
    branch_grad = after(branch_all, last_halves)
    branch_all, d_branches, dots = back_outer(
        branch_grad, w_out, projected, y, gain_t, slots.shape[0]
    )
    out_sums = weight_grads(in_group, 1, [([branch_all], [branches], 0, inner_t + q_t)])
    dots = after(everywhere(dots), out_sums)
    out_sums = scatter(out_sums[0])
    mlp_grads = pass_on(after(mlp_sums, dots))
    proj_grad, small = mixer_backward(
        slots, projected, taps_t, bias_t, steps_t, skip_t, turns, gain_t, y, d_branches, root,
        dots, *sizes,
    )
    small = everywhere(small)
    in_sums = weight_grads(
        in_plane if cube else in_group,
        2 if cube else 1,
        [([after(normed, mlp_grads)], [proj_grad], 0, in_cols)],
    )
    norm_halves = back_out(after(proj_grad, in_sums), w_in, 0)
    pairs = pair_send(norm_halves, last_halves)
    if cube:
        block, half = TP * shard, TP * shard // 2
        counts = (block, block, block, half, half)
        keep, send = in_sums
        mine, along_y, along_x, across_x, across_y = by_columns(
            chip_kernel, counts, keep, after(swap(send, 1, "core"), (out_sums, norm_halves, small))
        )
        to_y, to_x = by_columns(
            along_kernel, (block, block), along_y, along_x, swap(across_x, 1, "x"), swap(across_y, 1, "y")
        )
        in_parts = swap(to_x, 1, "x"), swap(to_y, 1, "y")
        pairs, out_sums = after((pairs, out_sums), to_x)
    norm_parts, last_parts = pair_finish(norm_halves, last_halves, *pairs)
    out_grads = pass_on(out_sums)
    small = absolute(small)
    if cube:
        small = small + swap(small, 1, "core")
        in_parts = after(in_parts, (norm_parts, last_parts, out_grads, small))
        in_sums = by_columns(plane_kernel, (shard,) * TP, mine, *in_parts)
        in_grads = exchange(in_sums)
    else:
        in_sums = scatter(in_sums[0])
        in_grads = pass_on(in_sums)
    small, mlp_grads, out_grads, norm_parts, last_parts = after(
        (small, mlp_grads, out_grads, norm_parts, last_parts), in_sums
    )
    if cube:
        small = small + swap(small, 1, "x")
        mlp_grads = after(mlp_grads, small)
        small = small + swap(small, 1, "y")
        out_grads = after(out_grads, small)
    else:
        small = lax.psum(small, plane)
    token_grads = whole_call(
        functools.partial(token_grad_kernel, places), f32, (), *norm_parts, d_hidden, source, gains
    )
    output = whole_call(
        functools.partial(output_kernel, places), bf16, (slots,), *last_parts, hidden
    )

    at_group = me[None].astype(jnp.int32)
    grad_gate, grad_up, grad_down, grad_second_gain = unpack(
        functools.partial(unpack_mlp_kernel, ff_t),
        at_group,
        mlp_grads,
        (gate_weight, up_weight, second_gain[:, None]),
        (hidden_units, hidden_units, hidden_units, 1),
    )
    grad_mamba_out, grad_output = unpack(
        functools.partial(unpack_out_kernel, inner_t, q_t), at_group, out_grads, (), (inner, q_cols)
    )
    grad_mamba_in, grad_query, grad_key, grad_value, grad_norm_gain = unpack(
        functools.partial(unpack_in_kernel, *sizes, pad),
        at_group,
        in_grads,
        (mamba_in, query_weight, key_weight, value_weight, norm_gain[:, None]),
        (mamba_in.shape[1], q_cols, kv_heads * HD, kv_heads * HD, 1),
    )
    grad_mamba_out, grad_output, grad_down = grad_mamba_out.T, grad_output.T, grad_down.T
    grad_norm_gain, grad_second_gain = grad_norm_gain[:, 0], grad_second_gain[:, 0]

    kernel = conv_taps.shape[0]
    conv = small[:, : kernel + 1, :conv_cols]
    conv = jnp.concatenate(
        [conv[:, :, :inner_t].transpose(1, 0, 2).reshape(kernel + 1, inner), conv[:, :, inner_t:].sum(0)],
        axis=1,
    )
    by_inner = small[:, :2, conv_cols : conv_cols + inner_t]
    by_step = small[:, :2, conv_cols + inner_t : conv_cols + inner_t + heads_t]
    return (
        output.reshape(tokens.shape),
        token_grads.reshape(tokens.shape),
        grad_norm_gain,
        grad_mamba_in,
        conv[:kernel],
        conv[kernel],
        by_step[:, 0].reshape(-1),
        by_step[:, 1].reshape(-1),
        by_inner[:, 1].reshape(heads, -1).sum(1),
        by_inner[:, 0].reshape(-1),
        grad_mamba_out,
        grad_query,
        grad_key,
        grad_value,
        grad_output,
        grad_second_gain,
        grad_gate,
        grad_up,
        grad_down,
    )


def solution(mesh):
    count = mesh.devices.size
    if tuple(mesh.devices.shape) == (8, 4):
        grid = Mesh(mesh.devices.reshape(TP, 2, 2, 2), ("tp", "x", "y", "core"))
        plane = ("core", "x", "y")
    else:
        grid = Mesh(mesh.devices.reshape(TP, count // TP), ("tp", "fs"))
        plane = ("fs",)
    every = grid.axis_names
    down, across, slots = P(every, None), P(None, every), P(None, every, None)
    line, copied = P(every), P()
    return jax.shard_map(
        functools.partial(local, plane),
        mesh=grid,
        in_specs=(
            slots, across, across, line, down, copied, copied, copied, copied, copied, copied,
            across, down, down, down, across, line, down, down, across, slots,
        ),
        out_specs=(
            slots, slots, line, down, copied, copied, copied, copied, copied, copied,
            across, down, down, down, across, line, down, down, across,
        ),
        check_vma=False,
    )
```

```python
import functools
import math

import jax
import jax.numpy as jnp
from jax import lax
from jax.experimental import pallas as pl
from jax.experimental.pallas import tpu as pltpu
from jax.sharding import Mesh
from jax.sharding import PartitionSpec as P

HD = 128
TP = 4

epsilon = 1e-05
rope_base = 100000000000.0
highest = lax.Precision.HIGHEST
f32 = jnp.float32
bf16 = jnp.bfloat16


def inverse_root(values):
    return lax.rsqrt(jnp.mean(values * values, axis=-1, keepdims=True) + epsilon)


def norm_back(values, root, grad):
    return root * grad - values * root**3 * jnp.mean(values * grad, axis=-1, keepdims=True)


def dot_nn(left, right):
    return jnp.dot(left, right, preferred_element_type=f32)


def dot_nt(left, right):
    return lax.dot_general(left, right, (((1,), (1,)), ((), ())), preferred_element_type=f32)


def inside_rows(length, offset, width):
    rows = jnp.arange(width, dtype=jnp.int32)[:, None]
    return ((rows >= offset) & (rows < offset + length)).astype(f32)


def turn_table(offsets, width):
    half = HD // 2
    freqs = rope_base ** (-jnp.arange(half, dtype=f32) * 2.0 / HD)
    rows = jnp.arange(width, dtype=jnp.int32)
    positions = (rows[None, :] - offsets[:, None]).astype(f32)
    angles = positions.reshape(-1, 1) * freqs
    cosine, sine = jnp.cos(angles), jnp.sin(angles)
    return jnp.concatenate([cosine, cosine, -sine, sine], axis=1)


def mm(left, right, dims, precision=lax.Precision.HIGH):
    return lax.dot_general(left, right, (dims, ((), ())), precision=precision, preferred_element_type=f32)


NN = ((1,), (0,))
NT = ((1,), (1,))
TN = ((0,), (0,))


def iota(shape, axis):
    return lax.broadcasted_iota(jnp.int32, shape, axis)


def down_rows(values, count):
    if count == 0:
        return values
    return jnp.where(iota(values.shape, 0) >= count, pltpu.roll(values, count, axis=0), 0.0)


def up_rows(values, count):
    if count == 0:
        return values
    length = values.shape[0]
    return jnp.where(
        iota(values.shape, 0) < length - count, pltpu.roll(values, length - count, axis=0), 0.0
    )


def head_sums(values, spread):
    return mm(values, spread, NT)


def mamba_shared(proj, start, count, taps_ref, bias_ref, steps_ref, inner, state, heads):
    length = proj.shape[0]
    conv_cols = inner + 2 * state
    row = iota((length, 1), 0)
    inside = ((row >= start) & (row < start + count)).astype(f32)
    conv_in = proj[:, inner : inner + conv_cols] * inside
    kernel = taps_ref.shape[0]
    conv = bias_ref[...] + jnp.zeros_like(conv_in)
    for tap in range(kernel):
        conv = conv + taps_ref[tap : tap + 1, :] * down_rows(conv_in, kernel - 1 - tap)
    sig = jax.nn.sigmoid(conv)
    active = conv * sig
    pad = steps_ref.shape[1]
    lane = iota((length, pad), 1)
    raw = jnp.where(lane < heads, proj[:, inner + conv_cols : inner + conv_cols + pad] + steps_ref[0:1, :], 0.0)
    step = jnp.where(lane < heads, jnp.maximum(raw, 0.0) + jnp.log1p(jnp.exp(-jnp.abs(raw))), 0.0)
    rate = -jnp.exp(steps_ref[1:2, :])
    lower = (iota((length, length), 0) >= iota((length, length), 1)).astype(f32)
    cum = mm(lower, step * rate, NN, highest)
    size = inner // heads
    spread = (iota((pad, inner), 0) == iota((pad, inner), 1) // size).astype(f32)
    step_x = mm(step, spread, NN)
    cum_x = mm(cum, spread, NN, highest)
    at = iota((length, inner), 1) % length
    diagonal = iota((length, inner), 0) == at
    cum_row = jnp.sum(jnp.where(diagonal, cum_x, 0.0), axis=0, keepdims=True)
    allowed = (
        (at <= iota((length, inner), 0)) & (inside > 0.0) & (at >= start) & (at < start + count)
    )
    decay = jnp.where(allowed, jnp.exp(jnp.where(allowed, cum_x - cum_row, 0.0)), 0.0)
    xs = active[:, :inner]
    b_state = active[:, inner : inner + state]
    c_state = active[:, inner + state :]
    inter = mm(c_state, b_state, NT)
    pair = jnp.concatenate([inter, inter], axis=1)
    mixing = decay * jnp.concatenate([pair] * (inner // pair.shape[1]), axis=1)
    return dict(
        inside=inside, conv_in=conv_in, conv=conv, sig=sig, raw=raw, step=step, rate=rate,
        spread=spread, step_x=step_x, diagonal=diagonal, decay=decay, mixing=mixing, xs=xs,
        b_state=b_state, c_state=c_state, lower=lower, lane=lane,
    )


def two_blocks(values):
    left = iota(values.shape, 1) < values.shape[1] // 2
    return jnp.concatenate([jnp.where(left, values, 0.0), jnp.where(left, 0.0, values)], axis=0)


def turn(values, cosine, sine):
    return values * cosine + pltpu.roll(values, HD // 2, axis=1) * sine


def attention_shared(proj, at, start, count, cosine, sine):
    length = proj.shape[0]
    kv = proj.shape[1] - 2 * HD
    queries = jnp.concatenate(
        [turn(proj[:, c : c + HD], cosine, sine) for c in range(at, kv, HD)], axis=0
    )
    keys = turn(proj[:, kv : kv + HD], cosine, sine)
    values = proj[:, kv + HD :]
    scores = mm(queries, keys, NT) * (1.0 / math.sqrt(HD))
    row = iota(scores.shape, 0) % length
    col = iota(scores.shape, 1)
    end = start + count
    allowed = ((row >= start) & (row < end) & (col >= start) & (col <= row)) | (row == col)
    scores = jnp.where(allowed, scores, -1e30)
    probs = jnp.exp(scores - jnp.max(scores, axis=1, keepdims=True))
    probs = probs / jnp.sum(probs, axis=1, keepdims=True)
    return queries, keys, values, probs


def specs(*shapes):
    return [pl.BlockSpec(s, lambda i: (0, 0)) for s in shapes]


def rows_spec(length, cols):
    return pl.BlockSpec((length, cols), lambda i: (i, 0))


def their_spec(length, each, k):
    return pl.BlockSpec((1, 1, length), lambda i: (i ^ (THEIRS[k][0] * each), 0, 0))


big = pltpu.CompilerParams(vmem_limit_bytes=50 * 1024 * 1024)


def costs(microseconds):
    return pl.CostEstimate(
        flops=microseconds * 10**9, bytes_accessed=microseconds * 10**5, transcendentals=0
    )


def inside_of(slots_ref, seq, length):
    row = iota((length, 1), 0)
    start = slots_ref[seq, 1]
    return ((row >= start) & (row < start + slots_ref[seq, 0])).astype(f32)


def as_row(column):
    length = column.shape[0]
    same = iota((length, length), 0) == iota((length, length), 1)
    return jnp.sum(jnp.where(same, column, 0.0), axis=0, keepdims=True)


def as_column(row):
    length = row.shape[1]
    same = iota((length, length), 0) == iota((length, length), 1)
    return jnp.sum(jnp.where(same, row, 0.0), axis=1, keepdims=True)


THEIRS = ((0, 1, 2, 3), (2, 3, 0, 1), (3, 2, 1, 0), (1, 0, 3, 2))


def group_total(refs, seq):
    each = refs[0].shape[0] // TP
    return sum(ref[THEIRS[k][seq // each] * each + seq % each] for k, ref in enumerate(refs))


def joined_rows(refs):
    own, far, pair, near, last = refs
    half = far.shape[1]
    count = own.shape[0]
    left = jnp.concatenate([own[:, :half], far[...], pair[...]], axis=0)
    right = jnp.concatenate([own[:, half:], last[:count, :], near[...], last[count:, :]], axis=0)
    return jnp.concatenate([left, right], axis=1)


def put_left(values, refs):
    half = values.shape[0] // 2
    refs[0][...] = values[:half]
    refs[1][...] = values[half:].astype(bf16)


def put_right(values, refs):
    one = values.shape[0] // TP
    refs[2][:one, :] = values[:one]
    refs[2][one:, :] = values[2 * one : 3 * one]
    refs[3][:one, :] = values[one : 2 * one].astype(bf16)
    refs[3][one:, :] = values[3 * one :].astype(bf16)


def put_tiles(values, refs):
    step = pl.program_id(0)
    middle = pl.num_programs(0) // 2

    @pl.when(step < middle)
    def _():
        put_left(values, refs)

    @pl.when(step >= middle)
    def _():
        put_right(values, refs)


def halves_out(rows, model, tile):
    middle = model // tile // 2
    left = pl.BlockSpec((rows // 2, tile), lambda j: (0, jnp.minimum(j, middle - 1)))
    right = pl.BlockSpec((rows // 2, tile), lambda j: (0, jnp.maximum(j - middle, 0)))
    shapes = [jax.ShapeDtypeStruct((rows // 2, model // 2), t) for t in (f32, bf16, f32, bf16)]
    return [left, left, right, right], shapes


def both_halves(refs):
    kept, got, kept_right, got_right = refs
    return jnp.concatenate(
        [kept[...] + got[...].astype(f32), kept_right[...] + got_right[...].astype(f32)], axis=1
    )


def inner_kernel(
    inner, state, heads, tiles, slots_ref, p0, p1, p2, p3, p4, weight_ref, gains_in_ref, taps_ref, bias_ref,
    steps_ref, skip_ref, turn_ref, normed_ref, proj_ref, y_ref, square_ref, mixed_ref, gains_ref,
):
    step = pl.program_id(0)
    tile = weight_ref.shape[1]

    @pl.when(step == 0)
    def _():
        rows = joined_rows((p0, p1, p2, p3, p4)).astype(f32)
        turned = jnp.transpose(gains_in_ref[...].astype(f32))
        gains_ref[0:1, :] = turned[heads : heads + 1]
        gains_ref[1:2, :] = turned[heads + 1 : heads + 2]
        normed_ref[...] = (rows * inverse_root(rows) * turned[heads : heads + 1]).astype(bf16)

    @pl.when(step < tiles)
    def _():
        at = pl.multiple_of(step * tile, tile)
        proj_ref[:, pl.ds(at, tile)] = jnp.dot(
            normed_ref[...], weight_ref[...], preferred_element_type=f32
        )

    @pl.when(step >= tiles)
    def _():
        seq = step - tiles
        length = y_ref.shape[0]
        proj = proj_ref[pl.ds(pl.multiple_of(seq * length, length), length), :]
        start = slots_ref[seq, 1]
        count = slots_ref[seq, 0]
        m = mamba_shared(proj, start, count, taps_ref, bias_ref, steps_ref, inner, state, heads)
        scaled = m["xs"] * m["step_x"]
        wide = 2 * length
        parts = [
            mm(m["mixing"][:, c : c + wide], two_blocks(scaled[:, c : c + wide]), NN)
            for c in range(0, inner, wide)
        ]
        y = jnp.concatenate(parts, axis=1) + skip_ref[...] * m["xs"]
        y_ref[...] = y
        gate = proj[:, :inner]
        gated = y * gate * jax.nn.sigmoid(gate)
        square_ref[0] = as_row(jnp.sum(gated * gated, axis=1, keepdims=True))
        at = 2 * inner + 2 * state + steps_ref.shape[1]
        _, _, values, probs = attention_shared(
            proj, at, start, count, turn_ref[:, :HD], turn_ref[:, HD:]
        )
        mixed = mm(probs, values, NN)
        mixed_ref[...] = jnp.concatenate(
            [mixed[r : r + length] for r in range(0, mixed.shape[0], length)], axis=1
        ).astype(mixed_ref.dtype)


def mixer_inner(slots, rows, weight, taps, bias, steps, skip, turns, inner, state, heads, tile=384):
    model, cols = weight.shape
    seqs = slots.shape[0]
    pieces = rows
    rows = TP * pieces[0].shape[0]
    length = rows // seqs
    tiles = cols // tile
    pad = steps.shape[1]
    at_steps = (2 * inner + 2 * state) // pad
    q_cols = cols - 2 * inner - 2 * state - pad - 2 * HD

    def seq_spec(*shape):
        zeros = (0,) * (len(shape) - 1)
        return pl.BlockSpec(shape, lambda j: (jnp.maximum(j - tiles, 0),) + zeros)

    return pl.pallas_call(
        functools.partial(inner_kernel, inner, state, heads, tiles),
        grid=(tiles + seqs,),
        in_specs=[pl.BlockSpec(memory_space=pltpu.SMEM)]
        + specs(*[p.shape for p in pieces])
        + [
            pl.BlockSpec((model, tile), lambda j: (0, jnp.minimum(j, tiles - 1))),
            pl.BlockSpec((model, pad), lambda j: (0, at_steps)),
        ]
        + specs(taps.shape, bias.shape, steps.shape, skip.shape)
        + [seq_spec(length, turns.shape[1])],
        out_specs=specs((rows, model), (rows, cols))
        + [seq_spec(length, inner), seq_spec(1, 1, length), seq_spec(length, q_cols)]
        + specs((8, model)),
        out_shape=[
            jax.ShapeDtypeStruct((rows, model), bf16),
            jax.ShapeDtypeStruct((rows, cols), f32),
            jax.ShapeDtypeStruct((rows, inner), f32),
            jax.ShapeDtypeStruct((seqs, 1, length), f32),
            jax.ShapeDtypeStruct((rows, q_cols), bf16),
            jax.ShapeDtypeStruct((8, model), f32),
        ],
        compiler_params=big,
        cost_estimate=costs(18),
    )(slots, *pieces, weight, weight, taps, bias, steps, skip, turns)


def outer_kernel(inner, gate_ref, y_ref, mixed_ref, gain_ref, s0, s1, s2, s3, weight_ref, branches_ref, root_ref, *halves):
    @pl.when(pl.program_id(0) == 0)
    def _():
        length = root_ref.shape[2]
        for seq in range(root_ref.shape[0]):
            rows = slice(seq * length, (seq + 1) * length)
            root = lax.rsqrt(group_total((s0, s1, s2, s3), seq) / (TP * inner) + epsilon)
            root_ref[seq] = root
            gate = gate_ref[rows, :]
            gated = y_ref[rows, :] * gate * jax.nn.sigmoid(gate)
            branches_ref[rows, :inner] = (gated * as_column(root) * gain_ref[...]).astype(bf16)
        branches_ref[:, inner:] = mixed_ref[...]

    put_tiles(dot_nt(branches_ref[...], weight_ref[...]), halves)


def mixer_outer(proj, y, mixed, gain, squares, weight, tile=512):
    rows, inner = y.shape
    model, cols = weight.shape
    half_specs, half_shapes = halves_out(rows, model, tile)
    return pl.pallas_call(
        functools.partial(outer_kernel, inner),
        grid=(model // tile,),
        in_specs=specs((rows, inner), y.shape, mixed.shape, gain.shape)
        + [pl.BlockSpec(squares[0].shape, lambda j: (0, 0, 0))] * TP
        + [pl.BlockSpec((tile, cols), lambda j: (j, 0))],
        out_specs=specs((rows, cols))
        + [pl.BlockSpec(squares[0].shape, lambda j: (0, 0, 0))]
        + half_specs,
        out_shape=[
            jax.ShapeDtypeStruct((rows, cols), bf16),
            jax.ShapeDtypeStruct(squares[0].shape, f32),
        ]
        + half_shapes,
        compiler_params=big,
        cost_estimate=costs(4),
    )(proj, y, mixed, gain, *squares, weight)


def back_out_kernel(left_ref, weight_ref, *halves):
    put_tiles(dot_nt(left_ref[...], weight_ref[...]), halves)


def back_out(left, weight, column, tile=512):
    rows, cols = left.shape
    model = weight.shape[0]
    half_specs, half_shapes = halves_out(rows, model, tile)
    return pl.pallas_call(
        back_out_kernel,
        grid=(model // tile,),
        in_specs=specs(left.shape) + [pl.BlockSpec((tile, cols), lambda j: (j, column))],
        out_specs=half_specs,
        out_shape=half_shapes,
        compiler_params=big,
        cost_estimate=costs(4),
    )(left, weight)


def inside_all(slots_ref, seqs, length):
    return jnp.concatenate([inside_of(slots_ref, seq, length) for seq in range(seqs)], axis=0)


def hidden_kernel(slots_ref, k0, k1, k2, k3, source_ref, gains_ref, hidden_ref, second_ref):
    length = source_ref.shape[0] * TP // slots_ref.shape[0]
    inside = inside_all(slots_ref, slots_ref.shape[0] // TP, length)
    hidden = source_ref[...].astype(f32) + inside * both_halves((k0, k1, k2, k3))
    hidden_ref[...] = hidden
    second_ref[...] = (hidden * inverse_root(hidden) * gains_ref[1:2, :]).astype(bf16)


def row_call(kernel, slots, halves, *others):
    shape = others[0].shape
    return pl.pallas_call(
        kernel,
        grid=(1,),
        in_specs=[pl.BlockSpec(memory_space=pltpu.SMEM)]
        + specs(*[h.shape for h in halves], *[o.shape for o in others]),
        out_specs=specs(shape, shape),
        out_shape=[jax.ShapeDtypeStruct(shape, f32), jax.ShapeDtypeStruct(shape, bf16)],
        compiler_params=big,
        cost_estimate=costs(2),
    )(slots, *halves, *others)


def feed_kernel(
    steps, blocks, slots_ref, table_ref, s0, s1, s2, s3, s4, c0, c1, c2, c3, c4, gate_ref, up_ref, down_ref,
    product_ref, h0, h1, h2, h3, grads_ref,
    second_ref, down_grad_ref, gate_grad_ref, up_grad_ref, total, second_turned, down_turned,
):
    step = pl.program_id(0)
    tile = gate_ref.shape[1]

    @pl.when(step == 0)
    def _():
        second_ref[...] = joined_rows((s0, s1, s2, s3, s4))
        seqs = slots_ref.shape[0]
        inside = inside_all(slots_ref, seqs, TP * s0.shape[0] // seqs)
        down_grad_ref[...] = (inside * joined_rows((c0, c1, c2, c3, c4)).astype(f32)).astype(bf16)
        total[...] = jnp.zeros_like(total)

    @pl.when(step < steps)
    def _():
        second = second_ref[...]
        gate = jnp.dot(second, gate_ref[...], preferred_element_type=f32)
        up = jnp.dot(second, up_ref[...], preferred_element_type=f32)
        d_product = jnp.dot(down_grad_ref[...], down_ref[...], preferred_element_type=f32)
        sig = jax.nn.sigmoid(gate)
        swish = gate * sig
        gate_grad = (d_product * up * sig * (1.0 + gate * (1.0 - sig))).astype(bf16)
        up_grad = (d_product * swish).astype(bf16)
        at = pl.ds(pl.multiple_of(step * tile, tile), tile)
        product_ref[:, at] = (swish * up).astype(bf16)
        gate_grad_ref[:, at] = gate_grad
        up_grad_ref[:, at] = up_grad
        total[...] += dot_nt(gate_grad, gate_ref[...]) + dot_nt(up_grad, up_ref[...])

    @pl.when(step == steps - 1)
    def _():
        middle = total.shape[1] // 2
        put_left(total[:, :middle], (h0, h1))
        put_right(total[:, middle:], (h0, h1, h2, h3))
        size = second_ref.shape[1] // blocks
        for source, turned in ((second_ref, second_turned), (down_grad_ref, down_turned)):
            plain = jnp.transpose(source[...])
            total_rows = plain.shape[0]
            grads_ref[:total_rows, : plain.shape[1]] = plain
            for block in range(blocks):
                start = pl.multiple_of(table_ref[block] * size, size)
                turned[block * size : (block + 1) * size, :] = grads_ref[pl.ds(start, size), : plain.shape[1]]

    for part, (turned, right) in enumerate(
        ((second_turned, gate_grad_ref), (second_turned, up_grad_ref), (down_turned, product_ref))
    ):

        @pl.when((step >= (part + 1) * steps) & (step < (part + 2) * steps))
        def _(part=part, turned=turned, right=right):
            at = pl.multiple_of((step - (part + 1) * steps) * tile, tile)
            grads_ref[...] = jnp.dot(
                turned[...], right[:, pl.ds(at, tile)], preferred_element_type=f32
            ).astype(bf16)


def feed_forward(slots, table, second, cotangent, weight, units, tile=512):
    count, model = second[0].shape
    rows = TP * count
    steps = units // tile
    half_shapes = halves_out(rows, model, tile)[1]
    shapes = [p.shape for p in second]
    return pl.pallas_call(
        functools.partial(feed_kernel, steps, table.shape[0]),
        grid=(4 * steps,),
        in_specs=[pl.BlockSpec(memory_space=pltpu.SMEM)] * 2
        + specs(*shapes, *shapes)
        + [
            pl.BlockSpec((model, tile), lambda j, at=at: (0, at * steps + jnp.minimum(j, steps - 1)))
            for at in range(3)
        ],
        out_specs=specs((rows, units), *[h.shape for h in half_shapes])
        + [pl.BlockSpec((model, tile), lambda j: (0, jnp.maximum(j - steps, 0)))],
        out_shape=[jax.ShapeDtypeStruct((rows, units), bf16)]
        + half_shapes
        + [jax.ShapeDtypeStruct((model, 3 * units), bf16)],
        scratch_shapes=[pltpu.VMEM((rows, model), bf16)] * 2
        + [pltpu.VMEM((rows, units), bf16)] * 2
        + [pltpu.VMEM((rows, model), f32)]
        + [pltpu.VMEM((model, rows), bf16)] * 2,
        compiler_params=big,
        cost_estimate=costs(30),
    )(slots, table, *second, *cotangent, weight, weight, weight)


def in_places(values, places):
    size = values.shape[1] // len(places)
    return jnp.concatenate([values[:, p * size : (p + 1) * size] for p in places], axis=1)


def output_kernel(places, slots_ref, k0, k1, k2, k3, hidden_ref, output_ref):
    seqs = slots_ref.shape[0]
    inside = inside_all(slots_ref, seqs // TP, hidden_ref.shape[0] * TP // seqs)
    output = (hidden_ref[...] + inside * both_halves((k0, k1, k2, k3))).astype(bf16)
    output_ref[...] = in_places(output, places)


def token_grad_kernel(places, k0, k1, k2, k3, hidden_ref, source_ref, gains_ref, grad_ref):
    grad = both_halves((k0, k1, k2, k3)) * gains_ref[0:1, :]
    source = source_ref[...].astype(f32)
    total = hidden_ref[...] + norm_back(source, inverse_root(source), grad)
    grad_ref[...] = in_places(total, places)


def whole_call(kernel, dtype, scalars, *arrays):
    shape = arrays[4].shape
    return pl.pallas_call(
        kernel,
        grid=(1,),
        in_specs=[pl.BlockSpec(memory_space=pltpu.SMEM)] * len(scalars) + specs(*[a.shape for a in arrays]),
        out_specs=pl.BlockSpec(shape, lambda i: (0, 0)),
        out_shape=jax.ShapeDtypeStruct(shape, dtype),
        compiler_params=big,
        cost_estimate=costs(3),
    )(*scalars, *arrays)


def back_hidden_kernel(slots_ref, k0, k1, k2, k3, hidden_ref, cotangent_ref, gains_ref, d_hidden_ref, branch_ref):
    grad = both_halves((k0, k1, k2, k3)) * gains_ref[1:2, :]
    hidden = hidden_ref[...]
    d_hidden = cotangent_ref[...].astype(f32) + norm_back(hidden, inverse_root(hidden), grad)
    d_hidden_ref[...] = d_hidden
    seqs = slots_ref.shape[0]
    inside = inside_all(slots_ref, seqs // TP, hidden.shape[0] * TP // seqs)
    branch_ref[...] = (inside * d_hidden).astype(bf16)


def back_outer_kernel(tiles, b0, b1, b2, b3, b4, weight_ref, gate_ref, y_ref, gain_ref, branch_ref, grad_ref, dots_ref, total):
    step = pl.program_id(0)

    @pl.when(step == 0)
    def _():
        branch_ref[...] = joined_rows((b0, b1, b2, b3, b4))
        total[...] = jnp.zeros_like(total)

    grad = jnp.dot(branch_ref[...], weight_ref[...], preferred_element_type=f32)
    grad_ref[...] = grad

    @pl.when(step < tiles)
    def _():
        gate = gate_ref[...]
        gated = y_ref[...] * gate * jax.nn.sigmoid(gate)
        total[...] += jnp.sum(gated * gain_ref[...] * grad, axis=1, keepdims=True)

    @pl.when(step == pl.num_programs(0) - 1)
    def _():
        length = dots_ref.shape[2]
        for seq in range(dots_ref.shape[0]):
            dots_ref[seq] = as_row(total[seq * length : (seq + 1) * length, :])


def back_outer(branch, weight, proj, y, gain, seqs, tile=256):
    model = weight.shape[0]
    rows, inner = y.shape
    cols = weight.shape[1]
    tiles = inner // tile
    length = rows // seqs
    inner_spec = pl.BlockSpec((rows, tile), lambda j: (0, jnp.minimum(j, tiles - 1)))
    return pl.pallas_call(
        functools.partial(back_outer_kernel, tiles),
        grid=(cols // tile,),
        in_specs=specs(*[p.shape for p in branch])
        + [
            pl.BlockSpec((model, tile), lambda j: (0, j)),
            inner_spec,
            inner_spec,
            pl.BlockSpec((1, tile), lambda j: (0, jnp.minimum(j, tiles - 1))),
        ],
        out_specs=specs((rows, model))
        + [
            pl.BlockSpec((rows, tile), lambda j: (0, j)),
            pl.BlockSpec((seqs, 1, length), lambda j: (0, 0, 0)),
        ],
        out_shape=[
            jax.ShapeDtypeStruct((rows, model), bf16),
            jax.ShapeDtypeStruct((rows, cols), f32),
            jax.ShapeDtypeStruct((seqs, 1, length), f32),
        ],
        scratch_shapes=[pltpu.VMEM((rows, 1), f32)],
        compiler_params=big,
        cost_estimate=costs(5),
    )(*branch, weight, proj, y, gain)


def backward_kernel(
    inner, state, heads, slots_ref, proj_ref, taps_ref, bias_ref, steps_ref, skip_ref, turn_ref,
    gain_ref, y_ref, grad_ref, root_ref, d0, d1, d2, d3, proj_grad_ref, small_ref,
):
    step_id = pl.program_id(0)
    start = slots_ref[step_id, 1]
    count = slots_ref[step_id, 0]
    proj = proj_ref[...]
    length = proj.shape[0]
    conv_cols = inner + 2 * state
    pad = steps_ref.shape[1]
    m = mamba_shared(proj, start, count, taps_ref, bias_ref, steps_ref, inner, state, heads)
    xs, decay, mixing = m["xs"], m["decay"], m["mixing"]
    scaled = xs * m["step_x"]
    gate = proj[:, :inner]
    gate_sig = jax.nn.sigmoid(gate)
    y = y_ref[...]
    root = as_column(root_ref[0])
    mean = as_column(sum(ref[0] for ref in (d0, d1, d2, d3))) / (TP * inner)
    gated = y * gate * gate_sig
    d_norm = grad_ref[:, :inner]
    d_gated = root * (d_norm * gain_ref[...]) - gated * (root * root * root * mean)
    dy = d_gated * gate * gate_sig
    d_gate = d_gated * y * gate_sig * (1.0 + gate * (1.0 - gate_sig))
    wide = 2 * length
    back, d_mix = [], []
    for c in range(0, inner, wide):
        dy_pair = dy[:, c : c + wide]
        full = mm(mixing[:, c : c + wide], dy_pair, TN)
        left = iota((length, wide), 1) < length
        back.append(jnp.where(left, full[:length], full[length:]))
        d_mix.append(mm(dy_pair, two_blocks(scaled[:, c : c + wide]), NT))
    back = jnp.concatenate(back, axis=1)
    d_mix = jnp.concatenate(d_mix, axis=1)
    d_xs = skip_ref[...] * dy + m["step_x"] * back
    flow = d_mix * mixing
    flow = flow - jnp.where(m["diagonal"], jnp.sum(flow, axis=0, keepdims=True), 0.0)
    d_cum = head_sums(flow, m["spread"])
    d_rate = mm(m["lower"], d_cum, TN, highest)
    d_step = head_sums(xs * back, m["spread"]) + d_rate * m["rate"]
    d_raw = jnp.where(m["lane"] < heads, d_step * jax.nn.sigmoid(m["raw"]), 0.0)
    d_inter = d_mix * decay
    pair = d_inter[:, :wide]
    for c in range(wide, inner, wide):
        pair = pair + d_inter[:, c : c + wide]
    d_inter = pair[:, :length] + pair[:, length:]
    d_b = mm(d_inter, m["c_state"], TN)
    d_c = mm(d_inter, m["b_state"], NN)
    d_active = jnp.concatenate([d_xs, d_b, d_c], axis=1)
    sig, conv = m["sig"], m["conv"]
    d_conv = d_active * sig * (1.0 + conv * (1.0 - sig))
    kernel = taps_ref.shape[0]
    d_in = jnp.zeros_like(d_conv)
    conv_rows = []
    for tap in range(kernel):
        back_by = kernel - 1 - tap
        d_in = d_in + taps_ref[tap : tap + 1, :] * up_rows(d_conv, back_by)
        conv_rows.append(jnp.sum(d_conv * down_rows(m["conv_in"], back_by), axis=0, keepdims=True))
    conv_rows.append(jnp.sum(d_conv, axis=0, keepdims=True))
    conv_rows.append(jnp.zeros((8 - kernel - 1, conv_cols), f32))
    conv_rows = jnp.concatenate(conv_rows, axis=0)
    inner_rows = jnp.concatenate(
        [
            jnp.sum(gated * root * d_norm, axis=0, keepdims=True),
            jnp.sum(dy * xs, axis=0, keepdims=True),
            jnp.zeros((6, inner), f32),
        ],
        axis=0,
    )
    step_rows = jnp.concatenate(
        [
            jnp.sum(d_raw, axis=0, keepdims=True),
            jnp.sum(d_rate * m["step"] * m["rate"], axis=0, keepdims=True),
            jnp.zeros((6, pad), f32),
        ],
        axis=0,
    )

    rows = jnp.concatenate([conv_rows, inner_rows, step_rows], axis=1)
    wide = small_ref.shape[1]
    rows = jnp.concatenate(
        [rows, jnp.zeros((8, small_ref.shape[0] // 8 * wide - rows.shape[1]), f32)], axis=1
    )
    rows = jnp.concatenate([rows[:, c : c + wide] for c in range(0, rows.shape[1], wide)], axis=0)

    @pl.when(step_id == 0)
    def _():
        small_ref[...] = jnp.zeros_like(small_ref)

    small_ref[...] += rows

    at = inner + conv_cols + pad
    cosine, sine = turn_ref[:, :HD], turn_ref[:, HD:]
    queries, keys, values, probs = attention_shared(proj, at, start, count, cosine, sine)
    d_out = jnp.concatenate(
        [grad_ref[:, c : c + HD] for c in range(inner, grad_ref.shape[1], HD)], axis=0
    )
    d_values = mm(probs, d_out, TN)
    d_probs = mm(d_out, values, NT)
    d_scores = probs * (d_probs - jnp.sum(probs * d_probs, axis=1, keepdims=True)) * (1.0 / math.sqrt(HD))
    d_queries = mm(d_scores, keys, NN)
    d_keys = mm(d_scores, queries, TN)
    outs = [d_gate, d_in * m["inside"], d_raw]
    outs += [turn(d_queries[r : r + length], cosine, -sine) for r in range(0, d_queries.shape[0], length)]
    outs += [turn(d_keys, cosine, -sine), d_values]
    proj_grad_ref[...] = jnp.concatenate(outs, axis=1).astype(proj_grad_ref.dtype)


def mixer_backward(
    slots, proj, taps, bias, steps, skip, turns, gain, y, grads, root, dots, inner, state, heads
):
    seqs = slots.shape[0]
    rows, cols = proj.shape
    length = rows // seqs
    conv_cols = inner + 2 * state
    pad = steps.shape[1]
    small_shape = (8 * pl.cdiv(conv_cols + inner + pad, grads.shape[1]), grads.shape[1])
    return pl.pallas_call(
        functools.partial(backward_kernel, inner, state, heads),
        grid=(seqs,),
        in_specs=[pl.BlockSpec(memory_space=pltpu.SMEM), rows_spec(length, cols)]
        + specs(taps.shape, bias.shape, steps.shape, skip.shape)
        + [rows_spec(length, turns.shape[1])]
        + specs(gain.shape)
        + [rows_spec(length, inner), rows_spec(length, grads.shape[1])]
        + [pl.BlockSpec((1, 1, length), lambda i: (i, 0, 0))]
        + [their_spec(length, seqs // TP, k) for k in range(TP)],
        out_specs=[rows_spec(length, cols)] + specs(small_shape),
        out_shape=[
            jax.ShapeDtypeStruct((rows, cols), bf16),
            jax.ShapeDtypeStruct(small_shape, f32),
        ],
        compiler_params=big,
        cost_estimate=costs(17),
    )(slots, proj, taps, bias, steps, skip, turns, gain, y, grads, root, *dots)


def chip_kernel(keep_ref, got_ref, mine_ref, along_y_ref, along_x_ref, across_x_ref, across_y_ref):
    total = (keep_ref[...].astype(f32) + got_ref[...].astype(f32)).astype(bf16)
    block = mine_ref.shape[0]
    half = across_x_ref.shape[0]
    mine_ref[...] = total[:block]
    along_y_ref[...] = total[block : 2 * block]
    along_x_ref[...] = total[2 * block : 3 * block]
    across_x_ref[...] = total[3 * block : 3 * block + half]
    across_y_ref[...] = total[3 * block + half :]


def along_kernel(along_y_ref, along_x_ref, by_x_ref, by_y_ref, to_y_ref, to_x_ref):
    half = by_x_ref.shape[0]
    to_y_ref[...] = along_y_ref[...]
    to_y_ref[:half, :] = (along_y_ref[:half, :].astype(f32) + by_x_ref[...].astype(f32)).astype(bf16)
    to_x_ref[...] = along_x_ref[...]
    to_x_ref[half:, :] = (along_x_ref[half:, :].astype(f32) + by_y_ref[...].astype(f32)).astype(bf16)


def plane_kernel(mine_ref, by_x_ref, by_y_ref, *outs):
    total = mine_ref[...].astype(f32) + by_x_ref[...].astype(f32) + by_y_ref[...].astype(f32)
    size = outs[0].shape[0]
    for k, out in enumerate(outs):
        out[...] = total[k * size : (k + 1) * size].astype(bf16)


def by_columns(kernel, row_counts, *arrays, tile=896):
    cols = arrays[0].shape[1]

    def of(rows):
        return pl.BlockSpec((rows, tile), lambda j: (0, j))

    return pl.pallas_call(
        kernel,
        grid=(cols // tile,),
        in_specs=[of(a.shape[0]) for a in arrays],
        out_specs=[of(r) for r in row_counts],
        out_shape=[jax.ShapeDtypeStruct((r, cols), bf16) for r in row_counts],
        compiler_params=big,
        cost_estimate=costs(3),
    )(*arrays)


def own_columns(me, refs, start, size, out_ref, at=0):
    for k, ref in enumerate(refs):
        place = pl.multiple_of((me ^ k) * size, 128)
        out_ref[:, pl.ds(at + place, size)] = ref[:, start : start + size].astype(f32)


def gain_sum(pairs, gain_ref):
    total = sum(
        jnp.sum(weight[...].astype(f32) * grad[...], axis=1, keepdims=True) for weight, grad in pairs
    )
    return total / gain_ref[...].astype(f32)


def unpack_mlp_kernel(units, me_ref, g0, g1, g2, g3, gate_ref, up_ref, gain_ref, grad_gate, grad_up, grad_down, grad_gain):
    for i, out in enumerate((grad_gate, grad_up, grad_down)):
        own_columns(me_ref[0], (g0, g1, g2, g3), i * units, units, out)
    grad_gain[...] = gain_sum(((gate_ref, grad_gate), (up_ref, grad_up)), gain_ref)


def unpack_out_kernel(inner, q_cols, me_ref, g0, g1, g2, g3, grad_mamba, grad_output):
    own_columns(me_ref[0], (g0, g1, g2, g3), 0, inner, grad_mamba)
    own_columns(me_ref[0], (g0, g1, g2, g3), inner, q_cols, grad_output)


def unpack_in_kernel(
    inner, state, heads, pad, me_ref, g0, g1, g2, g3, mamba_ref, query_ref, key_ref, value_ref, gain_ref,
    grad_mamba, grad_query, grad_key, grad_value, grad_gain,
):
    me = me_ref[0]
    refs = (g0, g1, g2, g3)
    own_columns(me, refs, 0, inner, grad_mamba)
    own_columns(me, refs, inner, inner, grad_mamba, TP * inner)
    at, out_at = 2 * inner, 2 * TP * inner
    shared = sum(ref[:, at : at + 2 * state].astype(f32) for ref in refs)
    grad_mamba[:, out_at : out_at + 2 * state] = shared
    at, out_at = at + 2 * state, out_at + 2 * state
    lane = iota((grad_mamba.shape[0], pad), 1)
    steps = jnp.zeros((grad_mamba.shape[0], pad), f32)
    for k, ref in enumerate(refs):
        piece = jnp.where(lane < heads, ref[:, at : at + pad].astype(f32), 0.0)
        steps = steps + pltpu.roll(piece, (me ^ k) * heads, axis=1)
    grad_mamba[:, out_at : out_at + TP * heads] = steps[:, : TP * heads]
    at += pad
    q_cols = query_ref.shape[1] // TP
    own_columns(me, refs, at, q_cols, grad_query)
    at += q_cols
    for out, start in ((grad_key, at), (grad_value, at + HD)):
        for first in (0, 2):
            both = refs[first][:, start : start + HD].astype(f32)
            both = both + refs[first + 1][:, start : start + HD].astype(f32)
            place = pl.multiple_of(((me ^ first) // 2) * HD, HD)
            out[:, pl.ds(place, HD)] = both
    pairs = ((mamba_ref, grad_mamba), (query_ref, grad_query), (key_ref, grad_key), (value_ref, grad_value))
    grad_gain[...] = gain_sum(pairs, gain_ref)


def unpack(kernel, me, parts, others, widths):
    rows = parts[0].shape[0]
    shapes = [(rows, w) for w in widths]
    return pl.pallas_call(
        kernel,
        grid=(1,),
        in_specs=[pl.BlockSpec(memory_space=pltpu.SMEM)]
        + specs(*[p.shape for p in parts], *[o.shape for o in others]),
        out_specs=specs(*shapes),
        out_shape=[jax.ShapeDtypeStruct(shape, f32) for shape in shapes],
        compiler_params=big,
        cost_estimate=costs(5),
    )(me, *parts, *others)


def weight_grad_kernel(bounds, mine, blocks, table_ref, *refs):
    parts = len(bounds)
    lefts = [refs[2 * mine * p : 2 * mine * p + mine] for p in range(parts)]
    rights = [refs[2 * mine * p + mine : 2 * mine * (p + 1)] for p in range(parts)]
    rest = refs[2 * mine * parts :]
    outs, plain, turned = rest[: -1 - parts], rest[-1 - parts], rest[-parts:]
    step = pl.program_id(0)
    size = plain.shape[0] // blocks

    @pl.when(step == 0)
    def _():
        for part in range(parts):
            plain[...] = jnp.concatenate([jnp.transpose(ref[...]) for ref in lefts[part]], axis=1)
            for block in range(blocks):
                at = pl.multiple_of(table_ref[block] * size, size)
                turned[part][block * size : (block + 1) * size, :] = plain[pl.ds(at, size), :]

    for part, (low, high) in enumerate(bounds):

        @pl.when((step >= low) & (step < high))
        def _(part=part):
            right = jnp.concatenate([ref[...] for ref in rights[part]], axis=0)
            full = jnp.dot(turned[part][...], right, preferred_element_type=f32)
            half = full.shape[0] // len(outs)
            for i, out in enumerate(outs):
                out[...] = full[i * half : (i + 1) * half].astype(out.dtype)


def weight_grads(table, pieces, pairs, tile=512):
    mine = len(pairs[0][0])
    rows, model = pairs[0][0][0].shape
    bounds, specs_in, args, low, cols = [], [], [], 0, 0
    for left, right, start, count in pairs:
        tiles = pl.cdiv(count, tile)
        first, last = low - start // tile, low + tiles - 1
        specs_in += [pl.BlockSpec((rows, model), lambda j: (0, 0))] * mine
        specs_in += [
            pl.BlockSpec(
                (rows, tile),
                lambda j, low=low, last=last, first=first: (0, jnp.clip(j, low, last) - first),
            )
        ] * mine
        args += list(left) + list(right)
        bounds.append((low, low + tiles))
        low += tiles
        cols += count
    return pl.pallas_call(
        functools.partial(weight_grad_kernel, tuple(bounds), mine, table.shape[0]),
        grid=(low,),
        in_specs=[pl.BlockSpec(memory_space=pltpu.SMEM)] + specs_in,
        out_specs=[pl.BlockSpec((model // pieces, tile), lambda j: (0, j))] * pieces,
        out_shape=[jax.ShapeDtypeStruct((model // pieces, cols), bf16)] * pieces,
        scratch_shapes=[pltpu.VMEM((model, mine * rows), bf16)] * (1 + len(pairs)),
        compiler_params=big,
        cost_estimate=costs(1 + cols // 256),
    )(table, *args)


def local(
    plane,
    tokens,
    lengths,
    offsets,
    norm_gain,
    mamba_in,
    conv_taps,
    conv_bias,
    step_bias,
    decay_log,
    skip_weight,
    mamba_gain,
    mamba_out,
    query_weight,
    key_weight,
    value_weight,
    output_weight,
    second_gain,
    gate_weight,
    up_weight,
    down_weight,
    cotangent,
):
    me = lax.axis_index("tp")
    peers = lax.axis_size(plane)
    batches, width, model = tokens.shape
    rows = batches * width
    shard = mamba_in.shape[0]
    inner = mamba_gain.shape[0]
    heads = step_bias.shape[0]
    state = (mamba_in.shape[1] - 2 * inner - heads) // 2
    q_cols = query_weight.shape[1]
    kv_heads = key_weight.shape[1] // HD
    hidden_units = gate_weight.shape[1]
    inner_t, heads_t, q_t, ff_t = inner // TP, heads // TP, q_cols // TP, hidden_units // TP
    pad = 128

    def swap(values, k, axis="tp"):
        size = lax.axis_size(axis)
        return lax.ppermute(values, axis, [(i, i ^ k) for i in range(size)])

    def spread_first(values):
        half = values.shape[1] // 2
        return swap(values[:, :half], 3), swap(values[:, half:], 1)

    def spread_second(values, far, near):
        half = values.shape[1] // 2
        pair = swap(jnp.concatenate([values[:, :half], far], axis=0), 1)
        last = swap(jnp.concatenate([values[:, half:], near], axis=0), 3)
        return values, far, pair, near, last

    def spread(values):
        return spread_second(values, *spread_first(values))

    def reduce_send(halves):
        return swap(halves[1], 1), swap(halves[3], 3)

    def reduce_add(halves, got, got_right):
        return halves[0] + got.astype(f32), halves[2] + got_right.astype(f32)

    def reduce_first(*halves):
        return reduce_add(halves, *reduce_send(halves))

    def reduce_second(pair, last):
        half = pair.shape[0] // 2
        got = swap(pair[half:].astype(bf16), 3)
        got_right = swap(last[half:].astype(bf16), 1)
        return pair[:half], got, last[:half], got_right

    def pair_finish(one, two, got_one, got_two):
        pairs = [reduce_add(one, *got_one), reduce_add(two, *got_two)]
        half = one[1].shape[0] // 2
        sends = [
            swap(jnp.concatenate([p[i][half:].astype(bf16) for p in pairs], axis=0), k)
            for i, k in ((0, 3), (1, 1))
        ]
        return [
            (p[0][:half], sends[0][i * half : (i + 1) * half], p[1][:half], sends[1][i * half : (i + 1) * half])
            for i, p in enumerate(pairs)
        ]

    def reduce(*halves):
        return reduce_second(*reduce_first(*halves))

    def everywhere(values):
        return [values] + [swap(values, k) for k in range(1, TP)]

    def absolute(parts):
        stacked = jnp.stack(parts)
        return jnp.concatenate(
            [lax.dynamic_index_in_dim(stacked, me ^ t, 0) for t in range(TP)], axis=0
        )

    cube = len(plane) == 3

    def order(values):
        lead = values.shape[:-1]
        if cube:
            split = values.reshape(lead + (TP, 2, 2, 2, shard))
            split = jnp.moveaxis(split, (-2, -4, -3, -5), (-5, -4, -3, -2))
        else:
            split = jnp.swapaxes(values.reshape(lead + (TP, peers, shard)), -3, -2)
        return split.reshape(values.shape)

    def place(n):
        group, at = divmod(n, peers)
        if cube:
            x, y, core = at // 4, at // 2 % 2, at % 2
            at = core * 4 + x * 2 + y
        return at * TP + group

    places = [place(n) for n in range(peers * TP)]

    blocks = jnp.arange(peers * TP, dtype=jnp.int32)
    in_group = blocks ^ me
    in_plane = blocks ^ (lax.axis_index(plane) * TP + me)

    def cut(weight, start, size, t):
        return lax.dynamic_slice_in_dim(weight, start + t * size, size, axis=1)

    def kv(weight, t):
        return cut(weight, 0, HD, t * kv_heads // TP)

    slot_column = jnp.concatenate([lengths[:, 0], offsets[:, 0]]).astype(bf16)[:, None]

    def in_slice(t):
        return jnp.concatenate(
            [
                cut(mamba_in, 0, inner_t, t),
                cut(mamba_in, inner, inner_t, t),
                mamba_in[:, 2 * inner : 2 * inner + 2 * state],
                cut(mamba_in, 2 * inner + 2 * state, heads_t, t),
                norm_gain[:, None],
                second_gain[:, None],
                jnp.pad(slot_column, ((0, shard - 2 * batches), (0, pad - heads_t - 3))),
                cut(query_weight, 0, q_t, t),
                kv(key_weight, t),
                kv(value_weight, t),
            ],
            axis=1,
        )

    def out_slice(t):
        return jnp.concatenate([cut(mamba_out.T, 0, inner_t, t), cut(output_weight.T, 0, q_t, t)], axis=1)

    def mlp_slice(t):
        return jnp.concatenate(
            [
                cut(gate_weight, 0, ff_t, t),
                cut(up_weight, 0, ff_t, t),
                cut(down_weight.T, 0, ff_t, t),
            ],
            axis=1,
        )

    def after(values, *earlier):
        return lax.optimization_barrier((values, earlier))[0]

    def slices(make):
        return [make(me ^ k) for k in range(TP)]

    def exchange(pieces):
        return [pieces[0]] + [swap(pieces[k], k) for k in range(1, TP)]

    def gather(parts):
        return lax.all_gather(absolute(parts).reshape(TP * shard, -1), plane, axis=0, tiled=True)

    def scatter(grads):
        return lax.psum_scatter(grads, plane, scatter_dimension=0, tiled=True)

    def pass_on(part):
        part = part.reshape(TP, shard, -1)
        return exchange([part[k] for k in range(TP)])

    conv_cols = inner_t + 2 * state
    at_q = inner_t + conv_cols + pad
    in_cols = at_q + q_t + 2 * HD

    def own(values, size):
        return lax.dynamic_slice_in_dim(values, me * size, size, axis=-1)

    taps_t = jnp.concatenate([own(conv_taps[:, :inner], inner_t), conv_taps[:, inner:]], axis=1)
    bias_t = jnp.concatenate([own(conv_bias[:inner], inner_t), conv_bias[inner:]])[None]
    steps_t = jnp.pad(
        jnp.stack([own(step_bias, heads_t), own(decay_log, heads_t)]), ((0, 0), (0, pad - heads_t))
    )
    skip_t = jnp.repeat(own(skip_weight, heads_t), inner_t // heads_t)[None]
    gain_t = own(mamba_gain, inner_t)[None]
    sizes = (inner_t, state, heads_t)

    in_slices = slices(in_slice)
    in_parts = exchange(in_slices)
    tokens, cotangent = after((tokens, cotangent), in_slices)
    source = order(tokens.reshape(rows, model))
    upstream = order(cotangent.reshape(rows, model))
    prepared = (
        source, upstream, slices(out_slice), slices(mlp_slice),
        taps_t, bias_t, steps_t, skip_t, gain_t, in_plane, in_group,
    )
    in_parts, prepared = lax.optimization_barrier((in_parts, prepared))
    source, upstream, out_slices, mlp_slices = prepared[:4]
    taps_t, bias_t, steps_t, skip_t, gain_t, in_plane, in_group = prepared[4:]
    w_in = gather(in_parts)
    source_some, upstream_some = spread_first(source), spread_first(upstream)
    column = inner_t + 2 * state + inner_t + heads_t + 2
    slots = jnp.stack([in_parts[k][: 2 * batches, column] for k in (0, 3, 1, 2)])
    slots = after(slots, source_some).astype(jnp.int32).reshape(TP, 2, batches)
    slots = jnp.swapaxes(slots, 1, 2).reshape(TP * batches, 2)
    turns = turn_table(slots[:, 1], width)
    source_all = spread_second(source, *source_some)
    out_parts = exchange(after(out_slices, (source_all, upstream_some)))
    w_out = gather(out_parts)
    mlp_slices, upstream_some = after((mlp_slices, upstream_some), out_parts[1:])
    mlp_parts = exchange(mlp_slices)
    upstream_all = spread_second(upstream, *upstream_some)

    normed, projected, y, squares, mixed, gains = mixer_inner(
        slots, after(source_all, out_parts[1:]), w_in, taps_t, bias_t, steps_t, skip_t, turns, *sizes
    )
    squares = everywhere(after(squares, upstream_all))
    w_mlp = gather(after(mlp_parts, squares[1:]))
    branches, root, *halves = mixer_outer(projected, y, mixed, gain_t, squares, w_out)
    hidden, second = row_call(hidden_kernel, slots, reduce(*halves), source, gains)

    product, *halves, mlp_sums = feed_forward(
        slots, in_group, spread(second), upstream_all, w_mlp, ff_t
    )
    mlp_sums = scatter(mlp_sums)
    d_hidden, branch_grad = row_call(
        back_hidden_kernel, slots, reduce(*halves), hidden, upstream, gains
    )

    branch_all = spread(branch_grad)
    last_halves = back_out(product, w_mlp, 2)
    branch_grad = after(branch_all, last_halves)
    branch_all, d_branches, dots = back_outer(
        branch_grad, w_out, projected, y, gain_t, slots.shape[0]
    )
    last_halves = after(last_halves, branch_grad)
    last_pair = reduce_send(last_halves)
    out_sums = weight_grads(in_group, 1, [([branch_all], [branches], 0, inner_t + q_t)])
    dots = after(everywhere(dots), (out_sums, last_pair))
    out_sums = scatter(out_sums[0])
    mlp_grads = pass_on(after(mlp_sums, dots))
    proj_grad, small = mixer_backward(
        slots, projected, taps_t, bias_t, steps_t, skip_t, turns, gain_t, y, d_branches, root,
        dots, *sizes,
    )
    in_sums = weight_grads(
        in_plane if cube else in_group,
        2 if cube else 1,
        [([after(normed, mlp_grads)], [proj_grad], 0, in_cols)],
    )
    riders = small.astype(bf16)
    out_sums, riders = after((out_sums, riders), in_sums)
    out_sums = out_sums.reshape(TP, shard, -1)
    received = [
        swap(jnp.concatenate([out_sums[k], riders], axis=0), k) for k in range(1, TP)
    ]
    norm_halves = back_out(after(proj_grad, in_sums), w_in, 0)
    norm_pair = reduce_send(norm_halves)
    if cube:
        block, half = TP * shard, TP * shard // 2
        counts = (block, block, block, half, half)
        keep, send = in_sums
        mine, along_y, along_x, across_x, across_y = by_columns(
            chip_kernel, counts, keep, after(swap(send, 1, "core"), (norm_halves, received))
        )
        across = swap(across_x, 1, "x"), swap(across_y, 1, "y")
        norm_pair, across = after((norm_pair, across), norm_pair)
        to_y, to_x = by_columns(
            along_kernel, (block, block), along_y, along_x, *across
        )
        in_parts = swap(to_x, 1, "x"), swap(to_y, 1, "y")
    norm_parts, last_parts = pair_finish(norm_halves, last_halves, norm_pair, last_pair)
    out_grads = [out_sums[0]] + [r[:shard] for r in received]
    small = absolute([small] + [r[shard:].astype(f32) for r in received])
    if cube:
        small = small + swap(small, 1, "core")
        in_parts = after(in_parts, (norm_parts, last_parts, small))
        in_sums = by_columns(plane_kernel, (shard,) * TP, mine, *in_parts)
        in_grads = exchange(in_sums)
    else:
        in_sums = scatter(in_sums[0])
        in_grads = pass_on(in_sums)
    small, mlp_grads, out_grads, norm_parts, last_parts = after(
        (small, mlp_grads, out_grads, norm_parts, last_parts), in_sums
    )
    if cube:
        small = small + swap(small, 1, "x")
        small = small + swap(small, 1, "y")
    else:
        small = lax.psum(small, plane)
    token_grads = whole_call(
        functools.partial(token_grad_kernel, places), f32, (), *norm_parts, d_hidden, source, gains
    )
    output = whole_call(
        functools.partial(output_kernel, places), bf16, (slots,), *last_parts, hidden
    )

    at_group = me[None].astype(jnp.int32)
    grad_gate, grad_up, grad_down, grad_second_gain = unpack(
        functools.partial(unpack_mlp_kernel, ff_t),
        at_group,
        mlp_grads,
        (gate_weight, up_weight, second_gain[:, None]),
        (hidden_units, hidden_units, hidden_units, 1),
    )
    grad_mamba_out, grad_output = unpack(
        functools.partial(unpack_out_kernel, inner_t, q_t), at_group, out_grads, (), (inner, q_cols)
    )
    in_grads = after(in_grads, (small, token_grads, output, grad_down, grad_output))
    grad_mamba_in, grad_query, grad_key, grad_value, grad_norm_gain = unpack(
        functools.partial(unpack_in_kernel, *sizes, pad),
        at_group,
        in_grads,
        (mamba_in, query_weight, key_weight, value_weight, norm_gain[:, None]),
        (mamba_in.shape[1], q_cols, kv_heads * HD, kv_heads * HD, 1),
    )
    grad_mamba_out, grad_output, grad_down = grad_mamba_out.T, grad_output.T, grad_down.T
    grad_norm_gain, grad_second_gain = grad_norm_gain[:, 0], grad_second_gain[:, 0]

    kernel = conv_taps.shape[0]
    small = small.reshape(TP, -1, 8, small.shape[-1])
    small = jnp.concatenate([small[:, i] for i in range(small.shape[1])], axis=-1)
    conv = small[:, : kernel + 1, :conv_cols]
    conv = jnp.concatenate(
        [conv[:, :, :inner_t].transpose(1, 0, 2).reshape(kernel + 1, inner), conv[:, :, inner_t:].sum(0)],
        axis=1,
    )
    by_inner = small[:, :2, conv_cols : conv_cols + inner_t]
    by_step = small[:, :2, conv_cols + inner_t : conv_cols + inner_t + heads_t]
    return (
        output.reshape(tokens.shape),
        token_grads.reshape(tokens.shape),
        grad_norm_gain,
        grad_mamba_in,
        conv[:kernel],
        conv[kernel],
        by_step[:, 0].reshape(-1),
        by_step[:, 1].reshape(-1),
        by_inner[:, 1].reshape(heads, -1).sum(1),
        by_inner[:, 0].reshape(-1),
        grad_mamba_out,
        grad_query,
        grad_key,
        grad_value,
        grad_output,
        grad_second_gain,
        grad_gate,
        grad_up,
        grad_down,
    )


def solution(mesh):
    count = mesh.devices.size
    if tuple(mesh.devices.shape) == (8, 4):
        grid = Mesh(mesh.devices.reshape(TP, 2, 2, 2), ("tp", "x", "y", "core"))
        plane = ("core", "x", "y")
    else:
        grid = Mesh(mesh.devices.reshape(TP, count // TP), ("tp", "fs"))
        plane = ("fs",)
    every = grid.axis_names
    down, across, slots = P(every, None), P(None, every), P(None, every, None)
    line, copied = P(every), P()
    return jax.shard_map(
        functools.partial(local, plane),
        mesh=grid,
        in_specs=(
            slots, across, across, line, down, copied, copied, copied, copied, copied, copied,
            across, down, down, down, across, line, down, down, across, slots,
        ),
        out_specs=(
            slots, slots, line, down, copied, copied, copied, copied, copied, copied,
            across, down, down, down, across, line, down, down, across,
        ),
        check_vma=False,
    )
```

```python
import functools
import math

import jax
import jax.numpy as jnp
from jax import lax
from jax.experimental import pallas as pl
from jax.experimental.pallas import tpu as pltpu
from jax.sharding import Mesh
from jax.sharding import PartitionSpec as P

HD = 128
TP = 4
PAD = 128

epsilon = 1e-05
rope_base = 100000000000.0
highest = lax.Precision.HIGHEST
f32 = jnp.float32
bf16 = jnp.bfloat16


def inverse_root(values):
    return lax.rsqrt(jnp.mean(values * values, axis=-1, keepdims=True) + epsilon)


def norm_back(values, root, grad):
    return root * grad - values * root**3 * jnp.mean(values * grad, axis=-1, keepdims=True)


def dot_nn(left, right):
    return jnp.dot(left, right, preferred_element_type=f32)


def dot_nt(left, right):
    return lax.dot_general(left, right, (((1,), (1,)), ((), ())), preferred_element_type=f32)


def inside_rows(length, offset, width):
    rows = jnp.arange(width, dtype=jnp.int32)[:, None]
    return ((rows >= offset) & (rows < offset + length)).astype(f32)


def turn_table(offsets, width):
    half = HD // 2
    freqs = rope_base ** (-jnp.arange(half, dtype=f32) * 2.0 / HD)
    rows = jnp.arange(width, dtype=jnp.int32)
    positions = (rows[None, :] - offsets[:, None]).astype(f32)
    angles = positions.reshape(-1, 1) * freqs
    cosine, sine = jnp.cos(angles), jnp.sin(angles)
    return jnp.concatenate([cosine, cosine, -sine, sine], axis=1)


def mm(left, right, dims, precision=lax.Precision.HIGH):
    return lax.dot_general(left, right, (dims, ((), ())), precision=precision, preferred_element_type=f32)


NN = ((1,), (0,))
NT = ((1,), (1,))
TN = ((0,), (0,))


def iota(shape, axis):
    return lax.broadcasted_iota(jnp.int32, shape, axis)


def down_rows(values, count):
    if count == 0:
        return values
    return jnp.where(iota(values.shape, 0) >= count, pltpu.roll(values, count, axis=0), 0.0)


def up_rows(values, count):
    if count == 0:
        return values
    length = values.shape[0]
    return jnp.where(
        iota(values.shape, 0) < length - count, pltpu.roll(values, length - count, axis=0), 0.0
    )


def head_sums(values, spread):
    return mm(values, spread, NT)


def parameters(ref, inner):
    values = ref[...]
    last = values.shape[0] - 1
    steps = jnp.concatenate([values[last:, :PAD], values[last:, PAD : 2 * PAD]], axis=0)
    return (
        values[: last - 3], values[last - 3 : last - 2], steps,
        values[last - 2 : last - 1, :inner], values[last - 1 : last, :inner],
    )


def mamba_shared(proj, start, count, taps_ref, bias_ref, steps_ref, inner, state, heads):
    length = proj.shape[0]
    conv_cols = inner + 2 * state
    row = iota((length, 1), 0)
    inside = ((row >= start) & (row < start + count)).astype(f32)
    conv_in = proj[:, inner : inner + conv_cols] * inside
    kernel = taps_ref.shape[0]
    conv = bias_ref[...] + jnp.zeros_like(conv_in)
    for tap in range(kernel):
        conv = conv + taps_ref[tap : tap + 1, :] * down_rows(conv_in, kernel - 1 - tap)
    sig = jax.nn.sigmoid(conv)
    active = conv * sig
    pad = steps_ref.shape[1]
    lane = iota((length, pad), 1)
    raw = jnp.where(lane < heads, proj[:, inner + conv_cols : inner + conv_cols + pad] + steps_ref[0:1, :], 0.0)
    step = jnp.where(lane < heads, jnp.maximum(raw, 0.0) + jnp.log1p(jnp.exp(-jnp.abs(raw))), 0.0)
    rate = -jnp.exp(steps_ref[1:2, :])
    lower = (iota((length, length), 0) >= iota((length, length), 1)).astype(f32)
    cum = mm(lower, step * rate, NN, highest)
    size = inner // heads
    spread = (iota((pad, inner), 0) == iota((pad, inner), 1) // size).astype(f32)
    step_x = mm(step, spread, NN)
    cum_x = mm(cum, spread, NN, highest)
    at = iota((length, inner), 1) % length
    diagonal = iota((length, inner), 0) == at
    cum_row = jnp.sum(jnp.where(diagonal, cum_x, 0.0), axis=0, keepdims=True)
    allowed = (
        (at <= iota((length, inner), 0)) & (inside > 0.0) & (at >= start) & (at < start + count)
    )
    decay = jnp.where(allowed, jnp.exp(jnp.where(allowed, cum_x - cum_row, 0.0)), 0.0)
    xs = active[:, :inner]
    b_state = active[:, inner : inner + state]
    c_state = active[:, inner + state :]
    inter = mm(c_state, b_state, NT)
    pair = jnp.concatenate([inter, inter], axis=1)
    mixing = decay * jnp.concatenate([pair] * (inner // pair.shape[1]), axis=1)
    return dict(
        inside=inside, conv_in=conv_in, conv=conv, sig=sig, raw=raw, step=step, rate=rate,
        spread=spread, step_x=step_x, diagonal=diagonal, decay=decay, mixing=mixing, xs=xs,
        b_state=b_state, c_state=c_state, lower=lower, lane=lane,
    )


def two_blocks(values):
    left = iota(values.shape, 1) < values.shape[1] // 2
    return jnp.concatenate([jnp.where(left, values, 0.0), jnp.where(left, 0.0, values)], axis=0)


def turn(values, cosine, sine):
    return values * cosine + pltpu.roll(values, HD // 2, axis=1) * sine


def attention_shared(proj, at, start, count, cosine, sine):
    length = proj.shape[0]
    kv = proj.shape[1] - 2 * HD
    queries = jnp.concatenate(
        [turn(proj[:, c : c + HD], cosine, sine) for c in range(at, kv, HD)], axis=0
    )
    keys = turn(proj[:, kv : kv + HD], cosine, sine)
    values = proj[:, kv + HD :]
    scores = mm(queries, keys, NT) * (1.0 / math.sqrt(HD))
    row = iota(scores.shape, 0) % length
    col = iota(scores.shape, 1)
    end = start + count
    allowed = ((row >= start) & (row < end) & (col >= start) & (col <= row)) | (row == col)
    scores = jnp.where(allowed, scores, -1e30)
    probs = jnp.exp(scores - jnp.max(scores, axis=1, keepdims=True))
    probs = probs / jnp.sum(probs, axis=1, keepdims=True)
    return queries, keys, values, probs


def specs(*shapes):
    return [pl.BlockSpec(s, lambda i: (0, 0)) for s in shapes]


def rows_spec(length, cols):
    return pl.BlockSpec((length, cols), lambda i: (i, 0))


def their_spec(length, each, k):
    return pl.BlockSpec((1, 1, length), lambda i: (i ^ (THEIRS[k][0] * each), 0, 0))


big = pltpu.CompilerParams(vmem_limit_bytes=50 * 1024 * 1024)


def costs(microseconds):
    return pl.CostEstimate(
        flops=microseconds * 10**9, bytes_accessed=microseconds * 10**5, transcendentals=0
    )


def inside_of(slots_ref, seq, length):
    row = iota((length, 1), 0)
    start = slots_ref[seq, 1]
    return ((row >= start) & (row < start + slots_ref[seq, 0])).astype(f32)


def as_row(column):
    length = column.shape[0]
    same = iota((length, length), 0) == iota((length, length), 1)
    return jnp.sum(jnp.where(same, column, 0.0), axis=0, keepdims=True)


def as_column(row):
    length = row.shape[1]
    same = iota((length, length), 0) == iota((length, length), 1)
    return jnp.sum(jnp.where(same, row, 0.0), axis=1, keepdims=True)


THEIRS = ((0, 1, 2, 3), (2, 3, 0, 1), (3, 2, 1, 0), (1, 0, 3, 2))


def group_total(refs, seq):
    each = refs[0].shape[0] // TP
    return sum(ref[THEIRS[k][seq // each] * each + seq % each] for k, ref in enumerate(refs))


def joined_rows(refs):
    own, far, pair, near, last = refs
    half = far.shape[1]
    count = own.shape[0]
    left = jnp.concatenate([own[:, :half], far[...], pair[...]], axis=0)
    right = jnp.concatenate([own[:, half:], last[:count, :], near[...], last[count:, :]], axis=0)
    return jnp.concatenate([left, right], axis=1)


def put_left(values, refs):
    half = values.shape[0] // 2
    refs[0][...] = values[:half]
    refs[1][...] = values[half:].astype(bf16)


def put_right(values, refs):
    one = values.shape[0] // TP
    refs[2][:one, :] = values[:one]
    refs[2][one:, :] = values[2 * one : 3 * one]
    refs[3][:one, :] = values[one : 2 * one].astype(bf16)
    refs[3][one:, :] = values[3 * one :].astype(bf16)


def put_tiles(values, refs):
    step = pl.program_id(0)
    middle = pl.num_programs(0) // 2

    @pl.when(step < middle)
    def _():
        put_left(values, refs)

    @pl.when(step >= middle)
    def _():
        put_right(values, refs)


def halves_out(rows, model, tile):
    middle = model // tile // 2
    left = pl.BlockSpec((rows // 2, tile), lambda j: (0, jnp.minimum(j, middle - 1)))
    right = pl.BlockSpec((rows // 2, tile), lambda j: (0, jnp.maximum(j - middle, 0)))
    shapes = [jax.ShapeDtypeStruct((rows // 2, model // 2), t) for t in (f32, bf16, f32, bf16)]
    return [left, left, right, right], shapes


def both_halves(refs):
    kept, got, kept_right, got_right = refs
    return jnp.concatenate(
        [kept[...] + got[...].astype(f32), kept_right[...] + got_right[...].astype(f32)], axis=1
    )


def inner_kernel(
    inner, state, heads, tiles, slots_ref, p0, p1, p2, p3, p4, weight_ref, gains_in_ref, params_ref,
    turn_ref, normed_ref, proj_ref, y_ref, square_ref, mixed_ref, gains_ref,
):
    step = pl.program_id(0)
    tile = weight_ref.shape[1]

    @pl.when(step == 0)
    def _():
        rows = joined_rows((p0, p1, p2, p3, p4)).astype(f32)
        turned = jnp.transpose(gains_in_ref[...].astype(f32))
        gains_ref[0:1, :] = turned[heads : heads + 1]
        gains_ref[1:2, :] = turned[heads + 1 : heads + 2]
        normed_ref[...] = (rows * inverse_root(rows) * turned[heads : heads + 1]).astype(bf16)

    @pl.when(step < tiles)
    def _():
        at = pl.multiple_of(step * tile, tile)
        proj_ref[:, pl.ds(at, tile)] = jnp.dot(
            normed_ref[...], weight_ref[...], preferred_element_type=f32
        )

    @pl.when(step >= tiles)
    def _():
        seq = step - tiles
        length = y_ref.shape[0]
        proj = proj_ref[pl.ds(pl.multiple_of(seq * length, length), length), :]
        start = slots_ref[seq, 1]
        count = slots_ref[seq, 0]
        taps, bias, steps, skip, _ = parameters(params_ref, inner)
        m = mamba_shared(proj, start, count, taps, bias, steps, inner, state, heads)
        scaled = m["xs"] * m["step_x"]
        wide = 2 * length
        parts = [
            mm(m["mixing"][:, c : c + wide], two_blocks(scaled[:, c : c + wide]), NN)
            for c in range(0, inner, wide)
        ]
        y = jnp.concatenate(parts, axis=1) + skip * m["xs"]
        y_ref[...] = y
        gate = proj[:, :inner]
        gated = y * gate * jax.nn.sigmoid(gate)
        square_ref[0] = as_row(jnp.sum(gated * gated, axis=1, keepdims=True))
        at = 2 * inner + 2 * state + PAD
        _, _, values, probs = attention_shared(
            proj, at, start, count, turn_ref[:, :HD], turn_ref[:, HD:]
        )
        mixed = mm(probs, values, NN)
        mixed_ref[...] = jnp.concatenate(
            [mixed[r : r + length] for r in range(0, mixed.shape[0], length)], axis=1
        ).astype(mixed_ref.dtype)


def mixer_inner(slots, rows, weight, params, turns, inner, state, heads, tile=384):
    model, cols = weight.shape
    seqs = slots.shape[0]
    pieces = rows
    rows = TP * pieces[0].shape[0]
    length = rows // seqs
    tiles = cols // tile
    pad = PAD
    at_steps = (2 * inner + 2 * state) // pad
    q_cols = cols - 2 * inner - 2 * state - pad - 2 * HD

    def seq_spec(*shape):
        zeros = (0,) * (len(shape) - 1)
        return pl.BlockSpec(shape, lambda j: (jnp.maximum(j - tiles, 0),) + zeros)

    return pl.pallas_call(
        functools.partial(inner_kernel, inner, state, heads, tiles),
        grid=(tiles + seqs,),
        in_specs=[pl.BlockSpec(memory_space=pltpu.SMEM)]
        + specs(*[p.shape for p in pieces])
        + [
            pl.BlockSpec((model, tile), lambda j: (0, jnp.minimum(j, tiles - 1))),
            pl.BlockSpec((model, pad), lambda j: (0, at_steps)),
        ]
        + specs(params.shape)
        + [seq_spec(length, turns.shape[1])],
        out_specs=specs((rows, model), (rows, cols))
        + [seq_spec(length, inner), seq_spec(1, 1, length), seq_spec(length, q_cols)]
        + specs((8, model)),
        out_shape=[
            jax.ShapeDtypeStruct((rows, model), bf16),
            jax.ShapeDtypeStruct((rows, cols), f32),
            jax.ShapeDtypeStruct((rows, inner), f32),
            jax.ShapeDtypeStruct((seqs, 1, length), f32),
            jax.ShapeDtypeStruct((rows, q_cols), bf16),
            jax.ShapeDtypeStruct((8, model), f32),
        ],
        compiler_params=big,
        cost_estimate=costs(18),
    )(slots, *pieces, weight, weight, params, turns)


def outer_kernel(inner, gate_ref, y_ref, mixed_ref, gain_ref, s0, s1, s2, s3, weight_ref, branches_ref, root_ref, *halves):
    @pl.when(pl.program_id(0) == 0)
    def _():
        length = root_ref.shape[2]
        for seq in range(root_ref.shape[0]):
            rows = slice(seq * length, (seq + 1) * length)
            root = lax.rsqrt(group_total((s0, s1, s2, s3), seq) / (TP * inner) + epsilon)
            root_ref[seq] = root
            gate = gate_ref[rows, :]
            gated = y_ref[rows, :] * gate * jax.nn.sigmoid(gate)
            branches_ref[rows, :inner] = (gated * as_column(root) * gain_ref[...]).astype(bf16)
        branches_ref[:, inner:] = mixed_ref[...]

    put_tiles(dot_nt(branches_ref[...], weight_ref[...]), halves)


def mixer_outer(proj, y, mixed, gain, squares, weight, tile=512):
    rows, inner = y.shape
    model, cols = weight.shape
    half_specs, half_shapes = halves_out(rows, model, tile)
    return pl.pallas_call(
        functools.partial(outer_kernel, inner),
        grid=(model // tile,),
        in_specs=specs((rows, inner), y.shape, mixed.shape, gain.shape)
        + [pl.BlockSpec(squares[0].shape, lambda j: (0, 0, 0))] * TP
        + [pl.BlockSpec((tile, cols), lambda j: (j, 0))],
        out_specs=specs((rows, cols))
        + [pl.BlockSpec(squares[0].shape, lambda j: (0, 0, 0))]
        + half_specs,
        out_shape=[
            jax.ShapeDtypeStruct((rows, cols), bf16),
            jax.ShapeDtypeStruct(squares[0].shape, f32),
        ]
        + half_shapes,
        compiler_params=big,
        cost_estimate=costs(4),
    )(proj, y, mixed, gain, *squares, weight)


def back_out_kernel(left_ref, weight_ref, *halves):
    put_tiles(dot_nt(left_ref[...], weight_ref[...]), halves)


def back_out(left, weight, column, tile=512):
    rows, cols = left.shape
    model = weight.shape[0]
    half_specs, half_shapes = halves_out(rows, model, tile)
    return pl.pallas_call(
        back_out_kernel,
        grid=(model // tile,),
        in_specs=specs(left.shape) + [pl.BlockSpec((tile, cols), lambda j: (j, column))],
        out_specs=half_specs,
        out_shape=half_shapes,
        compiler_params=big,
        cost_estimate=costs(4),
    )(left, weight)


def inside_all(slots_ref, seqs, length):
    return jnp.concatenate([inside_of(slots_ref, seq, length) for seq in range(seqs)], axis=0)


def hidden_kernel(slots_ref, k0, k1, k2, k3, source_ref, gains_ref, hidden_ref, second_ref):
    length = source_ref.shape[0] * TP // slots_ref.shape[0]
    inside = inside_all(slots_ref, slots_ref.shape[0] // TP, length)
    hidden = source_ref[...].astype(f32) + inside * both_halves((k0, k1, k2, k3))
    hidden_ref[...] = hidden
    second_ref[...] = (hidden * inverse_root(hidden) * gains_ref[1:2, :]).astype(bf16)


def row_call(kernel, slots, halves, *others):
    shape = others[0].shape
    return pl.pallas_call(
        kernel,
        grid=(1,),
        in_specs=[pl.BlockSpec(memory_space=pltpu.SMEM)]
        + specs(*[h.shape for h in halves], *[o.shape for o in others]),
        out_specs=specs(shape, shape),
        out_shape=[jax.ShapeDtypeStruct(shape, f32), jax.ShapeDtypeStruct(shape, bf16)],
        compiler_params=big,
        cost_estimate=costs(2),
    )(slots, *halves, *others)


def feed_kernel(
    steps, blocks, slots_ref, table_ref, s0, s1, s2, s3, s4, c0, c1, c2, c3, c4, gate_ref, up_ref, down_ref,
    product_ref, h0, h1, h2, h3, grads_ref,
    second_ref, down_grad_ref, gate_grad_ref, up_grad_ref, total, second_turned, down_turned,
):
    step = pl.program_id(0)
    tile = gate_ref.shape[1]

    @pl.when(step == 0)
    def _():
        second_ref[...] = joined_rows((s0, s1, s2, s3, s4))
        seqs = slots_ref.shape[0]
        inside = inside_all(slots_ref, seqs, TP * s0.shape[0] // seqs)
        down_grad_ref[...] = (inside * joined_rows((c0, c1, c2, c3, c4)).astype(f32)).astype(bf16)
        total[...] = jnp.zeros_like(total)

    @pl.when(step < steps)
    def _():
        second = second_ref[...]
        gate = jnp.dot(second, gate_ref[...], preferred_element_type=f32)
        up = jnp.dot(second, up_ref[...], preferred_element_type=f32)
        d_product = jnp.dot(down_grad_ref[...], down_ref[...], preferred_element_type=f32)
        sig = jax.nn.sigmoid(gate)
        swish = gate * sig
        gate_grad = (d_product * up * sig * (1.0 + gate * (1.0 - sig))).astype(bf16)
        up_grad = (d_product * swish).astype(bf16)
        at = pl.ds(pl.multiple_of(step * tile, tile), tile)
        product_ref[:, at] = (swish * up).astype(bf16)
        gate_grad_ref[:, at] = gate_grad
        up_grad_ref[:, at] = up_grad
        total[...] += dot_nt(gate_grad, gate_ref[...]) + dot_nt(up_grad, up_ref[...])

    @pl.when(step == steps - 1)
    def _():
        middle = total.shape[1] // 2
        put_left(total[:, :middle], (h0, h1))
        put_right(total[:, middle:], (h0, h1, h2, h3))
        size = second_ref.shape[1] // blocks
        for source, turned in ((second_ref, second_turned), (down_grad_ref, down_turned)):
            plain = jnp.transpose(source[...])
            total_rows = plain.shape[0]
            grads_ref[:total_rows, : plain.shape[1]] = plain
            for block in range(blocks):
                start = pl.multiple_of(table_ref[block] * size, size)
                turned[block * size : (block + 1) * size, :] = grads_ref[pl.ds(start, size), : plain.shape[1]]

    for part, (turned, right) in enumerate(
        ((second_turned, gate_grad_ref), (second_turned, up_grad_ref), (down_turned, product_ref))
    ):

        @pl.when((step >= (part + 1) * steps) & (step < (part + 2) * steps))
        def _(part=part, turned=turned, right=right):
            at = pl.multiple_of((step - (part + 1) * steps) * tile, tile)
            grads_ref[...] = jnp.dot(
                turned[...], right[:, pl.ds(at, tile)], preferred_element_type=f32
            ).astype(bf16)


def feed_forward(slots, table, second, cotangent, weight, units, tile=512):
    count, model = second[0].shape
    rows = TP * count
    steps = units // tile
    half_shapes = halves_out(rows, model, tile)[1]
    shapes = [p.shape for p in second]
    return pl.pallas_call(
        functools.partial(feed_kernel, steps, table.shape[0]),
        grid=(4 * steps,),
        in_specs=[pl.BlockSpec(memory_space=pltpu.SMEM)] * 2
        + specs(*shapes, *shapes)
        + [
            pl.BlockSpec((model, tile), lambda j, at=at: (0, at * steps + jnp.minimum(j, steps - 1)))
            for at in range(3)
        ],
        out_specs=specs((rows, units), *[h.shape for h in half_shapes])
        + [pl.BlockSpec((model, tile), lambda j: (0, jnp.maximum(j - steps, 0)))],
        out_shape=[jax.ShapeDtypeStruct((rows, units), bf16)]
        + half_shapes
        + [jax.ShapeDtypeStruct((model, 3 * units), bf16)],
        scratch_shapes=[pltpu.VMEM((rows, model), bf16)] * 2
        + [pltpu.VMEM((rows, units), bf16)] * 2
        + [pltpu.VMEM((rows, model), f32)]
        + [pltpu.VMEM((model, rows), bf16)] * 2,
        compiler_params=big,
        cost_estimate=costs(30),
    )(slots, table, *second, *cotangent, weight, weight, weight)


def in_places(values, places):
    size = values.shape[1] // len(places)
    return jnp.concatenate([values[:, p * size : (p + 1) * size] for p in places], axis=1)


def output_kernel(places, slots_ref, k0, k1, k2, k3, hidden_ref, output_ref):
    seqs = slots_ref.shape[0]
    inside = inside_all(slots_ref, seqs // TP, hidden_ref.shape[0] * TP // seqs)
    output = (hidden_ref[...] + inside * both_halves((k0, k1, k2, k3))).astype(bf16)
    output_ref[...] = in_places(output, places)


def token_grad_kernel(places, k0, k1, k2, k3, hidden_ref, source_ref, gains_ref, grad_ref):
    grad = both_halves((k0, k1, k2, k3)) * gains_ref[0:1, :]
    source = source_ref[...].astype(f32)
    total = hidden_ref[...] + norm_back(source, inverse_root(source), grad)
    grad_ref[...] = in_places(total, places)


def whole_call(kernel, dtype, scalars, *arrays):
    shape = arrays[4].shape
    return pl.pallas_call(
        kernel,
        grid=(1,),
        in_specs=[pl.BlockSpec(memory_space=pltpu.SMEM)] * len(scalars) + specs(*[a.shape for a in arrays]),
        out_specs=pl.BlockSpec(shape, lambda i: (0, 0)),
        out_shape=jax.ShapeDtypeStruct(shape, dtype),
        compiler_params=big,
        cost_estimate=costs(3),
    )(*scalars, *arrays)


def back_hidden_kernel(slots_ref, k0, k1, k2, k3, hidden_ref, cotangent_ref, gains_ref, d_hidden_ref, branch_ref):
    grad = both_halves((k0, k1, k2, k3)) * gains_ref[1:2, :]
    hidden = hidden_ref[...]
    d_hidden = cotangent_ref[...].astype(f32) + norm_back(hidden, inverse_root(hidden), grad)
    d_hidden_ref[...] = d_hidden
    seqs = slots_ref.shape[0]
    inside = inside_all(slots_ref, seqs // TP, hidden.shape[0] * TP // seqs)
    branch_ref[...] = (inside * d_hidden).astype(bf16)


def back_outer_kernel(tiles, b0, b1, b2, b3, b4, weight_ref, gate_ref, y_ref, gain_ref, branch_ref, grad_ref, dots_ref, total):
    step = pl.program_id(0)

    @pl.when(step == 0)
    def _():
        branch_ref[...] = joined_rows((b0, b1, b2, b3, b4))
        total[...] = jnp.zeros_like(total)

    grad = jnp.dot(branch_ref[...], weight_ref[...], preferred_element_type=f32)
    grad_ref[...] = grad

    @pl.when(step < tiles)
    def _():
        gate = gate_ref[...]
        gated = y_ref[...] * gate * jax.nn.sigmoid(gate)
        total[...] += jnp.sum(gated * gain_ref[...] * grad, axis=1, keepdims=True)

    @pl.when(step == pl.num_programs(0) - 1)
    def _():
        length = dots_ref.shape[2]
        for seq in range(dots_ref.shape[0]):
            dots_ref[seq] = as_row(total[seq * length : (seq + 1) * length, :])


def back_outer(branch, weight, proj, y, gain, seqs, tile=256):
    model = weight.shape[0]
    rows, inner = y.shape
    cols = weight.shape[1]
    tiles = inner // tile
    length = rows // seqs
    inner_spec = pl.BlockSpec((rows, tile), lambda j: (0, jnp.minimum(j, tiles - 1)))
    return pl.pallas_call(
        functools.partial(back_outer_kernel, tiles),
        grid=(cols // tile,),
        in_specs=specs(*[p.shape for p in branch])
        + [
            pl.BlockSpec((model, tile), lambda j: (0, j)),
            inner_spec,
            inner_spec,
            pl.BlockSpec((1, tile), lambda j: (0, jnp.minimum(j, tiles - 1))),
        ],
        out_specs=specs((rows, model))
        + [
            pl.BlockSpec((rows, tile), lambda j: (0, j)),
            pl.BlockSpec((seqs, 1, length), lambda j: (0, 0, 0)),
        ],
        out_shape=[
            jax.ShapeDtypeStruct((rows, model), bf16),
            jax.ShapeDtypeStruct((rows, cols), f32),
            jax.ShapeDtypeStruct((seqs, 1, length), f32),
        ],
        scratch_shapes=[pltpu.VMEM((rows, 1), f32)],
        compiler_params=big,
        cost_estimate=costs(5),
    )(*branch, weight, proj, y, gain)


def backward_kernel(
    inner, state, heads, slots_ref, proj_ref, params_ref, turn_ref, y_ref, grad_ref, root_ref, d0, d1, d2, d3, proj_grad_ref, small_ref,
):
    step_id = pl.program_id(0)
    start = slots_ref[step_id, 1]
    count = slots_ref[step_id, 0]
    proj = proj_ref[...]
    length = proj.shape[0]
    conv_cols = inner + 2 * state
    pad = PAD
    taps, bias, steps, skip, gain = parameters(params_ref, inner)
    m = mamba_shared(proj, start, count, taps, bias, steps, inner, state, heads)
    xs, decay, mixing = m["xs"], m["decay"], m["mixing"]
    scaled = xs * m["step_x"]
    gate = proj[:, :inner]
    gate_sig = jax.nn.sigmoid(gate)
    y = y_ref[...]
    root = as_column(root_ref[0])
    mean = as_column(sum(ref[0] for ref in (d0, d1, d2, d3))) / (TP * inner)
    gated = y * gate * gate_sig
    d_norm = grad_ref[:, :inner]
    d_gated = root * (d_norm * gain) - gated * (root * root * root * mean)
    dy = d_gated * gate * gate_sig
    d_gate = d_gated * y * gate_sig * (1.0 + gate * (1.0 - gate_sig))
    wide = 2 * length
    back, d_mix = [], []
    for c in range(0, inner, wide):
        dy_pair = dy[:, c : c + wide]
        full = mm(mixing[:, c : c + wide], dy_pair, TN)
        left = iota((length, wide), 1) < length
        back.append(jnp.where(left, full[:length], full[length:]))
        d_mix.append(mm(dy_pair, two_blocks(scaled[:, c : c + wide]), NT))
    back = jnp.concatenate(back, axis=1)
    d_mix = jnp.concatenate(d_mix, axis=1)
    d_xs = skip * dy + m["step_x"] * back
    flow = d_mix * mixing
    flow = flow - jnp.where(m["diagonal"], jnp.sum(flow, axis=0, keepdims=True), 0.0)
    d_cum = head_sums(flow, m["spread"])
    d_rate = mm(m["lower"], d_cum, TN, highest)
    d_step = head_sums(xs * back, m["spread"]) + d_rate * m["rate"]
    d_raw = jnp.where(m["lane"] < heads, d_step * jax.nn.sigmoid(m["raw"]), 0.0)
    d_inter = d_mix * decay
    pair = d_inter[:, :wide]
    for c in range(wide, inner, wide):
        pair = pair + d_inter[:, c : c + wide]
    d_inter = pair[:, :length] + pair[:, length:]
    d_b = mm(d_inter, m["c_state"], TN)
    d_c = mm(d_inter, m["b_state"], NN)
    d_active = jnp.concatenate([d_xs, d_b, d_c], axis=1)
    sig, conv = m["sig"], m["conv"]
    d_conv = d_active * sig * (1.0 + conv * (1.0 - sig))
    kernel = taps.shape[0]
    d_in = jnp.zeros_like(d_conv)
    conv_rows = []
    for tap in range(kernel):
        back_by = kernel - 1 - tap
        d_in = d_in + taps[tap : tap + 1, :] * up_rows(d_conv, back_by)
        conv_rows.append(jnp.sum(d_conv * down_rows(m["conv_in"], back_by), axis=0, keepdims=True))
    conv_rows.append(jnp.sum(d_conv, axis=0, keepdims=True))
    conv_rows.append(jnp.zeros((8 - kernel - 1, conv_cols), f32))
    conv_rows = jnp.concatenate(conv_rows, axis=0)
    inner_rows = jnp.concatenate(
        [
            jnp.sum(gated * root * d_norm, axis=0, keepdims=True),
            jnp.sum(dy * xs, axis=0, keepdims=True),
            jnp.zeros((6, inner), f32),
        ],
        axis=0,
    )
    step_rows = jnp.concatenate(
        [
            jnp.sum(d_raw, axis=0, keepdims=True),
            jnp.sum(d_rate * m["step"] * m["rate"], axis=0, keepdims=True),
            jnp.zeros((6, pad), f32),
        ],
        axis=0,
    )

    rows = jnp.concatenate([conv_rows, inner_rows, step_rows], axis=1)
    wide = small_ref.shape[1]
    rows = jnp.concatenate(
        [rows, jnp.zeros((8, small_ref.shape[0] // 8 * wide - rows.shape[1]), f32)], axis=1
    )
    rows = jnp.concatenate([rows[:, c : c + wide] for c in range(0, rows.shape[1], wide)], axis=0)

    @pl.when(step_id == 0)
    def _():
        small_ref[...] = jnp.zeros_like(small_ref)

    small_ref[...] += rows

    at = inner + conv_cols + pad
    cosine, sine = turn_ref[:, :HD], turn_ref[:, HD:]
    queries, keys, values, probs = attention_shared(proj, at, start, count, cosine, sine)
    d_out = jnp.concatenate(
        [grad_ref[:, c : c + HD] for c in range(inner, grad_ref.shape[1], HD)], axis=0
    )
    d_values = mm(probs, d_out, TN)
    d_probs = mm(d_out, values, NT)
    d_scores = probs * (d_probs - jnp.sum(probs * d_probs, axis=1, keepdims=True)) * (1.0 / math.sqrt(HD))
    d_queries = mm(d_scores, keys, NN)
    d_keys = mm(d_scores, queries, TN)
    outs = [d_gate, d_in * m["inside"], d_raw]
    outs += [turn(d_queries[r : r + length], cosine, -sine) for r in range(0, d_queries.shape[0], length)]
    outs += [turn(d_keys, cosine, -sine), d_values]
    proj_grad_ref[...] = jnp.concatenate(outs, axis=1).astype(proj_grad_ref.dtype)


def mixer_backward(
    slots, proj, params, turns, y, grads, root, dots, inner, state, heads
):
    seqs = slots.shape[0]
    rows, cols = proj.shape
    length = rows // seqs
    conv_cols = inner + 2 * state
    pad = PAD
    small_shape = (8 * pl.cdiv(conv_cols + inner + pad, grads.shape[1]), grads.shape[1])
    return pl.pallas_call(
        functools.partial(backward_kernel, inner, state, heads),
        grid=(seqs,),
        in_specs=[pl.BlockSpec(memory_space=pltpu.SMEM), rows_spec(length, cols)]
        + specs(params.shape)
        + [rows_spec(length, turns.shape[1])]
        + [rows_spec(length, inner), rows_spec(length, grads.shape[1])]
        + [pl.BlockSpec((1, 1, length), lambda i: (i, 0, 0))]
        + [their_spec(length, seqs // TP, k) for k in range(TP)],
        out_specs=[rows_spec(length, cols)] + specs(small_shape),
        out_shape=[
            jax.ShapeDtypeStruct((rows, cols), bf16),
            jax.ShapeDtypeStruct(small_shape, f32),
        ],
        compiler_params=big,
        cost_estimate=costs(17),
    )(slots, proj, params, turns, y, grads, root, *dots)


def chip_kernel(keep_ref, got_ref, mine_ref, along_y_ref, along_x_ref, across_x_ref, across_y_ref):
    total = (keep_ref[...].astype(f32) + got_ref[...].astype(f32)).astype(bf16)
    block = mine_ref.shape[0]
    half = across_x_ref.shape[0]
    mine_ref[...] = total[:block]
    along_y_ref[...] = total[block : 2 * block]
    along_x_ref[...] = total[2 * block : 3 * block]
    across_x_ref[...] = total[3 * block : 3 * block + half]
    across_y_ref[...] = total[3 * block + half :]


def along_kernel(along_y_ref, along_x_ref, by_x_ref, by_y_ref, to_y_ref, to_x_ref):
    half = by_x_ref.shape[0]
    to_y_ref[...] = along_y_ref[...]
    to_y_ref[:half, :] = (along_y_ref[:half, :].astype(f32) + by_x_ref[...].astype(f32)).astype(bf16)
    to_x_ref[...] = along_x_ref[...]
    to_x_ref[half:, :] = (along_x_ref[half:, :].astype(f32) + by_y_ref[...].astype(f32)).astype(bf16)


def plane_kernel(mine_ref, by_x_ref, by_y_ref, *outs):
    total = mine_ref[...].astype(f32) + by_x_ref[...].astype(f32) + by_y_ref[...].astype(f32)
    size = outs[0].shape[0]
    for k, out in enumerate(outs):
        out[...] = total[k * size : (k + 1) * size].astype(bf16)


def by_columns(kernel, row_counts, *arrays, tile=896):
    cols = arrays[0].shape[1]

    def of(rows):
        return pl.BlockSpec((rows, tile), lambda j: (0, j))

    return pl.pallas_call(
        kernel,
        grid=(cols // tile,),
        in_specs=[of(a.shape[0]) for a in arrays],
        out_specs=[of(r) for r in row_counts],
        out_shape=[jax.ShapeDtypeStruct((r, cols), bf16) for r in row_counts],
        compiler_params=big,
        cost_estimate=costs(3),
    )(*arrays)


def own_columns(me, refs, start, size, out_ref, at=0):
    for k, ref in enumerate(refs):
        place = pl.multiple_of((me ^ k) * size, 128)
        out_ref[:, pl.ds(at + place, size)] = ref[:, start : start + size].astype(f32)


def gain_sum(pairs, gain_ref):
    total = sum(
        jnp.sum(weight[...].astype(f32) * grad[...], axis=1, keepdims=True) for weight, grad in pairs
    )
    return total / gain_ref[...].astype(f32)


def unpack_mlp_kernel(units, me_ref, g0, g1, g2, g3, gate_ref, up_ref, gain_ref, grad_gate, grad_up, grad_down, grad_gain):
    for i, out in enumerate((grad_gate, grad_up, grad_down)):
        own_columns(me_ref[0], (g0, g1, g2, g3), i * units, units, out)
    grad_gain[...] = gain_sum(((gate_ref, grad_gate), (up_ref, grad_up)), gain_ref)


def unpack_out_kernel(inner, q_cols, me_ref, g0, g1, g2, g3, grad_mamba, grad_output):
    own_columns(me_ref[0], (g0, g1, g2, g3), 0, inner, grad_mamba)
    own_columns(me_ref[0], (g0, g1, g2, g3), inner, q_cols, grad_output)


def unpack_in_kernel(
    inner, state, heads, pad, me_ref, g0, g1, g2, g3, mamba_ref, query_ref, key_ref, value_ref, gain_ref,
    grad_mamba, grad_query, grad_key, grad_value, grad_gain,
):
    me = me_ref[0]
    refs = (g0, g1, g2, g3)
    own_columns(me, refs, 0, inner, grad_mamba)
    own_columns(me, refs, inner, inner, grad_mamba, TP * inner)
    at, out_at = 2 * inner, 2 * TP * inner
    shared = sum(ref[:, at : at + 2 * state].astype(f32) for ref in refs)
    grad_mamba[:, out_at : out_at + 2 * state] = shared
    at, out_at = at + 2 * state, out_at + 2 * state
    lane = iota((grad_mamba.shape[0], pad), 1)
    steps = jnp.zeros((grad_mamba.shape[0], pad), f32)
    for k, ref in enumerate(refs):
        piece = jnp.where(lane < heads, ref[:, at : at + pad].astype(f32), 0.0)
        steps = steps + pltpu.roll(piece, (me ^ k) * heads, axis=1)
    grad_mamba[:, out_at : out_at + TP * heads] = steps[:, : TP * heads]
    at += pad
    q_cols = query_ref.shape[1] // TP
    own_columns(me, refs, at, q_cols, grad_query)
    at += q_cols
    for out, start in ((grad_key, at), (grad_value, at + HD)):
        for first in (0, 2):
            both = refs[first][:, start : start + HD].astype(f32)
            both = both + refs[first + 1][:, start : start + HD].astype(f32)
            place = pl.multiple_of(((me ^ first) // 2) * HD, HD)
            out[:, pl.ds(place, HD)] = both
    pairs = ((mamba_ref, grad_mamba), (query_ref, grad_query), (key_ref, grad_key), (value_ref, grad_value))
    grad_gain[...] = gain_sum(pairs, gain_ref)


def unpack(kernel, me, parts, others, widths):
    rows = parts[0].shape[0]
    shapes = [(rows, w) for w in widths]
    return pl.pallas_call(
        kernel,
        grid=(1,),
        in_specs=[pl.BlockSpec(memory_space=pltpu.SMEM)]
        + specs(*[p.shape for p in parts], *[o.shape for o in others]),
        out_specs=specs(*shapes),
        out_shape=[jax.ShapeDtypeStruct(shape, f32) for shape in shapes],
        compiler_params=big,
        cost_estimate=costs(5),
    )(me, *parts, *others)


def weight_grad_kernel(bounds, mine, blocks, table_ref, *refs):
    parts = len(bounds)
    lefts = [refs[2 * mine * p : 2 * mine * p + mine] for p in range(parts)]
    rights = [refs[2 * mine * p + mine : 2 * mine * (p + 1)] for p in range(parts)]
    rest = refs[2 * mine * parts :]
    outs, plain, turned = rest[: -1 - parts], rest[-1 - parts], rest[-parts:]
    step = pl.program_id(0)
    size = plain.shape[0] // blocks

    @pl.when(step == 0)
    def _():
        for part in range(parts):
            plain[...] = jnp.concatenate([jnp.transpose(ref[...]) for ref in lefts[part]], axis=1)
            for block in range(blocks):
                at = pl.multiple_of(table_ref[block] * size, size)
                turned[part][block * size : (block + 1) * size, :] = plain[pl.ds(at, size), :]

    for part, (low, high) in enumerate(bounds):

        @pl.when((step >= low) & (step < high))
        def _(part=part):
            right = jnp.concatenate([ref[...] for ref in rights[part]], axis=0)
            full = jnp.dot(turned[part][...], right, preferred_element_type=f32)
            half = full.shape[0] // len(outs)
            for i, out in enumerate(outs):
                out[...] = full[i * half : (i + 1) * half].astype(out.dtype)


def weight_grads(table, pieces, pairs, tile=512):
    mine = len(pairs[0][0])
    rows, model = pairs[0][0][0].shape
    bounds, specs_in, args, low, cols = [], [], [], 0, 0
    for left, right, start, count in pairs:
        tiles = pl.cdiv(count, tile)
        first, last = low - start // tile, low + tiles - 1
        specs_in += [pl.BlockSpec((rows, model), lambda j: (0, 0))] * mine
        specs_in += [
            pl.BlockSpec(
                (rows, tile),
                lambda j, low=low, last=last, first=first: (0, jnp.clip(j, low, last) - first),
            )
        ] * mine
        args += list(left) + list(right)
        bounds.append((low, low + tiles))
        low += tiles
        cols += count
    return pl.pallas_call(
        functools.partial(weight_grad_kernel, tuple(bounds), mine, table.shape[0]),
        grid=(low,),
        in_specs=[pl.BlockSpec(memory_space=pltpu.SMEM)] + specs_in,
        out_specs=[pl.BlockSpec((model // pieces, tile), lambda j: (0, j))] * pieces,
        out_shape=[jax.ShapeDtypeStruct((model // pieces, cols), bf16)] * pieces,
        scratch_shapes=[pltpu.VMEM((model, mine * rows), bf16)] * (1 + len(pairs)),
        compiler_params=big,
        cost_estimate=costs(1 + cols // 256),
    )(table, *args)


def local(
    plane,
    tokens,
    lengths,
    offsets,
    norm_gain,
    mamba_in,
    conv_taps,
    conv_bias,
    step_bias,
    decay_log,
    skip_weight,
    mamba_gain,
    mamba_out,
    query_weight,
    key_weight,
    value_weight,
    output_weight,
    second_gain,
    gate_weight,
    up_weight,
    down_weight,
    cotangent,
):
    me = lax.axis_index("tp")
    peers = lax.axis_size(plane)
    batches, width, model = tokens.shape
    rows = batches * width
    shard = mamba_in.shape[0]
    inner = mamba_gain.shape[0]
    heads = step_bias.shape[0]
    state = (mamba_in.shape[1] - 2 * inner - heads) // 2
    q_cols = query_weight.shape[1]
    kv_heads = key_weight.shape[1] // HD
    hidden_units = gate_weight.shape[1]
    inner_t, heads_t, q_t, ff_t = inner // TP, heads // TP, q_cols // TP, hidden_units // TP
    pad = 128

    def swap(values, k, axis="tp"):
        size = lax.axis_size(axis)
        return lax.ppermute(values, axis, [(i, i ^ k) for i in range(size)])

    def spread_first(values):
        half = values.shape[1] // 2
        return swap(values[:, :half], 3), swap(values[:, half:], 1)

    def spread_second(values, far, near):
        half = values.shape[1] // 2
        pair = swap(jnp.concatenate([values[:, :half], far], axis=0), 1)
        last = swap(jnp.concatenate([values[:, half:], near], axis=0), 3)
        return values, far, pair, near, last

    def spread(values):
        return spread_second(values, *spread_first(values))

    def reduce_send(halves):
        return swap(halves[1], 1), swap(halves[3], 3)

    def reduce_add(halves, got, got_right):
        return halves[0] + got.astype(f32), halves[2] + got_right.astype(f32)

    def reduce_first(*halves):
        return reduce_add(halves, *reduce_send(halves))

    def reduce_second(pair, last):
        half = pair.shape[0] // 2
        got = swap(pair[half:].astype(bf16), 3)
        got_right = swap(last[half:].astype(bf16), 1)
        return pair[:half], got, last[:half], got_right

    def pair_finish(one, two, got_one, got_two):
        pairs = [reduce_add(one, *got_one), reduce_add(two, *got_two)]
        half = one[1].shape[0] // 2
        sends = [
            swap(jnp.concatenate([p[i][half:].astype(bf16) for p in pairs], axis=0), k)
            for i, k in ((0, 3), (1, 1))
        ]
        return [
            (p[0][:half], sends[0][i * half : (i + 1) * half], p[1][:half], sends[1][i * half : (i + 1) * half])
            for i, p in enumerate(pairs)
        ]

    def reduce(*halves):
        return reduce_second(*reduce_first(*halves))

    def everywhere(values):
        return [values] + [swap(values, k) for k in range(1, TP)]

    def absolute(parts):
        stacked = jnp.stack(parts)
        return jnp.concatenate(
            [lax.dynamic_index_in_dim(stacked, me ^ t, 0) for t in range(TP)], axis=0
        )

    cube = len(plane) == 3

    def order(values):
        lead = values.shape[:-1]
        if cube:
            split = values.reshape(lead + (TP, 2, 2, 2, shard))
            split = jnp.moveaxis(split, (-2, -4, -3, -5), (-5, -4, -3, -2))
        else:
            split = jnp.swapaxes(values.reshape(lead + (TP, peers, shard)), -3, -2)
        return split.reshape(values.shape)

    def place(n):
        group, at = divmod(n, peers)
        if cube:
            x, y, core = at // 4, at // 2 % 2, at % 2
            at = core * 4 + x * 2 + y
        return at * TP + group

    places = [place(n) for n in range(peers * TP)]

    blocks = jnp.arange(peers * TP, dtype=jnp.int32)
    in_group = blocks ^ me
    in_plane = blocks ^ (lax.axis_index(plane) * TP + me)

    def cut(weight, start, size, t):
        return lax.dynamic_slice_in_dim(weight, start + t * size, size, axis=1)

    def kv(weight, t):
        return cut(weight, 0, HD, t * kv_heads // TP)

    slot_column = jnp.concatenate([lengths[:, 0], offsets[:, 0]]).astype(bf16)[:, None]

    def in_slice(t):
        return jnp.concatenate(
            [
                cut(mamba_in, 0, inner_t, t),
                cut(mamba_in, inner, inner_t, t),
                mamba_in[:, 2 * inner : 2 * inner + 2 * state],
                cut(mamba_in, 2 * inner + 2 * state, heads_t, t),
                norm_gain[:, None],
                second_gain[:, None],
                jnp.pad(slot_column, ((0, shard - 2 * batches), (0, pad - heads_t - 3))),
                cut(query_weight, 0, q_t, t),
                kv(key_weight, t),
                kv(value_weight, t),
            ],
            axis=1,
        )

    def out_slice(t):
        return jnp.concatenate([cut(mamba_out.T, 0, inner_t, t), cut(output_weight.T, 0, q_t, t)], axis=1)

    def mlp_slice(t):
        return jnp.concatenate(
            [
                cut(gate_weight, 0, ff_t, t),
                cut(up_weight, 0, ff_t, t),
                cut(down_weight.T, 0, ff_t, t),
            ],
            axis=1,
        )

    def after(values, *earlier):
        return lax.optimization_barrier((values, earlier))[0]

    def slices(make):
        return [make(me ^ k) for k in range(TP)]

    def exchange(pieces):
        return [pieces[0]] + [swap(pieces[k], k) for k in range(1, TP)]

    def gather(parts):
        return lax.all_gather(absolute(parts).reshape(TP * shard, -1), plane, axis=0, tiled=True)

    def scatter(grads):
        return lax.psum_scatter(grads, plane, scatter_dimension=0, tiled=True)

    def pass_on(part):
        part = part.reshape(TP, shard, -1)
        return exchange([part[k] for k in range(TP)])

    conv_cols = inner_t + 2 * state
    at_q = inner_t + conv_cols + pad
    in_cols = at_q + q_t + 2 * HD

    def own(values, size):
        return lax.dynamic_slice_in_dim(values, me * size, size, axis=-1)

    taps_t = jnp.concatenate([own(conv_taps[:, :inner], inner_t), conv_taps[:, inner:]], axis=1)
    bias_t = jnp.concatenate([own(conv_bias[:inner], inner_t), conv_bias[inner:]])[None]
    steps_t = jnp.pad(
        jnp.stack([own(step_bias, heads_t), own(decay_log, heads_t)]), ((0, 0), (0, pad - heads_t))
    )
    skip_t = jnp.repeat(own(skip_weight, heads_t), inner_t // heads_t)[None]
    gain_t = own(mamba_gain, inner_t)[None]
    sizes = (inner_t, state, heads_t)

    def widened(values):
        return jnp.pad(values, ((0, 0), (0, conv_cols - values.shape[1])))

    params = jnp.concatenate(
        [taps_t, bias_t, widened(skip_t), widened(gain_t), widened(steps_t.reshape(1, -1))], axis=0
    )

    in_slices = slices(in_slice)
    in_parts = exchange(in_slices)
    tokens, cotangent = after((tokens, cotangent), in_slices)
    source = order(tokens.reshape(rows, model))
    upstream = order(cotangent.reshape(rows, model))
    prepared = (
        source, upstream, slices(out_slice), slices(mlp_slice),
        params, gain_t, in_plane, in_group,
    )
    in_parts, prepared = lax.optimization_barrier((in_parts, prepared))
    source, upstream, out_slices, mlp_slices = prepared[:4]
    params, gain_t, in_plane, in_group = prepared[4:]
    w_in = gather(in_parts)
    source_some, upstream_some = spread_first(source), spread_first(upstream)
    column = inner_t + 2 * state + inner_t + heads_t + 2
    slots = jnp.stack([in_parts[k][: 2 * batches, column] for k in (0, 3, 1, 2)])
    slots = after(slots, source_some).astype(jnp.int32).reshape(TP, 2, batches)
    slots = jnp.swapaxes(slots, 1, 2).reshape(TP * batches, 2)
    turns = turn_table(slots[:, 1], width)
    source_all = spread_second(source, *source_some)
    out_parts = exchange(after(out_slices, (source_all, upstream_some)))
    w_out = gather(out_parts)
    mlp_slices, upstream_some = after((mlp_slices, upstream_some), out_parts[1:])
    mlp_parts = exchange(mlp_slices)
    upstream_all = spread_second(upstream, *upstream_some)

    normed, projected, y, squares, mixed, gains = mixer_inner(
        slots, after(source_all, (out_parts[1:], mlp_parts[1])), w_in, params, turns, *sizes
    )
    squares = everywhere(after(squares, upstream_all))
    w_mlp = gather(after(mlp_parts, squares[1:]))
    branches, root, *halves = mixer_outer(projected, y, mixed, gain_t, squares, w_out)
    hidden, second = row_call(hidden_kernel, slots, reduce(*halves), source, gains)

    product, *halves, mlp_sums = feed_forward(
        slots, in_group, spread(second), upstream_all, w_mlp, ff_t
    )
    mlp_sums = scatter(mlp_sums)
    d_hidden, branch_grad = row_call(
        back_hidden_kernel, slots, reduce(*halves), hidden, upstream, gains
    )

    branch_all = spread(branch_grad)
    last_halves = back_out(product, w_mlp, 2)
    branch_grad = after(branch_all, last_halves)
    branch_all, d_branches, dots = back_outer(
        branch_grad, w_out, projected, y, gain_t, slots.shape[0]
    )
    last_halves = after(last_halves, branch_grad)
    last_pair = reduce_send(last_halves)
    out_sums = weight_grads(in_group, 1, [([branch_all], [branches], 0, inner_t + q_t)])
    dots = after(everywhere(dots), (out_sums, last_pair))
    out_sums = scatter(out_sums[0])
    mlp_grads = pass_on(after(mlp_sums, dots))
    proj_grad, small = mixer_backward(
        slots, projected, params, turns, y, d_branches, root, dots, *sizes,
    )
    in_sums = weight_grads(
        in_plane if cube else in_group,
        2 if cube else 1,
        [([after(normed, mlp_grads)], [proj_grad], 0, in_cols)],
    )
    riders = small.astype(bf16)
    out_sums, riders = after((out_sums, riders), in_sums)
    out_sums = out_sums.reshape(TP, shard, -1)
    received = [
        swap(jnp.concatenate([out_sums[k], riders], axis=0), k) for k in range(1, TP)
    ]
    norm_halves = back_out(after(proj_grad, in_sums), w_in, 0)
    norm_pair = reduce_send(norm_halves)
    if cube:
        block, half = TP * shard, TP * shard // 2
        counts = (block, block, block, half, half)
        keep, send = in_sums
        mine, along_y, along_x, across_x, across_y = by_columns(
            chip_kernel, counts, keep, after(swap(send, 1, "core"), (norm_halves, received))
        )
        across = swap(across_x, 1, "x"), swap(across_y, 1, "y")
        norm_pair, across = after((norm_pair, across), norm_pair)
        to_y, to_x = by_columns(
            along_kernel, (block, block), along_y, along_x, *across
        )
        in_parts = swap(to_x, 1, "x"), swap(to_y, 1, "y")
    last_pair = after(last_pair, norm_pair)
    norm_parts, last_parts = pair_finish(norm_halves, last_halves, norm_pair, last_pair)
    out_grads = [out_sums[0]] + [r[:shard] for r in received]
    small = absolute([small] + [r[shard:].astype(f32) for r in received])
    if cube:
        small = small + swap(small, 1, "core")
        in_parts = after(in_parts, (norm_parts, last_parts, small))
        in_sums = by_columns(plane_kernel, (shard,) * TP, mine, *in_parts)
        in_grads = exchange(in_sums)
    else:
        in_sums = scatter(in_sums[0])
        in_grads = pass_on(in_sums)
    small, mlp_grads, out_grads, norm_parts, last_parts = after(
        (small, mlp_grads, out_grads, norm_parts, last_parts), in_sums
    )
    if cube:
        small = small + swap(small, 1, "x")
        small = small + swap(small, 1, "y")
    else:
        small = lax.psum(small, plane)
    token_grads = whole_call(
        functools.partial(token_grad_kernel, places), f32, (), *norm_parts, d_hidden, source, gains
    )
    output = whole_call(
        functools.partial(output_kernel, places), bf16, (slots,), *last_parts, hidden
    )

    at_group = me[None].astype(jnp.int32)
    grad_gate, grad_up, grad_down, grad_second_gain = unpack(
        functools.partial(unpack_mlp_kernel, ff_t),
        at_group,
        mlp_grads,
        (gate_weight, up_weight, second_gain[:, None]),
        (hidden_units, hidden_units, hidden_units, 1),
    )
    grad_mamba_out, grad_output = unpack(
        functools.partial(unpack_out_kernel, inner_t, q_t), at_group, out_grads, (), (inner, q_cols)
    )
    in_grads = after(in_grads, (small, token_grads, output, grad_down, grad_output))
    grad_mamba_in, grad_query, grad_key, grad_value, grad_norm_gain = unpack(
        functools.partial(unpack_in_kernel, *sizes, pad),
        at_group,
        in_grads,
        (mamba_in, query_weight, key_weight, value_weight, norm_gain[:, None]),
        (mamba_in.shape[1], q_cols, kv_heads * HD, kv_heads * HD, 1),
    )
    grad_mamba_out, grad_output, grad_down = grad_mamba_out.T, grad_output.T, grad_down.T
    grad_norm_gain, grad_second_gain = grad_norm_gain[:, 0], grad_second_gain[:, 0]

    kernel = conv_taps.shape[0]
    small = small.reshape(TP, -1, 8, small.shape[-1])
    small = jnp.concatenate([small[:, i] for i in range(small.shape[1])], axis=-1)
    conv = small[:, : kernel + 1, :conv_cols]
    conv = jnp.concatenate(
        [conv[:, :, :inner_t].transpose(1, 0, 2).reshape(kernel + 1, inner), conv[:, :, inner_t:].sum(0)],
        axis=1,
    )
    by_inner = small[:, :2, conv_cols : conv_cols + inner_t]
    by_step = small[:, :2, conv_cols + inner_t : conv_cols + inner_t + heads_t]
    return (
        output.reshape(tokens.shape),
        token_grads.reshape(tokens.shape),
        grad_norm_gain,
        grad_mamba_in,
        conv[:kernel],
        conv[kernel],
        by_step[:, 0].reshape(-1),
        by_step[:, 1].reshape(-1),
        by_inner[:, 1].reshape(heads, -1).sum(1),
        by_inner[:, 0].reshape(-1),
        grad_mamba_out,
        grad_query,
        grad_key,
        grad_value,
        grad_output,
        grad_second_gain,
        grad_gate,
        grad_up,
        grad_down,
    )


def solution(mesh):
    count = mesh.devices.size
    if tuple(mesh.devices.shape) == (8, 4):
        grid = Mesh(mesh.devices.reshape(TP, 2, 2, 2), ("tp", "x", "y", "core"))
        plane = ("core", "x", "y")
    else:
        grid = Mesh(mesh.devices.reshape(TP, count // TP), ("tp", "fs"))
        plane = ("fs",)
    every = grid.axis_names
    down, across, slots = P(every, None), P(None, every), P(None, every, None)
    line, copied = P(every), P()
    return jax.shard_map(
        functools.partial(local, plane),
        mesh=grid,
        in_specs=(
            slots, across, across, line, down, copied, copied, copied, copied, copied, copied,
            across, down, down, down, across, line, down, down, across, slots,
        ),
        out_specs=(
            slots, slots, line, down, copied, copied, copied, copied, copied, copied,
            across, down, down, down, across, line, down, down, across,
        ),
        check_vma=False,
    )
```

```python
import functools
import math

import jax
import jax.numpy as jnp
from jax import lax
from jax.experimental import pallas as pl
from jax.experimental.pallas import tpu as pltpu
from jax.sharding import Mesh
from jax.sharding import PartitionSpec as P

HD = 128
TP = 4
PAD = 128

epsilon = 1e-05
rope_base = 100000000000.0
highest = lax.Precision.HIGHEST
f32 = jnp.float32
bf16 = jnp.bfloat16


def inverse_root(values):
    return lax.rsqrt(jnp.mean(values * values, axis=-1, keepdims=True) + epsilon)


def norm_back(values, root, grad):
    return root * grad - values * root**3 * jnp.mean(values * grad, axis=-1, keepdims=True)


def dot_nn(left, right):
    return jnp.dot(left, right, preferred_element_type=f32)


def dot_nt(left, right):
    return lax.dot_general(left, right, (((1,), (1,)), ((), ())), preferred_element_type=f32)


def inside_rows(length, offset, width):
    rows = jnp.arange(width, dtype=jnp.int32)[:, None]
    return ((rows >= offset) & (rows < offset + length)).astype(f32)


def turn_table(offsets, width):
    half = HD // 2
    freqs = rope_base ** (-jnp.arange(half, dtype=f32) * 2.0 / HD)
    rows = jnp.arange(width, dtype=jnp.int32)
    positions = (rows[None, :] - offsets[:, None]).astype(f32)
    angles = positions.reshape(-1, 1) * freqs
    cosine, sine = jnp.cos(angles), jnp.sin(angles)
    return jnp.concatenate([cosine, cosine, -sine, sine], axis=1)


def mm(left, right, dims, precision=lax.Precision.HIGH):
    return lax.dot_general(left, right, (dims, ((), ())), precision=precision, preferred_element_type=f32)


NN = ((1,), (0,))
NT = ((1,), (1,))
TN = ((0,), (0,))


def iota(shape, axis):
    return lax.broadcasted_iota(jnp.int32, shape, axis)


def down_rows(values, count):
    if count == 0:
        return values
    return jnp.where(iota(values.shape, 0) >= count, pltpu.roll(values, count, axis=0), 0.0)


def up_rows(values, count):
    if count == 0:
        return values
    length = values.shape[0]
    return jnp.where(
        iota(values.shape, 0) < length - count, pltpu.roll(values, length - count, axis=0), 0.0
    )


def head_sums(values, spread):
    return mm(values, spread, NT)


def parameters(ref, inner):
    values = ref[...]
    last = values.shape[0] - 1
    steps = jnp.concatenate([values[last:, :PAD], values[last:, PAD : 2 * PAD]], axis=0)
    return (
        values[: last - 3], values[last - 3 : last - 2], steps,
        values[last - 2 : last - 1, :inner], values[last - 1 : last, :inner],
    )


def mamba_shared(proj, start, count, taps_ref, bias_ref, steps_ref, inner, state, heads):
    length = proj.shape[0]
    conv_cols = inner + 2 * state
    row = iota((length, 1), 0)
    inside = ((row >= start) & (row < start + count)).astype(f32)
    conv_in = proj[:, inner : inner + conv_cols] * inside
    kernel = taps_ref.shape[0]
    conv = bias_ref[...] + jnp.zeros_like(conv_in)
    for tap in range(kernel):
        conv = conv + taps_ref[tap : tap + 1, :] * down_rows(conv_in, kernel - 1 - tap)
    sig = jax.nn.sigmoid(conv)
    active = conv * sig
    pad = steps_ref.shape[1]
    lane = iota((length, pad), 1)
    raw = jnp.where(lane < heads, proj[:, inner + conv_cols : inner + conv_cols + pad] + steps_ref[0:1, :], 0.0)
    step = jnp.where(lane < heads, jnp.maximum(raw, 0.0) + jnp.log1p(jnp.exp(-jnp.abs(raw))), 0.0)
    rate = -jnp.exp(steps_ref[1:2, :])
    lower = (iota((length, length), 0) >= iota((length, length), 1)).astype(f32)
    cum = mm(lower, step * rate, NN, highest)
    size = inner // heads
    spread = (iota((pad, inner), 0) == iota((pad, inner), 1) // size).astype(f32)
    step_x = mm(step, spread, NN)
    cum_x = mm(cum, spread, NN, highest)
    at = iota((length, inner), 1) % length
    diagonal = iota((length, inner), 0) == at
    cum_row = jnp.sum(jnp.where(diagonal, cum_x, 0.0), axis=0, keepdims=True)
    allowed = (
        (at <= iota((length, inner), 0)) & (inside > 0.0) & (at >= start) & (at < start + count)
    )
    decay = jnp.where(allowed, jnp.exp(jnp.where(allowed, cum_x - cum_row, 0.0)), 0.0)
    xs = active[:, :inner]
    b_state = active[:, inner : inner + state]
    c_state = active[:, inner + state :]
    inter = mm(c_state, b_state, NT)
    pair = jnp.concatenate([inter, inter], axis=1)
    mixing = decay * jnp.concatenate([pair] * (inner // pair.shape[1]), axis=1)
    return dict(
        inside=inside, conv_in=conv_in, conv=conv, sig=sig, raw=raw, step=step, rate=rate,
        spread=spread, step_x=step_x, diagonal=diagonal, decay=decay, mixing=mixing, xs=xs,
        b_state=b_state, c_state=c_state, lower=lower, lane=lane,
    )


def two_blocks(values):
    left = iota(values.shape, 1) < values.shape[1] // 2
    return jnp.concatenate([jnp.where(left, values, 0.0), jnp.where(left, 0.0, values)], axis=0)


def turn(values, cosine, sine):
    return values * cosine + pltpu.roll(values, HD // 2, axis=1) * sine


def attention_shared(proj, at, start, count, cosine, sine):
    length = proj.shape[0]
    kv = proj.shape[1] - 2 * HD
    queries = jnp.concatenate(
        [turn(proj[:, c : c + HD], cosine, sine) for c in range(at, kv, HD)], axis=0
    )
    keys = turn(proj[:, kv : kv + HD], cosine, sine)
    values = proj[:, kv + HD :]
    scores = mm(queries, keys, NT) * (1.0 / math.sqrt(HD))
    row = iota(scores.shape, 0) % length
    col = iota(scores.shape, 1)
    end = start + count
    allowed = ((row >= start) & (row < end) & (col >= start) & (col <= row)) | (row == col)
    scores = jnp.where(allowed, scores, -1e30)
    probs = jnp.exp(scores - jnp.max(scores, axis=1, keepdims=True))
    probs = probs / jnp.sum(probs, axis=1, keepdims=True)
    return queries, keys, values, probs


def specs(*shapes):
    return [pl.BlockSpec(s, lambda i: (0, 0)) for s in shapes]


def rows_spec(length, cols):
    return pl.BlockSpec((length, cols), lambda i: (i, 0))


def their_spec(length, each, k):
    return pl.BlockSpec((1, 1, length), lambda i: (i ^ (THEIRS[k][0] * each), 0, 0))


big = pltpu.CompilerParams(vmem_limit_bytes=50 * 1024 * 1024)


def costs(microseconds):
    return pl.CostEstimate(
        flops=microseconds * 10**9, bytes_accessed=microseconds * 10**5, transcendentals=0
    )


def inside_of(slots_ref, seq, length):
    row = iota((length, 1), 0)
    start = slots_ref[seq, 1]
    return ((row >= start) & (row < start + slots_ref[seq, 0])).astype(f32)


def as_row(column):
    length = column.shape[0]
    same = iota((length, length), 0) == iota((length, length), 1)
    return jnp.sum(jnp.where(same, column, 0.0), axis=0, keepdims=True)


def as_column(row):
    length = row.shape[1]
    same = iota((length, length), 0) == iota((length, length), 1)
    return jnp.sum(jnp.where(same, row, 0.0), axis=1, keepdims=True)


THEIRS = ((0, 1, 2, 3), (2, 3, 0, 1), (3, 2, 1, 0), (1, 0, 3, 2))


def group_total(refs, seq):
    each = refs[0].shape[0] // TP
    return sum(ref[THEIRS[k][seq // each] * each + seq % each] for k, ref in enumerate(refs))


def joined_rows(refs):
    own, far, pair, near, last = refs
    half = far.shape[1]
    count = own.shape[0]
    left = jnp.concatenate([own[:, :half], far[...], pair[...]], axis=0)
    right = jnp.concatenate([own[:, half:], last[:count, :], near[...], last[count:, :]], axis=0)
    return jnp.concatenate([left, right], axis=1)


def put_left(values, refs):
    half = values.shape[0] // 2
    refs[0][...] = values[:half]
    refs[1][...] = values[half:].astype(bf16)


def put_right(values, refs):
    one = values.shape[0] // TP
    refs[2][:one, :] = values[:one]
    refs[2][one:, :] = values[2 * one : 3 * one]
    refs[3][:one, :] = values[one : 2 * one].astype(bf16)
    refs[3][one:, :] = values[3 * one :].astype(bf16)


def put_tiles(values, refs):
    step = pl.program_id(0)
    middle = pl.num_programs(0) // 2

    @pl.when(step < middle)
    def _():
        put_left(values, refs)

    @pl.when(step >= middle)
    def _():
        put_right(values, refs)


def halves_out(rows, model, tile):
    middle = model // tile // 2
    left = pl.BlockSpec((rows // 2, tile), lambda j: (0, jnp.minimum(j, middle - 1)))
    right = pl.BlockSpec((rows // 2, tile), lambda j: (0, jnp.maximum(j - middle, 0)))
    shapes = [jax.ShapeDtypeStruct((rows // 2, model // 2), t) for t in (f32, bf16, f32, bf16)]
    return [left, left, right, right], shapes


def both_halves(refs):
    kept, got, kept_right, got_right = refs
    return jnp.concatenate(
        [kept[...] + got[...].astype(f32), kept_right[...] + got_right[...].astype(f32)], axis=1
    )


def inner_kernel(
    inner, state, heads, tiles, slots_ref, p0, p1, p2, p3, p4, weight_ref, gains_in_ref, params_ref,
    turn_ref, normed_ref, proj_ref, y_ref, square_ref, mixed_ref, gains_ref,
):
    step = pl.program_id(0)
    tile = weight_ref.shape[1]

    @pl.when(step == 0)
    def _():
        rows = joined_rows((p0, p1, p2, p3, p4)).astype(f32)
        turned = jnp.transpose(gains_in_ref[...].astype(f32))
        gains_ref[0:1, :] = turned[heads : heads + 1]
        gains_ref[1:2, :] = turned[heads + 1 : heads + 2]
        normed_ref[...] = (rows * inverse_root(rows) * turned[heads : heads + 1]).astype(bf16)

    @pl.when(step < tiles)
    def _():
        at = pl.multiple_of(step * tile, tile)
        proj_ref[:, pl.ds(at, tile)] = jnp.dot(
            normed_ref[...], weight_ref[...], preferred_element_type=f32
        )

    @pl.when(step >= tiles)
    def _():
        seq = step - tiles
        length = y_ref.shape[0]
        proj = proj_ref[pl.ds(pl.multiple_of(seq * length, length), length), :]
        start = slots_ref[seq, 1]
        count = slots_ref[seq, 0]
        taps, bias, steps, skip, _ = parameters(params_ref, inner)
        m = mamba_shared(proj, start, count, taps, bias, steps, inner, state, heads)
        scaled = m["xs"] * m["step_x"]
        wide = 2 * length
        parts = [
            mm(m["mixing"][:, c : c + wide], two_blocks(scaled[:, c : c + wide]), NN)
            for c in range(0, inner, wide)
        ]
        y = jnp.concatenate(parts, axis=1) + skip * m["xs"]
        y_ref[...] = y
        gate = proj[:, :inner]
        gated = y * gate * jax.nn.sigmoid(gate)
        square_ref[0] = as_row(jnp.sum(gated * gated, axis=1, keepdims=True))
        at = 2 * inner + 2 * state + PAD
        _, _, values, probs = attention_shared(
            proj, at, start, count, turn_ref[:, :HD], turn_ref[:, HD:]
        )
        mixed = mm(probs, values, NN)
        mixed_ref[...] = jnp.concatenate(
            [mixed[r : r + length] for r in range(0, mixed.shape[0], length)], axis=1
        ).astype(mixed_ref.dtype)


def mixer_inner(slots, rows, weight, params, turns, inner, state, heads, tile=896):
    model, cols = weight.shape
    seqs = slots.shape[0]
    pieces = rows
    rows = TP * pieces[0].shape[0]
    length = rows // seqs
    tiles = cols // tile
    pad = PAD
    at_steps = (2 * inner + 2 * state) // pad
    q_cols = cols - 2 * inner - 2 * state - pad - 2 * HD

    def seq_spec(*shape):
        zeros = (0,) * (len(shape) - 1)
        return pl.BlockSpec(shape, lambda j: (jnp.maximum(j - tiles, 0),) + zeros)

    return pl.pallas_call(
        functools.partial(inner_kernel, inner, state, heads, tiles),
        grid=(tiles + seqs,),
        in_specs=[pl.BlockSpec(memory_space=pltpu.SMEM)]
        + specs(*[p.shape for p in pieces])
        + [
            pl.BlockSpec((model, tile), lambda j: (0, jnp.minimum(j, tiles - 1))),
            pl.BlockSpec((model, pad), lambda j: (0, at_steps)),
        ]
        + specs(params.shape)
        + [seq_spec(length, turns.shape[1])],
        out_specs=specs((rows, model), (rows, cols))
        + [seq_spec(length, inner), seq_spec(1, 1, length), seq_spec(length, q_cols)]
        + specs((8, model)),
        out_shape=[
            jax.ShapeDtypeStruct((rows, model), bf16),
            jax.ShapeDtypeStruct((rows, cols), f32),
            jax.ShapeDtypeStruct((rows, inner), f32),
            jax.ShapeDtypeStruct((seqs, 1, length), f32),
            jax.ShapeDtypeStruct((rows, q_cols), bf16),
            jax.ShapeDtypeStruct((8, model), f32),
        ],
        compiler_params=big,
        cost_estimate=costs(18),
    )(slots, *pieces, weight, weight, params, turns)


def outer_kernel(inner, gate_ref, y_ref, mixed_ref, gain_ref, s0, s1, s2, s3, weight_ref, branches_ref, root_ref, *halves):
    @pl.when(pl.program_id(0) == 0)
    def _():
        length = root_ref.shape[2]
        for seq in range(root_ref.shape[0]):
            rows = slice(seq * length, (seq + 1) * length)
            root = lax.rsqrt(group_total((s0, s1, s2, s3), seq) / (TP * inner) + epsilon)
            root_ref[seq] = root
            gate = gate_ref[rows, :]
            gated = y_ref[rows, :] * gate * jax.nn.sigmoid(gate)
            branches_ref[rows, :inner] = (gated * as_column(root) * gain_ref[...]).astype(bf16)
        branches_ref[:, inner:] = mixed_ref[...]

    put_tiles(dot_nt(branches_ref[...], weight_ref[...]), halves)


def mixer_outer(proj, y, mixed, gain, squares, weight, tile=512):
    rows, inner = y.shape
    model, cols = weight.shape
    half_specs, half_shapes = halves_out(rows, model, tile)
    return pl.pallas_call(
        functools.partial(outer_kernel, inner),
        grid=(model // tile,),
        in_specs=specs((rows, inner), y.shape, mixed.shape, gain.shape)
        + [pl.BlockSpec(squares[0].shape, lambda j: (0, 0, 0))] * TP
        + [pl.BlockSpec((tile, cols), lambda j: (j, 0))],
        out_specs=specs((rows, cols))
        + [pl.BlockSpec(squares[0].shape, lambda j: (0, 0, 0))]
        + half_specs,
        out_shape=[
            jax.ShapeDtypeStruct((rows, cols), bf16),
            jax.ShapeDtypeStruct(squares[0].shape, f32),
        ]
        + half_shapes,
        compiler_params=big,
        cost_estimate=costs(4),
    )(proj, y, mixed, gain, *squares, weight)


def back_out_kernel(left_ref, weight_ref, *halves):
    put_tiles(dot_nt(left_ref[...], weight_ref[...]), halves)


def back_out(left, weight, column, tile=512):
    rows, cols = left.shape
    model = weight.shape[0]
    half_specs, half_shapes = halves_out(rows, model, tile)
    return pl.pallas_call(
        back_out_kernel,
        grid=(model // tile,),
        in_specs=specs(left.shape) + [pl.BlockSpec((tile, cols), lambda j: (j, column))],
        out_specs=half_specs,
        out_shape=half_shapes,
        compiler_params=big,
        cost_estimate=costs(4),
    )(left, weight)


def inside_all(slots_ref, seqs, length):
    return jnp.concatenate([inside_of(slots_ref, seq, length) for seq in range(seqs)], axis=0)


def hidden_kernel(slots_ref, k0, k1, k2, k3, source_ref, gains_ref, hidden_ref, second_ref):
    length = source_ref.shape[0] * TP // slots_ref.shape[0]
    inside = inside_all(slots_ref, slots_ref.shape[0] // TP, length)
    hidden = source_ref[...].astype(f32) + inside * both_halves((k0, k1, k2, k3))
    hidden_ref[...] = hidden
    second_ref[...] = (hidden * inverse_root(hidden) * gains_ref[1:2, :]).astype(bf16)


def row_call(kernel, slots, halves, *others):
    shape = others[0].shape
    return pl.pallas_call(
        kernel,
        grid=(1,),
        in_specs=[pl.BlockSpec(memory_space=pltpu.SMEM)]
        + specs(*[h.shape for h in halves], *[o.shape for o in others]),
        out_specs=specs(shape, shape),
        out_shape=[jax.ShapeDtypeStruct(shape, f32), jax.ShapeDtypeStruct(shape, bf16)],
        compiler_params=big,
        cost_estimate=costs(2),
    )(slots, *halves, *others)


def feed_kernel(
    steps, blocks, slots_ref, table_ref, s0, s1, s2, s3, s4, c0, c1, c2, c3, c4, gate_ref, up_ref, down_ref,
    product_ref, h0, h1, h2, h3, grads_ref,
    second_ref, down_grad_ref, gate_grad_ref, up_grad_ref, total, second_turned, down_turned,
):
    step = pl.program_id(0)
    tile = gate_ref.shape[1]

    @pl.when(step == 0)
    def _():
        second_ref[...] = joined_rows((s0, s1, s2, s3, s4))
        seqs = slots_ref.shape[0]
        inside = inside_all(slots_ref, seqs, TP * s0.shape[0] // seqs)
        down_grad_ref[...] = (inside * joined_rows((c0, c1, c2, c3, c4)).astype(f32)).astype(bf16)
        total[...] = jnp.zeros_like(total)

    @pl.when(step < steps)
    def _():
        second = second_ref[...]
        gate = jnp.dot(second, gate_ref[...], preferred_element_type=f32)
        up = jnp.dot(second, up_ref[...], preferred_element_type=f32)
        d_product = jnp.dot(down_grad_ref[...], down_ref[...], preferred_element_type=f32)
        sig = jax.nn.sigmoid(gate)
        swish = gate * sig
        gate_grad = (d_product * up * sig * (1.0 + gate * (1.0 - sig))).astype(bf16)
        up_grad = (d_product * swish).astype(bf16)
        at = pl.ds(pl.multiple_of(step * tile, tile), tile)
        product_ref[:, at] = (swish * up).astype(bf16)
        gate_grad_ref[:, at] = gate_grad
        up_grad_ref[:, at] = up_grad
        total[...] += dot_nt(gate_grad, gate_ref[...]) + dot_nt(up_grad, up_ref[...])

    @pl.when(step == steps - 1)
    def _():
        middle = total.shape[1] // 2
        put_left(total[:, :middle], (h0, h1))
        put_right(total[:, middle:], (h0, h1, h2, h3))
        size = second_ref.shape[1] // blocks
        for source, turned in ((second_ref, second_turned), (down_grad_ref, down_turned)):
            plain = jnp.transpose(source[...])
            total_rows = plain.shape[0]
            grads_ref[:total_rows, : plain.shape[1]] = plain
            for block in range(blocks):
                start = pl.multiple_of(table_ref[block] * size, size)
                turned[block * size : (block + 1) * size, :] = grads_ref[pl.ds(start, size), : plain.shape[1]]

    for part, (turned, right) in enumerate(
        ((second_turned, gate_grad_ref), (second_turned, up_grad_ref), (down_turned, product_ref))
    ):

        @pl.when((step >= (part + 1) * steps) & (step < (part + 2) * steps))
        def _(part=part, turned=turned, right=right):
            at = pl.multiple_of((step - (part + 1) * steps) * tile, tile)
            grads_ref[...] = jnp.dot(
                turned[...], right[:, pl.ds(at, tile)], preferred_element_type=f32
            ).astype(bf16)


def feed_forward(slots, table, second, cotangent, weight, units, tile=512):
    count, model = second[0].shape
    rows = TP * count
    steps = units // tile
    half_shapes = halves_out(rows, model, tile)[1]
    shapes = [p.shape for p in second]
    return pl.pallas_call(
        functools.partial(feed_kernel, steps, table.shape[0]),
        grid=(4 * steps,),
        in_specs=[pl.BlockSpec(memory_space=pltpu.SMEM)] * 2
        + specs(*shapes, *shapes)
        + [
            pl.BlockSpec((model, tile), lambda j, at=at: (0, at * steps + jnp.minimum(j, steps - 1)))
            for at in range(3)
        ],
        out_specs=specs((rows, units), *[h.shape for h in half_shapes])
        + [pl.BlockSpec((model, tile), lambda j: (0, jnp.maximum(j - steps, 0)))],
        out_shape=[jax.ShapeDtypeStruct((rows, units), bf16)]
        + half_shapes
        + [jax.ShapeDtypeStruct((model, 3 * units), bf16)],
        scratch_shapes=[pltpu.VMEM((rows, model), bf16)] * 2
        + [pltpu.VMEM((rows, units), bf16)] * 2
        + [pltpu.VMEM((rows, model), f32)]
        + [pltpu.VMEM((model, rows), bf16)] * 2,
        compiler_params=big,
        cost_estimate=costs(30),
    )(slots, table, *second, *cotangent, weight, weight, weight)


def in_places(values, places):
    size = values.shape[1] // len(places)
    return jnp.concatenate([values[:, p * size : (p + 1) * size] for p in places], axis=1)


def output_kernel(places, slots_ref, k0, k1, k2, k3, hidden_ref, output_ref):
    seqs = slots_ref.shape[0]
    inside = inside_all(slots_ref, seqs // TP, hidden_ref.shape[0] * TP // seqs)
    output = (hidden_ref[...] + inside * both_halves((k0, k1, k2, k3))).astype(bf16)
    output_ref[...] = in_places(output, places)


def token_grad_kernel(places, k0, k1, k2, k3, hidden_ref, source_ref, gains_ref, grad_ref):
    grad = both_halves((k0, k1, k2, k3)) * gains_ref[0:1, :]
    source = source_ref[...].astype(f32)
    total = hidden_ref[...] + norm_back(source, inverse_root(source), grad)
    grad_ref[...] = in_places(total, places)


def whole_call(kernel, dtype, scalars, *arrays):
    shape = arrays[4].shape
    return pl.pallas_call(
        kernel,
        grid=(1,),
        in_specs=[pl.BlockSpec(memory_space=pltpu.SMEM)] * len(scalars) + specs(*[a.shape for a in arrays]),
        out_specs=pl.BlockSpec(shape, lambda i: (0, 0)),
        out_shape=jax.ShapeDtypeStruct(shape, dtype),
        compiler_params=big,
        cost_estimate=costs(3),
    )(*scalars, *arrays)


def back_hidden_kernel(slots_ref, k0, k1, k2, k3, hidden_ref, cotangent_ref, gains_ref, d_hidden_ref, branch_ref):
    grad = both_halves((k0, k1, k2, k3)) * gains_ref[1:2, :]
    hidden = hidden_ref[...]
    d_hidden = cotangent_ref[...].astype(f32) + norm_back(hidden, inverse_root(hidden), grad)
    d_hidden_ref[...] = d_hidden
    seqs = slots_ref.shape[0]
    inside = inside_all(slots_ref, seqs // TP, hidden.shape[0] * TP // seqs)
    branch_ref[...] = (inside * d_hidden).astype(bf16)


def back_outer_kernel(tiles, b0, b1, b2, b3, b4, weight_ref, gate_ref, y_ref, gain_ref, branch_ref, grad_ref, dots_ref, total):
    step = pl.program_id(0)

    @pl.when(step == 0)
    def _():
        branch_ref[...] = joined_rows((b0, b1, b2, b3, b4))
        total[...] = jnp.zeros_like(total)

    grad = jnp.dot(branch_ref[...], weight_ref[...], preferred_element_type=f32)
    grad_ref[...] = grad

    @pl.when(step < tiles)
    def _():
        gate = gate_ref[...]
        gated = y_ref[...] * gate * jax.nn.sigmoid(gate)
        total[...] += jnp.sum(gated * gain_ref[...] * grad, axis=1, keepdims=True)

    @pl.when(step == pl.num_programs(0) - 1)
    def _():
        length = dots_ref.shape[2]
        for seq in range(dots_ref.shape[0]):
            dots_ref[seq] = as_row(total[seq * length : (seq + 1) * length, :])


def back_outer(branch, weight, proj, y, gain, seqs, tile=256):
    model = weight.shape[0]
    rows, inner = y.shape
    cols = weight.shape[1]
    tiles = inner // tile
    length = rows // seqs
    inner_spec = pl.BlockSpec((rows, tile), lambda j: (0, jnp.minimum(j, tiles - 1)))
    return pl.pallas_call(
        functools.partial(back_outer_kernel, tiles),
        grid=(cols // tile,),
        in_specs=specs(*[p.shape for p in branch])
        + [
            pl.BlockSpec((model, tile), lambda j: (0, j)),
            inner_spec,
            inner_spec,
            pl.BlockSpec((1, tile), lambda j: (0, jnp.minimum(j, tiles - 1))),
        ],
        out_specs=specs((rows, model))
        + [
            pl.BlockSpec((rows, tile), lambda j: (0, j)),
            pl.BlockSpec((seqs, 1, length), lambda j: (0, 0, 0)),
        ],
        out_shape=[
            jax.ShapeDtypeStruct((rows, model), bf16),
            jax.ShapeDtypeStruct((rows, cols), f32),
            jax.ShapeDtypeStruct((seqs, 1, length), f32),
        ],
        scratch_shapes=[pltpu.VMEM((rows, 1), f32)],
        compiler_params=big,
        cost_estimate=costs(5),
    )(*branch, weight, proj, y, gain)


def backward_kernel(
    inner, state, heads, slots_ref, proj_ref, params_ref, turn_ref, y_ref, grad_ref, root_ref, d0, d1, d2, d3, proj_grad_ref, small_ref,
):
    step_id = pl.program_id(0)
    start = slots_ref[step_id, 1]
    count = slots_ref[step_id, 0]
    proj = proj_ref[...]
    length = proj.shape[0]
    conv_cols = inner + 2 * state
    pad = PAD
    taps, bias, steps, skip, gain = parameters(params_ref, inner)
    m = mamba_shared(proj, start, count, taps, bias, steps, inner, state, heads)
    xs, decay, mixing = m["xs"], m["decay"], m["mixing"]
    scaled = xs * m["step_x"]
    gate = proj[:, :inner]
    gate_sig = jax.nn.sigmoid(gate)
    y = y_ref[...]
    root = as_column(root_ref[0])
    mean = as_column(sum(ref[0] for ref in (d0, d1, d2, d3))) / (TP * inner)
    gated = y * gate * gate_sig
    d_norm = grad_ref[:, :inner]
    d_gated = root * (d_norm * gain) - gated * (root * root * root * mean)
    dy = d_gated * gate * gate_sig
    d_gate = d_gated * y * gate_sig * (1.0 + gate * (1.0 - gate_sig))
    wide = 2 * length
    back, d_mix = [], []
    for c in range(0, inner, wide):
        dy_pair = dy[:, c : c + wide]
        full = mm(mixing[:, c : c + wide], dy_pair, TN)
        left = iota((length, wide), 1) < length
        back.append(jnp.where(left, full[:length], full[length:]))
        d_mix.append(mm(dy_pair, two_blocks(scaled[:, c : c + wide]), NT))
    back = jnp.concatenate(back, axis=1)
    d_mix = jnp.concatenate(d_mix, axis=1)
    d_xs = skip * dy + m["step_x"] * back
    flow = d_mix * mixing
    flow = flow - jnp.where(m["diagonal"], jnp.sum(flow, axis=0, keepdims=True), 0.0)
    d_cum = head_sums(flow, m["spread"])
    d_rate = mm(m["lower"], d_cum, TN, highest)
    d_step = head_sums(xs * back, m["spread"]) + d_rate * m["rate"]
    d_raw = jnp.where(m["lane"] < heads, d_step * jax.nn.sigmoid(m["raw"]), 0.0)
    d_inter = d_mix * decay
    pair = d_inter[:, :wide]
    for c in range(wide, inner, wide):
        pair = pair + d_inter[:, c : c + wide]
    d_inter = pair[:, :length] + pair[:, length:]
    d_b = mm(d_inter, m["c_state"], TN)
    d_c = mm(d_inter, m["b_state"], NN)
    d_active = jnp.concatenate([d_xs, d_b, d_c], axis=1)
    sig, conv = m["sig"], m["conv"]
    d_conv = d_active * sig * (1.0 + conv * (1.0 - sig))
    kernel = taps.shape[0]
    d_in = jnp.zeros_like(d_conv)
    conv_rows = []
    for tap in range(kernel):
        back_by = kernel - 1 - tap
        d_in = d_in + taps[tap : tap + 1, :] * up_rows(d_conv, back_by)
        conv_rows.append(jnp.sum(d_conv * down_rows(m["conv_in"], back_by), axis=0, keepdims=True))
    conv_rows.append(jnp.sum(d_conv, axis=0, keepdims=True))
    conv_rows.append(jnp.zeros((8 - kernel - 1, conv_cols), f32))
    conv_rows = jnp.concatenate(conv_rows, axis=0)
    inner_rows = jnp.concatenate(
        [
            jnp.sum(gated * root * d_norm, axis=0, keepdims=True),
            jnp.sum(dy * xs, axis=0, keepdims=True),
            jnp.zeros((6, inner), f32),
        ],
        axis=0,
    )
    step_rows = jnp.concatenate(
        [
            jnp.sum(d_raw, axis=0, keepdims=True),
            jnp.sum(d_rate * m["step"] * m["rate"], axis=0, keepdims=True),
            jnp.zeros((6, pad), f32),
        ],
        axis=0,
    )

    rows = jnp.concatenate([conv_rows, inner_rows, step_rows], axis=1)
    wide = small_ref.shape[1]
    rows = jnp.concatenate(
        [rows, jnp.zeros((8, small_ref.shape[0] // 8 * wide - rows.shape[1]), f32)], axis=1
    )
    rows = jnp.concatenate([rows[:, c : c + wide] for c in range(0, rows.shape[1], wide)], axis=0)

    @pl.when(step_id == 0)
    def _():
        small_ref[...] = jnp.zeros_like(small_ref)

    small_ref[...] += rows

    at = inner + conv_cols + pad
    cosine, sine = turn_ref[:, :HD], turn_ref[:, HD:]
    queries, keys, values, probs = attention_shared(proj, at, start, count, cosine, sine)
    d_out = jnp.concatenate(
        [grad_ref[:, c : c + HD] for c in range(inner, grad_ref.shape[1], HD)], axis=0
    )
    d_values = mm(probs, d_out, TN)
    d_probs = mm(d_out, values, NT)
    d_scores = probs * (d_probs - jnp.sum(probs * d_probs, axis=1, keepdims=True)) * (1.0 / math.sqrt(HD))
    d_queries = mm(d_scores, keys, NN)
    d_keys = mm(d_scores, queries, TN)
    outs = [d_gate, d_in * m["inside"], d_raw]
    outs += [turn(d_queries[r : r + length], cosine, -sine) for r in range(0, d_queries.shape[0], length)]
    outs += [turn(d_keys, cosine, -sine), d_values]
    proj_grad_ref[...] = jnp.concatenate(outs, axis=1).astype(proj_grad_ref.dtype)


def mixer_backward(
    slots, proj, params, turns, y, grads, root, dots, inner, state, heads
):
    seqs = slots.shape[0]
    rows, cols = proj.shape
    length = rows // seqs
    conv_cols = inner + 2 * state
    pad = PAD
    small_shape = (8 * pl.cdiv(conv_cols + inner + pad, grads.shape[1]), grads.shape[1])
    return pl.pallas_call(
        functools.partial(backward_kernel, inner, state, heads),
        grid=(seqs,),
        in_specs=[pl.BlockSpec(memory_space=pltpu.SMEM), rows_spec(length, cols)]
        + specs(params.shape)
        + [rows_spec(length, turns.shape[1])]
        + [rows_spec(length, inner), rows_spec(length, grads.shape[1])]
        + [pl.BlockSpec((1, 1, length), lambda i: (i, 0, 0))]
        + [their_spec(length, seqs // TP, k) for k in range(TP)],
        out_specs=[rows_spec(length, cols)] + specs(small_shape),
        out_shape=[
            jax.ShapeDtypeStruct((rows, cols), bf16),
            jax.ShapeDtypeStruct(small_shape, f32),
        ],
        compiler_params=big,
        cost_estimate=costs(17),
    )(slots, proj, params, turns, y, grads, root, *dots)


def chip_kernel(keep_ref, got_ref, mine_ref, along_y_ref, along_x_ref, across_x_ref, across_y_ref):
    total = (keep_ref[...].astype(f32) + got_ref[...].astype(f32)).astype(bf16)
    block = mine_ref.shape[0]
    half = across_x_ref.shape[0]
    mine_ref[...] = total[:block]
    along_y_ref[...] = total[block : 2 * block]
    along_x_ref[...] = total[2 * block : 3 * block]
    across_x_ref[...] = total[3 * block : 3 * block + half]
    across_y_ref[...] = total[3 * block + half :]


def along_kernel(along_y_ref, along_x_ref, by_x_ref, by_y_ref, to_y_ref, to_x_ref):
    half = by_x_ref.shape[0]
    to_y_ref[...] = along_y_ref[...]
    to_y_ref[:half, :] = (along_y_ref[:half, :].astype(f32) + by_x_ref[...].astype(f32)).astype(bf16)
    to_x_ref[...] = along_x_ref[...]
    to_x_ref[half:, :] = (along_x_ref[half:, :].astype(f32) + by_y_ref[...].astype(f32)).astype(bf16)


def plane_kernel(mine_ref, by_x_ref, by_y_ref, *outs):
    total = mine_ref[...].astype(f32) + by_x_ref[...].astype(f32) + by_y_ref[...].astype(f32)
    size = outs[0].shape[0]
    for k, out in enumerate(outs):
        out[...] = total[k * size : (k + 1) * size].astype(bf16)


def by_columns(kernel, row_counts, *arrays, tile=896):
    cols = arrays[0].shape[1]

    def of(rows):
        return pl.BlockSpec((rows, tile), lambda j: (0, j))

    return pl.pallas_call(
        kernel,
        grid=(cols // tile,),
        in_specs=[of(a.shape[0]) for a in arrays],
        out_specs=[of(r) for r in row_counts],
        out_shape=[jax.ShapeDtypeStruct((r, cols), bf16) for r in row_counts],
        compiler_params=big,
        cost_estimate=costs(3),
    )(*arrays)


def own_columns(me, refs, start, size, out_ref, at=0):
    for k, ref in enumerate(refs):
        place = pl.multiple_of((me ^ k) * size, 128)
        out_ref[:, pl.ds(at + place, size)] = ref[:, start : start + size].astype(f32)


def gain_sum(pairs, gain_ref):
    total = sum(
        jnp.sum(weight[...].astype(f32) * grad[...], axis=1, keepdims=True) for weight, grad in pairs
    )
    return total / gain_ref[...].astype(f32)


def unpack_mlp_kernel(units, me_ref, g0, g1, g2, g3, gate_ref, up_ref, gain_ref, grad_gate, grad_up, grad_down, grad_gain):
    for i, out in enumerate((grad_gate, grad_up, grad_down)):
        own_columns(me_ref[0], (g0, g1, g2, g3), i * units, units, out)
    grad_gain[...] = gain_sum(((gate_ref, grad_gate), (up_ref, grad_up)), gain_ref)


def unpack_out_kernel(inner, q_cols, me_ref, g0, g1, g2, g3, grad_mamba, grad_output):
    own_columns(me_ref[0], (g0, g1, g2, g3), 0, inner, grad_mamba)
    own_columns(me_ref[0], (g0, g1, g2, g3), inner, q_cols, grad_output)


def unpack_in_kernel(
    inner, state, heads, pad, me_ref, g0, g1, g2, g3, mamba_ref, query_ref, key_ref, value_ref, gain_ref,
    grad_mamba, grad_query, grad_key, grad_value, grad_gain,
):
    me = me_ref[0]
    refs = (g0, g1, g2, g3)
    own_columns(me, refs, 0, inner, grad_mamba)
    own_columns(me, refs, inner, inner, grad_mamba, TP * inner)
    at, out_at = 2 * inner, 2 * TP * inner
    shared = sum(ref[:, at : at + 2 * state].astype(f32) for ref in refs)
    grad_mamba[:, out_at : out_at + 2 * state] = shared
    at, out_at = at + 2 * state, out_at + 2 * state
    lane = iota((grad_mamba.shape[0], pad), 1)
    steps = jnp.zeros((grad_mamba.shape[0], pad), f32)
    for k, ref in enumerate(refs):
        piece = jnp.where(lane < heads, ref[:, at : at + pad].astype(f32), 0.0)
        steps = steps + pltpu.roll(piece, (me ^ k) * heads, axis=1)
    grad_mamba[:, out_at : out_at + TP * heads] = steps[:, : TP * heads]
    at += pad
    q_cols = query_ref.shape[1] // TP
    own_columns(me, refs, at, q_cols, grad_query)
    at += q_cols
    for out, start in ((grad_key, at), (grad_value, at + HD)):
        for first in (0, 2):
            both = refs[first][:, start : start + HD].astype(f32)
            both = both + refs[first + 1][:, start : start + HD].astype(f32)
            place = pl.multiple_of(((me ^ first) // 2) * HD, HD)
            out[:, pl.ds(place, HD)] = both
    pairs = ((mamba_ref, grad_mamba), (query_ref, grad_query), (key_ref, grad_key), (value_ref, grad_value))
    grad_gain[...] = gain_sum(pairs, gain_ref)


def unpack(kernel, me, parts, others, widths):
    rows = parts[0].shape[0]
    shapes = [(rows, w) for w in widths]
    return pl.pallas_call(
        kernel,
        grid=(1,),
        in_specs=[pl.BlockSpec(memory_space=pltpu.SMEM)]
        + specs(*[p.shape for p in parts], *[o.shape for o in others]),
        out_specs=specs(*shapes),
        out_shape=[jax.ShapeDtypeStruct(shape, f32) for shape in shapes],
        compiler_params=big,
        cost_estimate=costs(5),
    )(me, *parts, *others)


def weight_grad_kernel(bounds, mine, blocks, table_ref, *refs):
    parts = len(bounds)
    lefts = [refs[2 * mine * p : 2 * mine * p + mine] for p in range(parts)]
    rights = [refs[2 * mine * p + mine : 2 * mine * (p + 1)] for p in range(parts)]
    rest = refs[2 * mine * parts :]
    outs, plain, turned = rest[: -1 - parts], rest[-1 - parts], rest[-parts:]
    step = pl.program_id(0)
    size = plain.shape[0] // blocks

    @pl.when(step == 0)
    def _():
        for part in range(parts):
            plain[...] = jnp.concatenate([jnp.transpose(ref[...]) for ref in lefts[part]], axis=1)
            for block in range(blocks):
                at = pl.multiple_of(table_ref[block] * size, size)
                turned[part][block * size : (block + 1) * size, :] = plain[pl.ds(at, size), :]

    for part, (low, high) in enumerate(bounds):

        @pl.when((step >= low) & (step < high))
        def _(part=part):
            right = jnp.concatenate([ref[...] for ref in rights[part]], axis=0)
            full = jnp.dot(turned[part][...], right, preferred_element_type=f32)
            half = full.shape[0] // len(outs)
            for i, out in enumerate(outs):
                out[...] = full[i * half : (i + 1) * half].astype(out.dtype)


def weight_grads(table, pieces, pairs, tile=512):
    mine = len(pairs[0][0])
    rows, model = pairs[0][0][0].shape
    bounds, specs_in, args, low, cols = [], [], [], 0, 0
    for left, right, start, count in pairs:
        tiles = pl.cdiv(count, tile)
        first, last = low - start // tile, low + tiles - 1
        specs_in += [pl.BlockSpec((rows, model), lambda j: (0, 0))] * mine
        specs_in += [
            pl.BlockSpec(
                (rows, tile),
                lambda j, low=low, last=last, first=first: (0, jnp.clip(j, low, last) - first),
            )
        ] * mine
        args += list(left) + list(right)
        bounds.append((low, low + tiles))
        low += tiles
        cols += count
    return pl.pallas_call(
        functools.partial(weight_grad_kernel, tuple(bounds), mine, table.shape[0]),
        grid=(low,),
        in_specs=[pl.BlockSpec(memory_space=pltpu.SMEM)] + specs_in,
        out_specs=[pl.BlockSpec((model // pieces, tile), lambda j: (0, j))] * pieces,
        out_shape=[jax.ShapeDtypeStruct((model // pieces, cols), bf16)] * pieces,
        scratch_shapes=[pltpu.VMEM((model, mine * rows), bf16)] * (1 + len(pairs)),
        compiler_params=big,
        cost_estimate=costs(1 + cols // 256),
    )(table, *args)


def local(
    plane,
    tokens,
    lengths,
    offsets,
    norm_gain,
    mamba_in,
    conv_taps,
    conv_bias,
    step_bias,
    decay_log,
    skip_weight,
    mamba_gain,
    mamba_out,
    query_weight,
    key_weight,
    value_weight,
    output_weight,
    second_gain,
    gate_weight,
    up_weight,
    down_weight,
    cotangent,
):
    me = lax.axis_index("tp")
    peers = lax.axis_size(plane)
    batches, width, model = tokens.shape
    rows = batches * width
    shard = mamba_in.shape[0]
    inner = mamba_gain.shape[0]
    heads = step_bias.shape[0]
    state = (mamba_in.shape[1] - 2 * inner - heads) // 2
    q_cols = query_weight.shape[1]
    kv_heads = key_weight.shape[1] // HD
    hidden_units = gate_weight.shape[1]
    inner_t, heads_t, q_t, ff_t = inner // TP, heads // TP, q_cols // TP, hidden_units // TP
    pad = 128

    def swap(values, k, axis="tp"):
        size = lax.axis_size(axis)
        return lax.ppermute(values, axis, [(i, i ^ k) for i in range(size)])

    def spread_first(values):
        half = values.shape[1] // 2
        return swap(values[:, :half], 3), swap(values[:, half:], 1)

    def spread_second(values, far, near):
        half = values.shape[1] // 2
        pair = swap(jnp.concatenate([values[:, :half], far], axis=0), 1)
        last = swap(jnp.concatenate([values[:, half:], near], axis=0), 3)
        return values, far, pair, near, last

    def spread(values):
        return spread_second(values, *spread_first(values))

    def reduce_send(halves):
        return swap(halves[1], 1), swap(halves[3], 3)

    def reduce_add(halves, got, got_right):
        return halves[0] + got.astype(f32), halves[2] + got_right.astype(f32)

    def reduce_first(*halves):
        return reduce_add(halves, *reduce_send(halves))

    def reduce_second(pair, last):
        half = pair.shape[0] // 2
        got = swap(pair[half:].astype(bf16), 3)
        got_right = swap(last[half:].astype(bf16), 1)
        return pair[:half], got, last[:half], got_right

    def pair_finish(one, two, got_one, got_two):
        pairs = [reduce_add(one, *got_one), reduce_add(two, *got_two)]
        half = one[1].shape[0] // 2
        sends = [
            swap(jnp.concatenate([p[i][half:].astype(bf16) for p in pairs], axis=0), k)
            for i, k in ((0, 3), (1, 1))
        ]
        return [
            (p[0][:half], sends[0][i * half : (i + 1) * half], p[1][:half], sends[1][i * half : (i + 1) * half])
            for i, p in enumerate(pairs)
        ]

    def reduce(*halves):
        return reduce_second(*reduce_first(*halves))

    def everywhere(values):
        return [values] + [swap(values, k) for k in range(1, TP)]

    def absolute(parts):
        stacked = jnp.stack(parts)
        return jnp.concatenate(
            [lax.dynamic_index_in_dim(stacked, me ^ t, 0) for t in range(TP)], axis=0
        )

    cube = len(plane) == 3

    def order(values):
        lead = values.shape[:-1]
        if cube:
            split = values.reshape(lead + (TP, 2, 2, 2, shard))
            split = jnp.moveaxis(split, (-2, -4, -3, -5), (-5, -4, -3, -2))
        else:
            split = jnp.swapaxes(values.reshape(lead + (TP, peers, shard)), -3, -2)
        return split.reshape(values.shape)

    def place(n):
        group, at = divmod(n, peers)
        if cube:
            x, y, core = at // 4, at // 2 % 2, at % 2
            at = core * 4 + x * 2 + y
        return at * TP + group

    places = [place(n) for n in range(peers * TP)]

    blocks = jnp.arange(peers * TP, dtype=jnp.int32)
    in_group = blocks ^ me
    in_plane = blocks ^ (lax.axis_index(plane) * TP + me)

    def cut(weight, start, size, t):
        return lax.dynamic_slice_in_dim(weight, start + t * size, size, axis=1)

    def kv(weight, t):
        return cut(weight, 0, HD, t * kv_heads // TP)

    slot_column = jnp.concatenate([lengths[:, 0], offsets[:, 0]]).astype(bf16)[:, None]

    def in_slice(t):
        return jnp.concatenate(
            [
                cut(mamba_in, 0, inner_t, t),
                cut(mamba_in, inner, inner_t, t),
                mamba_in[:, 2 * inner : 2 * inner + 2 * state],
                cut(mamba_in, 2 * inner + 2 * state, heads_t, t),
                norm_gain[:, None],
                second_gain[:, None],
                jnp.pad(slot_column, ((0, shard - 2 * batches), (0, pad - heads_t - 3))),
                cut(query_weight, 0, q_t, t),
                kv(key_weight, t),
                kv(value_weight, t),
            ],
            axis=1,
        )

    def out_slice(t):
        return jnp.concatenate([cut(mamba_out.T, 0, inner_t, t), cut(output_weight.T, 0, q_t, t)], axis=1)

    def mlp_slice(t):
        return jnp.concatenate(
            [
                cut(gate_weight, 0, ff_t, t),
                cut(up_weight, 0, ff_t, t),
                cut(down_weight.T, 0, ff_t, t),
            ],
            axis=1,
        )

    def after(values, *earlier):
        return lax.optimization_barrier((values, earlier))[0]

    def slices(make):
        return [make(me ^ k) for k in range(TP)]

    def exchange(pieces):
        return [pieces[0]] + [swap(pieces[k], k) for k in range(1, TP)]

    def gather(parts):
        return lax.all_gather(absolute(parts).reshape(TP * shard, -1), plane, axis=0, tiled=True)

    def scatter(grads):
        return lax.psum_scatter(grads, plane, scatter_dimension=0, tiled=True)

    def pass_on(part):
        part = part.reshape(TP, shard, -1)
        return exchange([part[k] for k in range(TP)])

    conv_cols = inner_t + 2 * state
    at_q = inner_t + conv_cols + pad
    in_cols = at_q + q_t + 2 * HD

    def own(values, size):
        return lax.dynamic_slice_in_dim(values, me * size, size, axis=-1)

    taps_t = jnp.concatenate([own(conv_taps[:, :inner], inner_t), conv_taps[:, inner:]], axis=1)
    bias_t = jnp.concatenate([own(conv_bias[:inner], inner_t), conv_bias[inner:]])[None]
    steps_t = jnp.pad(
        jnp.stack([own(step_bias, heads_t), own(decay_log, heads_t)]), ((0, 0), (0, pad - heads_t))
    )
    skip_t = jnp.repeat(own(skip_weight, heads_t), inner_t // heads_t)[None]
    gain_t = own(mamba_gain, inner_t)[None]
    sizes = (inner_t, state, heads_t)

    def widened(values):
        return jnp.pad(values, ((0, 0), (0, conv_cols - values.shape[1])))

    params = jnp.concatenate(
        [taps_t, bias_t, widened(skip_t), widened(gain_t), widened(steps_t.reshape(1, -1))], axis=0
    )

    in_slices = slices(in_slice)
    in_parts = exchange(in_slices)
    tokens, cotangent = after((tokens, cotangent), in_slices)
    source = order(tokens.reshape(rows, model))
    upstream = order(cotangent.reshape(rows, model))
    prepared = (
        source, upstream, slices(out_slice), slices(mlp_slice),
        params, gain_t, in_plane, in_group,
    )
    in_parts, prepared = lax.optimization_barrier((in_parts, prepared))
    source, upstream, out_slices, mlp_slices = prepared[:4]
    params, gain_t, in_plane, in_group = prepared[4:]
    w_in = gather(in_parts)
    source_some, upstream_some = spread_first(source), spread_first(upstream)
    column = inner_t + 2 * state + inner_t + heads_t + 2
    slots = jnp.stack([in_parts[k][: 2 * batches, column] for k in (0, 3, 1, 2)])
    slots = after(slots, source_some).astype(jnp.int32).reshape(TP, 2, batches)
    slots = jnp.swapaxes(slots, 1, 2).reshape(TP * batches, 2)
    turns = turn_table(slots[:, 1], width)
    source_all = spread_second(source, *source_some)
    out_parts = exchange(after(out_slices, (source_all, upstream_some)))
    w_out = gather(out_parts)
    mlp_slices, upstream_some = after((mlp_slices, upstream_some), out_parts[1:])
    mlp_parts = exchange(mlp_slices)
    upstream_all = spread_second(upstream, *upstream_some)

    normed, projected, y, squares, mixed, gains = mixer_inner(
        slots, after(source_all, (out_parts[1:], mlp_parts[1])), w_in, params, turns, *sizes
    )
    squares = everywhere(after(squares, upstream_all))
    w_mlp = gather(after(mlp_parts, squares[1:]))
    branches, root, *halves = mixer_outer(projected, y, mixed, gain_t, squares, w_out)
    hidden, second = row_call(hidden_kernel, slots, reduce(*halves), source, gains)

    product, *halves, mlp_sums = feed_forward(
        slots, in_group, spread(second), upstream_all, w_mlp, ff_t
    )
    mlp_sums = scatter(mlp_sums)
    d_hidden, branch_grad = row_call(
        back_hidden_kernel, slots, reduce(*halves), hidden, upstream, gains
    )

    branch_all = spread(branch_grad)
    last_halves = back_out(product, w_mlp, 2)
    branch_grad = after(branch_all, last_halves)
    branch_all, d_branches, dots = back_outer(
        branch_grad, w_out, projected, y, gain_t, slots.shape[0]
    )
    last_halves = after(last_halves, branch_grad)
    last_pair = reduce_send(last_halves)
    out_sums = weight_grads(in_group, 1, [([branch_all], [branches], 0, inner_t + q_t)])
    dots = after(everywhere(dots), (out_sums, last_pair))
    out_sums = scatter(out_sums[0])
    mlp_grads = pass_on(after(mlp_sums, dots))
    proj_grad, small = mixer_backward(
        slots, projected, params, turns, y, d_branches, root, dots, *sizes,
    )
    in_sums = weight_grads(
        in_plane if cube else in_group,
        2 if cube else 1,
        [([after(normed, mlp_grads)], [proj_grad], 0, in_cols)],
        tile=896,
    )
    riders = small.astype(bf16)
    out_sums, riders = after((out_sums, riders), in_sums)
    out_sums = out_sums.reshape(TP, shard, -1)
    received = [
        swap(jnp.concatenate([out_sums[k], riders], axis=0), k) for k in range(1, TP)
    ]
    norm_halves = back_out(after(proj_grad, in_sums), w_in, 0)
    norm_pair = reduce_send(norm_halves)
    if cube:
        block, half = TP * shard, TP * shard // 2
        counts = (block, block, block, half, half)
        keep, send = in_sums
        mine, along_y, along_x, across_x, across_y = by_columns(
            chip_kernel, counts, keep, after(swap(send, 1, "core"), (norm_halves, received))
        )
        across = swap(across_x, 1, "x"), swap(across_y, 1, "y")
        norm_pair, across = after((norm_pair, across), norm_pair)
        to_y, to_x = by_columns(
            along_kernel, (block, block), along_y, along_x, *across
        )
        in_parts = swap(to_x, 1, "x"), swap(to_y, 1, "y")
    last_pair = after(last_pair, norm_pair)
    norm_parts, last_parts = pair_finish(norm_halves, last_halves, norm_pair, last_pair)
    out_grads = [out_sums[0]] + [r[:shard] for r in received]
    small = absolute([small] + [r[shard:].astype(f32) for r in received])
    if cube:
        small = small + swap(small, 1, "core")
        in_parts = after(in_parts, (norm_parts, last_parts, small))
        in_sums = by_columns(plane_kernel, (shard,) * TP, mine, *in_parts)
        in_grads = exchange(in_sums)
    else:
        in_sums = scatter(in_sums[0])
        in_grads = pass_on(in_sums)
    small, mlp_grads, out_grads, norm_parts, last_parts = after(
        (small, mlp_grads, out_grads, norm_parts, last_parts), in_sums
    )
    if cube:
        small = small + swap(small, 1, "x")
        small = small + swap(small, 1, "y")
    else:
        small = lax.psum(small, plane)
    token_grads = whole_call(
        functools.partial(token_grad_kernel, places), f32, (), *norm_parts, d_hidden, source, gains
    )
    output = whole_call(
        functools.partial(output_kernel, places), bf16, (slots,), *last_parts, hidden
    )

    at_group = me[None].astype(jnp.int32)
    grad_gate, grad_up, grad_down, grad_second_gain = unpack(
        functools.partial(unpack_mlp_kernel, ff_t),
        at_group,
        mlp_grads,
        (gate_weight, up_weight, second_gain[:, None]),
        (hidden_units, hidden_units, hidden_units, 1),
    )
    grad_mamba_out, grad_output = unpack(
        functools.partial(unpack_out_kernel, inner_t, q_t), at_group, out_grads, (), (inner, q_cols)
    )
    in_grads = after(in_grads, (small, token_grads, output, grad_down, grad_output))
    grad_mamba_in, grad_query, grad_key, grad_value, grad_norm_gain = unpack(
        functools.partial(unpack_in_kernel, *sizes, pad),
        at_group,
        in_grads,
        (mamba_in, query_weight, key_weight, value_weight, norm_gain[:, None]),
        (mamba_in.shape[1], q_cols, kv_heads * HD, kv_heads * HD, 1),
    )
    grad_mamba_out, grad_output, grad_down = grad_mamba_out.T, grad_output.T, grad_down.T
    grad_norm_gain, grad_second_gain = grad_norm_gain[:, 0], grad_second_gain[:, 0]

    kernel = conv_taps.shape[0]
    small = small.reshape(TP, -1, 8, small.shape[-1])
    small = jnp.concatenate([small[:, i] for i in range(small.shape[1])], axis=-1)
    conv = small[:, : kernel + 1, :conv_cols]
    conv = jnp.concatenate(
        [conv[:, :, :inner_t].transpose(1, 0, 2).reshape(kernel + 1, inner), conv[:, :, inner_t:].sum(0)],
        axis=1,
    )
    by_inner = small[:, :2, conv_cols : conv_cols + inner_t]
    by_step = small[:, :2, conv_cols + inner_t : conv_cols + inner_t + heads_t]
    return (
        output.reshape(tokens.shape),
        token_grads.reshape(tokens.shape),
        grad_norm_gain,
        grad_mamba_in,
        conv[:kernel],
        conv[kernel],
        by_step[:, 0].reshape(-1),
        by_step[:, 1].reshape(-1),
        by_inner[:, 1].reshape(heads, -1).sum(1),
        by_inner[:, 0].reshape(-1),
        grad_mamba_out,
        grad_query,
        grad_key,
        grad_value,
        grad_output,
        grad_second_gain,
        grad_gate,
        grad_up,
        grad_down,
    )


def solution(mesh):
    count = mesh.devices.size
    if tuple(mesh.devices.shape) == (8, 4):
        grid = Mesh(mesh.devices.reshape(TP, 2, 2, 2), ("tp", "x", "y", "core"))
        plane = ("core", "x", "y")
    else:
        grid = Mesh(mesh.devices.reshape(TP, count // TP), ("tp", "fs"))
        plane = ("fs",)
    every = grid.axis_names
    down, across, slots = P(every, None), P(None, every), P(None, every, None)
    line, copied = P(every), P()
    return jax.shard_map(
        functools.partial(local, plane),
        mesh=grid,
        in_specs=(
            slots, across, across, line, down, copied, copied, copied, copied, copied, copied,
            across, down, down, down, across, line, down, down, across, slots,
        ),
        out_specs=(
            slots, slots, line, down, copied, copied, copied, copied, copied, copied,
            across, down, down, down, across, line, down, down, across,
        ),
        check_vma=False,
    )
```
